128 devices in a mesh: row: 8 (over y, core), col: 16 (over z, x).
Axes of the slice: x: 4, y: 4, z: 4, core: 2. Of those that a mesh axis runs over, the one named last changes fastest.
Arguments:
- latent: bfloat16 [256, 64, 2048], P(None, 'row', 'col'), may hold values from -6 to 6
- norm_gain: float32 [256], replicated, may hold values from 0.1 to 1.9
- qkv_weight: bfloat16 [768, 256], replicated, may hold values from -0.375 to 0.375
- out_weight: bfloat16 [256, 256], replicated, may hold values from -0.375 to 0.375
- cos_scale: float32 [4], replicated, may hold values from 2 to 12
- grad_output: bfloat16 [256, 64, 2048], P(None, 'row', 'col'), may hold values from -6 to 6
Outputs:
- grad_latent: bfloat16 [256, 64, 2048], P(None, 'row', 'col')
- grad_qkv_weight: float32 [768, 256], replicated
- grad_out_weight: float32 [256, 256], replicated
The draws below stay inside these ranges and needn't reach their ends.
All inputs are finite; a program needn't handle non-finite values.
Results may differ from the reference program's by a relative error of at most 0.009.
Values may be sent and summed in bfloat16 or wider, within the bound.
A program may use at most 256 MiB of HBM per device.

```python
import math
import jax
import jax.numpy as jnp
from jax import lax

D = 256
HEADS = 4
RADIUS = 3
IMG_ROWS = 64
IMG_COLS = 2048


def block_scale(rng, shape, split, low, largest):
    level, own = 1.0, jax.random.fold_in(rng, 6)
    for dim, blocks in split:
        heights = jnp.exp(jax.random.uniform(jax.random.fold_in(own, dim), (blocks,), jnp.float32, low / len(split), largest / len(split)))
        level = level * jnp.repeat(heights, shape[dim] // blocks).reshape([-1 if axis == dim else 1 for axis in range(len(shape))])
    return level


def scatter_about(rng, dims, scale, limit, split=(), kind=jnp.bfloat16):
    array = jax.random.normal(rng, dims, jnp.float32) * scale
    if len(split) > 0:
        array = block_scale(rng, dims, split, -0.22, 0.18) * array
    return jnp.clip(array, min=-limit, max=limit).astype(kind)


def setup_inputs(seed: int = 0) -> dict:
    key_list = jax.random.split(jax.random.key(seed), 7)
    latent = scatter_about(key_list[0], (D, IMG_ROWS, IMG_COLS), 1.0, 6.0, ((1, 8), (2, 16)))
    norm_gain = jnp.clip(1.0 + 0.18 * jax.random.normal(key_list[1], (D,), jnp.float32), 0.1, 1.9)
    qkv_weight = scatter_about(key_list[2], (3 * D, D), D ** -0.5, 0.375)
    out_weight = scatter_about(key_list[3], (D, D), D ** -0.5, 0.375)
    cos_scale = jnp.clip(jnp.exp(jax.random.uniform(key_list[4], (HEADS,), jnp.float32, math.log(2.0), math.log(12.0))), 2.0, 12.0)
    grad_output = scatter_about(key_list[5], (D, IMG_ROWS, IMG_COLS), 1.0, 6.0, ((1, 8), (2, 16)))
    return dict(latent=latent, norm_gain=norm_gain, qkv_weight=qkv_weight, out_weight=out_weight, cos_scale=cos_scale, grad_output=grad_output)


EPS = 1e-06

def head_norm(raw):
    inverse = lax.rsqrt(lax.optimization_barrier(jnp.mean(raw * raw, axis=-3, keepdims=True)) + EPS)
    return ((raw * inverse).astype(jnp.bfloat16), inverse)

def norm_back(raw, inverse, grad):
    inner = lax.optimization_barrier(jnp.mean(grad * raw, axis=-3, keepdims=True))
    return inverse * (grad - raw * inverse * inverse * inner)

def neighbor_pass(queries, key_ext, value_ext, valid_ext, grad_attn, scales):
    head_count, head_width, height, length = queries.shape
    window = 2 * RADIUS + 1
    factor = (scales / head_width)[:, None, None]
    query32 = queries.astype(jnp.float32)
    places = [(a, b) for a in range(window) for b in range(window)]

    def key_at(a, b):
        return key_ext[:, :, a:a + height, b:b + length].astype(jnp.float32)

    def value_at(a, b):
        return value_ext[:, :, a:a + height, b:b + length].astype(jnp.float32)

    def spread(term, a, b):
        return jnp.pad(term, ((0, 0), (0, 0), (a, window - 1 - a), (b, window - 1 - b)))
    exponents = []
    products = []
    for a, b in places:
        logits = factor * lax.optimization_barrier(jnp.sum(query32 * key_at(a, b), axis=1))
        exponents.append(jnp.exp(logits) * valid_ext[a:a + height, b:b + length])
        products.append(lax.optimization_barrier(jnp.sum(grad_attn * value_at(a, b), axis=1)))
    totals = sum(exponents)
    weights = [item / totals for item in exponents]
    mean_dot = sum((w_item * p_item for w_item, p_item in zip(weights, products)))
    slopes = [factor * w_item * (p_item - mean_dot) for w_item, p_item in zip(weights, products)]
    attn = sum((weights[i][:, None] * value_at(a, b) for i, (a, b) in enumerate(places))).astype(jnp.bfloat16)
    grad_q = sum((slopes[i][:, None] * key_at(a, b) for i, (a, b) in enumerate(places)))
    grad_k_ext = sum((spread(slopes[i][:, None] * query32, a, b) for i, (a, b) in enumerate(places)))
    grad_v_ext = sum((spread(weights[i][:, None] * grad_attn, a, b) for i, (a, b) in enumerate(places)))
    return (attn, grad_q, grad_k_ext, grad_v_ext)

def reference(latent, norm_gain, qkv_weight, out_weight, cos_scale, grad_output):
    depth, height, length = latent.shape
    head_width = depth // HEADS
    latent32 = latent.astype(jnp.float32)
    inverse = lax.rsqrt(lax.optimization_barrier(jnp.mean(latent32 * latent32, axis=0, keepdims=True)) + EPS)
    normed = (latent32 * inverse * norm_gain[:, None, None]).astype(jnp.bfloat16)
    flat = normed.reshape(depth, height * length)
    projected = jnp.dot(qkv_weight, flat, preferred_element_type=jnp.float32).reshape(3, HEADS, head_width, height, length)
    queries, query_inv = head_norm(projected[0])
    key_norm, key_inv = head_norm(projected[1])
    values = projected[2].astype(jnp.bfloat16)
    padding = ((0, 0), (0, 0), (RADIUS, RADIUS), (RADIUS, RADIUS))
    key_ext = jnp.pad(key_norm, padding)
    value_ext = jnp.pad(values, padding)
    valid_ext = jnp.pad(jnp.ones((height, length), jnp.float32), RADIUS)
    out_flat = grad_output.reshape(depth, height * length)
    grad_attn = lax.dot_general(out_weight, out_flat, (((0,), (0,)), ((), ())), preferred_element_type=jnp.float32)
    grad_attn = grad_attn.reshape(HEADS, head_width, height, length)

    def one_head(pieces):
        results = neighbor_pass(pieces[0][None], pieces[1][None], pieces[2][None], valid_ext, pieces[3][None], pieces[4][None])
        return tuple((item[0] for item in results))
    attn, grad_q, grad_k_ext, grad_v_ext = lax.map(one_head, (queries, key_ext, value_ext, grad_attn, cos_scale))
    grad_k = grad_k_ext[:, :, RADIUS:-RADIUS, RADIUS:-RADIUS]
    grad_v = grad_v_ext[:, :, RADIUS:-RADIUS, RADIUS:-RADIUS]
    attn_flat = attn.reshape(depth, height * length)
    grad_wout = lax.dot_general(out_flat, attn_flat, (((1,), (1,)), ((), ())), preferred_element_type=jnp.float32)
    grad_qraw = norm_back(projected[0], query_inv, grad_q)
    grad_kraw = norm_back(projected[1], key_inv, grad_k)
    grad_proj = jnp.stack([grad_qraw, grad_kraw, grad_v]).reshape(3 * depth, height * length)
    grad_wqkv = lax.dot_general(grad_proj, flat.astype(jnp.float32), (((1,), (1,)), ((), ())), precision=lax.Precision.HIGHEST, preferred_element_type=jnp.float32)
    grad_normed = lax.dot_general(qkv_weight.astype(jnp.float32), grad_proj, (((0,), (0,)), ((), ())), precision=lax.Precision.HIGHEST, preferred_element_type=jnp.float32)
    grad_normed = grad_normed.reshape(depth, height, length) * norm_gain[:, None, None]
    grad_latent = norm_back(latent32, inverse, grad_normed).astype(jnp.bfloat16)
    factor = 1.0 / math.sqrt(height * length)
    return (grad_latent, grad_wqkv * factor, grad_wout * factor)
```

```python
import collections
import functools
import math

import jax
import jax.numpy as jnp
from jax import lax
from jax.experimental import pallas as pl
from jax.experimental.pallas import tpu as pltpu
from jax.sharding import PartitionSpec as P

MESH = pl.DeviceIdType.MESH
F32 = jnp.float32
BF16 = jnp.bfloat16

D = 256
HEADS = 4
HW = 64
RADIUS = 3
EPS = 1e-06
H = 8
W = 128
B = 16
NB = W // B
NG = NB + 1
ER = 16
GC = ER * B
WT = 4 * D

DIRS = ((-1, 0), (1, 0), (0, -1), (0, 1), (-1, -1), (-1, 1), (1, -1), (1, 1))


def dot(a, b):
    return lax.dot_general(a, b, (((1,), (0,)), ((), ())), preferred_element_type=F32)


def dot_nt(a, b):
    return lax.dot_general(a, b, (((1,), (1,)), ((), ())), preferred_element_type=F32)


def heads(x):
    return x.reshape(HEADS, HW, x.shape[-1])


def flat(x):
    return x.reshape(HEADS * HW, x.shape[-1])


def scratch_shapes(nr, nc):
    cc = 2 * D // nc
    return collections.OrderedDict(
        l32=pltpu.VMEM((D * H, W), F32),
        g32=pltpu.VMEM((D * H, W), F32),
        inv=pltpu.VMEM((H, W), F32),
        xr=pltpu.VMEM((H * W, D), BF16),
        xe32=pltpu.VMEM((2, H * 8, D), F32),
        xe=pltpu.VMEM((2, H * 8, D), BF16),
        rx_row=pltpu.VMEM((2, RADIUS * W, D), BF16),
        rx_col=pltpu.VMEM((2, H * 8, D), BF16),
        rx_cor=pltpu.VMEM((4, 32, D), BF16),
        xg=pltpu.VMEM((NG, GC, D), BF16),
        xb=pltpu.VMEM((NB, H * B, D), BF16),
        gob=pltpu.VMEM((NB, H * B, D), BF16),
        wot=pltpu.VMEM((D, D), BF16),
        wt=pltpu.VMEM((D, 3 * D), BF16),
        kraw=pltpu.VMEM((NG, D, GC), F32),
        kinv=pltpu.VMEM((NG, HEADS, 1, GC), F32),
        kc=pltpu.VMEM((NG, GC, D), BF16),
        vc=pltpu.VMEM((NG, GC, D), BF16),
        kt=pltpu.VMEM((NG, D, GC), BF16),
        vt=pltpu.VMEM((NG, D, GC), BF16),
        qraw=pltpu.VMEM((NB, D, H * B), F32),
        qinv=pltpu.VMEM((NB, HEADS, 1, H * B), F32),
        qm=pltpu.VMEM((NB, 2, 2 * HW, 2 * H * B), BF16),
        gm=pltpu.VMEM((NB, 2, 2 * HW, 2 * H * B), BF16),
        mask=pltpu.VMEM((3, 2 * GC, H * B), F32),
        gk=pltpu.VMEM((NG, D, GC), F32),
        gv=pltpu.VMEM((NG, D, GC), F32),
        gq=pltpu.VMEM((NB, D, H * B), F32),
        at=pltpu.VMEM((NB, D, H * B), BF16),
        gqb=pltpu.VMEM((NB, D, H * B), BF16),
        gkv=pltpu.VMEM((NG, 2 * D, GC), BF16),
        gn=pltpu.VMEM((2 * RADIUS + H, NG * B, D), F32),
        tx_row=pltpu.VMEM((2, RADIUS * W, D), BF16),
        tx_col=pltpu.VMEM((2, H * 8, D), BF16),
        tx_cor=pltpu.VMEM((4, 32, D), BF16),
        ry_row=pltpu.VMEM((2, RADIUS * W, D), BF16),
        ry_col=pltpu.VMEM((2, H * 8, D), BF16),
        ry_cor=pltpu.VMEM((4, 32, D), BF16),
        wg=pltpu.VMEM((WT, D), F32),
        wb=pltpu.VMEM((WT, D), BF16),
        rx_half=pltpu.VMEM((WT // 2, D), BF16),
        half=pltpu.VMEM((WT // 2, D), F32),
        hb=pltpu.VMEM((WT // 2, D), BF16),
        rx_pl=pltpu.VMEM((nc, cc, D), BF16),
        ys=pltpu.VMEM((nr // 2, cc, D), F32),
        fb=pltpu.VMEM((WT, D), BF16),
        s_hal=pltpu.SemaphoreType.DMA((8,)),
        r_hal=pltpu.SemaphoreType.DMA((8,)),
        s_ret=pltpu.SemaphoreType.DMA((8,)),
        r_ret=pltpu.SemaphoreType.DMA((8,)),
        s_core=pltpu.SemaphoreType.DMA((2,)),
        r_core=pltpu.SemaphoreType.DMA((2,)),
        s_pl=pltpu.SemaphoreType.DMA((2, nc)),
        r_pl=pltpu.SemaphoreType.DMA((2, nc)),
        s_y=pltpu.SemaphoreType.DMA((nr // 2,)),
        r_y=pltpu.SemaphoreType.DMA((nr // 2,)),
    )


def kernel(nr, nc, names, *refs):
    S = collections.namedtuple("S", names)(*refs)
    row, col = lax.axis_index("row"), lax.axis_index("col")
    core, ypos = lax.rem(row, 2), lax.div(row, 2)
    ny = nr // 2
    cc = 2 * D // nc

    def at(dr, dc):
        return (lax.rem(row + (dr % nr), nr), lax.rem(col + (dc % nc), nc))

    mate = (row + 1 - 2 * core, col)

    def remote(src, dst, send, recv, device):
        return pltpu.make_async_remote_copy(
            src_ref=src, dst_ref=dst, send_sem=send, recv_sem=recv, device_id=device, device_id_type=MESH
        )

    partners = list(DIRS)
    partners += [(0, k) for k in range(2, nc - 1)]
    partners += [(2 * m, 0) for m in range(1, ny)]
    barrier = pltpu.get_barrier_semaphore()
    for dr, dc in partners:
        pl.semaphore_signal(barrier, inc=1, device_id=at(dr, dc), device_id_type=MESH)

    step = 32

    def load(i, acc):
        x = S.lat[pl.ds(i * step, step)].astype(F32)
        S.l32[pl.ds(pl.multiple_of(i * step * H, step * H), step * H), :] = x.reshape(step * H, W)
        g = S.go[pl.ds(i * step, step)].astype(F32)
        S.g32[pl.ds(pl.multiple_of(i * step * H, step * H), step * H), :] = g.reshape(step * H, W)
        return acc + jnp.sum(x * x, axis=0)

    total = lax.fori_loop(0, D // step, load, jnp.zeros((H, W), F32))
    S.inv[...] = lax.rsqrt(total * (1.0 / D) + EPS)
    gain = S.gain[...]

    def cells(r, carry):
        x = S.l32[pl.ds(r, D, stride=H), :] * S.inv[pl.ds(r, 1), :]
        xn = x.T * gain
        xnb = xn.astype(BF16)
        S.xr[pl.ds(pl.multiple_of(r * W, W), W), :] = xnb
        S.xe32[0, pl.ds(pl.multiple_of(r * 8, 8), 8), :] = xn[:8]
        S.xe32[1, pl.ds(pl.multiple_of(r * 8, 8), 8), :] = xn[W - 8 :]
        own = pl.ds(pl.multiple_of(r * B, B), B)
        ext = pl.ds(pl.multiple_of(r * B + RADIUS * B, B), B)
        for j in range(NB):
            S.xb[j, own, :] = xnb[j * B : (j + 1) * B]
        for g in range(1, NB):
            S.xg[g, ext, :] = xn[g * B - 8 : g * B + 8].astype(BF16)
        return carry

    lax.fori_loop(0, H, cells, 0)
    S.xe[...] = S.xe32[...].astype(BF16)

    pl.semaphore_wait(barrier, len(partners))
    near = 3 * W
    edge = {-1: slice(0, near), 1: slice(H * W - near, H * W)}
    part = {-1: slice(0, 32), 1: slice(32, 64)}
    halo = []
    for i, (dr, dc) in enumerate(DIRS):
        if dc == 0:
            src, dst = S.xr.at[edge[dr]], S.rx_row.at[i]
        elif dr == 0:
            src, dst = S.xe.at[(dc + 1) // 2], S.rx_col.at[i - 2]
        else:
            src, dst = S.xe.at[(dc + 1) // 2, part[dr]], S.rx_cor.at[i - 4]
        halo.append(remote(src, dst, S.s_hal.at[i], S.r_hal.at[i], at(dr, dc)))
        halo[-1].start()

    S.wot[...] = S.wo[...].T
    for i in range(3):
        S.wt[:, i * D : (i + 1) * D] = S.wqkv[i * D : (i + 1) * D, :].T

    def grads(r, carry):
        g = S.g32[pl.ds(r, D, stride=H), :].T.astype(BF16)
        own = pl.ds(pl.multiple_of(r * B, B), B)
        for j in range(NB):
            S.gob[j, own, :] = g[j * B : (j + 1) * B]
        return carry

    lax.fori_loop(0, H, grads, 0)

    mshape = (2, ER, B, H * B)
    half_, kr, kc = (lax.broadcasted_iota(jnp.int32, mshape, a) for a in range(3))
    lane = lax.broadcasted_iota(jnp.int32, mshape, 3)
    qr, qc = lax.div(lane, B), lax.rem(lane, B)
    dr = kr - RADIUS - qr
    off = B * half_ + kc - 8
    dc = off - qc
    grow = row * H + kr - RADIUS
    ok = (dr >= -RADIUS) & (dr <= RADIUS) & (dc >= -RADIUS) & (dc <= RADIUS)
    ok = ok & (grow >= 0) & (grow < nr * H)
    one = jnp.where(ok, 1.0, 0.0).astype(F32).reshape(2 * GC, H * B)
    off = off.reshape(2 * GC, H * B)
    S.mask[0] = jnp.where((col * W + off >= 0), one, 0.0)
    S.mask[1] = one
    S.mask[2] = jnp.where(col * W + W - B + off < nc * W, one, 0.0)

    def queries(j, carry):
        q = heads(dot_nt(S.wqkv[0:D, :], S.xb[j]))
        inv = lax.rsqrt(jnp.mean(q * q, axis=1, keepdims=True) + EPS)
        qn = (q * inv).astype(BF16)
        S.qraw[j] = flat(q)
        S.qinv[j] = inv
        ga = heads(dot_nt(S.wot[...], S.gob[j])).astype(BF16)
        z = jnp.zeros((HW, H * B), BF16)
        for p in range(2):
            for x, out in ((qn, S.qm), (ga, S.gm)):
                out[j, p, 0:HW, :] = jnp.concatenate([x[2 * p], z], axis=1)
                out[j, p, HW : 2 * HW, :] = jnp.concatenate([z, x[2 * p + 1]], axis=1)
        return carry

    lax.fori_loop(0, NB, queries, 0)

    for c in halo:
        c.wait_recv()
    left = S.rx_col[1].astype(F32)
    right = S.rx_col[0].astype(F32)

    def ends(er, cells_, l8, r8):
        S.xg[0, er * B : (er + 1) * B, :] = jnp.concatenate([l8, cells_[:8]], axis=0).astype(BF16)
        S.xg[NB, er * B : (er + 1) * B, :] = jnp.concatenate([cells_[-8:], r8], axis=0).astype(BF16)

    for r in range(H):
        ends(
            r + RADIUS,
            jnp.concatenate([S.xe32[0, r * 8 : r * 8 + 8, :], S.xe32[1, r * 8 : r * 8 + 8, :]], axis=0),
            left[r * 8 : r * 8 + 8],
            right[r * 8 : r * 8 + 8],
        )
    for up in (0, 1):
        l_cor = S.rx_cor[2 * up + 1].astype(F32)
        r_cor = S.rx_cor[2 * up].astype(F32)
        for i in range(RADIUS):
            er = i if up == 1 else RADIUS + H + i
            at_cor = (i + 1) * 8 if up == 1 else i * 8
            line = S.rx_row[up, i * W : (i + 1) * W, :].astype(F32)
            for g in range(1, NB):
                S.xg[g, er * B : (er + 1) * B, :] = line[g * B - 8 : g * B + 8].astype(BF16)
            ends(er, line, l_cor[at_cor : at_cor + 8], r_cor[at_cor : at_cor + 8])
    for g in range(NG):
        S.xg[g, (2 * RADIUS + H) * B :, :] = jnp.zeros((2 * B, D), BF16)

    def pairs(g, carry):
        kv = dot_nt(S.wqkv[D : 3 * D, :], S.xg[g])
        k = heads(kv[:D])
        inv = lax.rsqrt(jnp.mean(k * k, axis=1, keepdims=True) + EPS)
        kn = flat(k * inv).astype(BF16)
        v = kv[D:].astype(BF16)
        S.kraw[g] = kv[:D]
        S.kinv[g] = inv
        S.kt[g] = kn
        S.vt[g] = v
        S.kc[g] = kn.T
        S.vc[g] = v.T
        return carry

    lax.fori_loop(0, NG, pairs, 0)

    S.gk[0] = jnp.zeros((D, GC), F32)
    S.gv[0] = jnp.zeros((D, GC), F32)
    factor = [S.cos[h] * (1.0 / HW) for h in range(HEADS)]
    lg = [f * math.log2(math.e) for f in factor]

    def attention(j, carry):
        which = jnp.where(j == 0, 0, jnp.where(j == NB - 1, 2, 1))
        for p in range(2):
            ch = slice(p * 2 * HW, (p + 1) * 2 * HW)
            qm, gm = S.qm[j, p], S.gm[j, p]
            keys = jnp.concatenate([S.kc[j, :, ch], S.kc[j + 1, :, ch]], axis=0)
            vals = jnp.concatenate([S.vc[j, :, ch], S.vc[j + 1, :, ch]], axis=0)
            score = dot(keys, qm)
            prod = dot(vals, gm)
            probs, slopes = [], []
            for i in range(2):
                lanes = slice(i * H * B, (i + 1) * H * B)
                e = jnp.exp2(score[:, lanes] * lg[2 * p + i]) * S.mask[which]
                w = e * (1.0 / jnp.sum(e, axis=0, keepdims=True))
                wd = w * prod[:, lanes]
                s = wd - w * jnp.sum(wd, axis=0, keepdims=True)
                probs.append(w.astype(BF16))
                slopes.append(s.astype(BF16))
            prob = jnp.concatenate(probs, axis=1)
            slope = jnp.concatenate(slopes, axis=1)
            keys_t = jnp.concatenate([S.kt[j, ch, :], S.kt[j + 1, ch, :]], axis=1)
            vals_t = jnp.concatenate([S.vt[j, ch, :], S.vt[j + 1, ch, :]], axis=1)
            attn = dot(vals_t, prob)
            grad_q = dot(keys_t, slope)
            for i in range(2):
                lanes = slice(i * H * B, (i + 1) * H * B)
                c = slice(i * HW, (i + 1) * HW)
                o = slice((2 * p + i) * HW, (2 * p + i + 1) * HW)
                S.at[j, o, :] = attn[c, lanes].astype(BF16)
                S.gq[j, o, :] = grad_q[c, lanes] * factor[2 * p + i]
            grad_k = dot_nt(qm, slope)
            grad_v = dot_nt(gm, prob)
            S.gk[j, ch, :] += grad_k[:, :GC]
            S.gk[j + 1, ch, :] = grad_k[:, GC:]
            S.gv[j, ch, :] += grad_v[:, :GC]
            S.gv[j + 1, ch, :] = grad_v[:, GC:]
        return carry

    lax.fori_loop(0, NB, attention, 0)

    def norm_back(raw, inv, grad):
        inner = jnp.mean(grad * raw, axis=1, keepdims=True)
        return inv * (grad - raw * (inv * inv * inner))

    S.wg[...] = jnp.zeros((WT, D), F32)

    def back_q(j, carry):
        g = flat(norm_back(heads(S.qraw[j]), S.qinv[j], heads(S.gq[j]))).astype(BF16)
        S.gqb[j] = g
        S.wg[0:D, :] += dot(g, S.xb[j])
        S.wg[3 * D :, :] += dot(S.at[j], S.gob[j])
        return carry

    lax.fori_loop(0, NB, back_q, 0)
    S.wg[3 * D :, :] = S.wg[3 * D :, :].T

    def back_kv(g, carry):
        gk = heads(S.gk[g])
        gk = jnp.concatenate([gk[h : h + 1] * factor[h] for h in range(HEADS)], axis=0)
        gk = flat(norm_back(heads(S.kraw[g]), S.kinv[g], gk)).astype(BF16)
        gkv = jnp.concatenate([gk, S.gv[g].astype(BF16)], axis=0)
        S.gkv[g] = gkv
        S.wg[D : 3 * D, :] += dot(gkv, S.xg[g])
        return carry

    lax.fori_loop(0, NG, back_kv, 0)

    hw = WT // 2
    S.wb[...] = S.wg[...].astype(BF16)
    mine = pl.ds(pl.multiple_of(core * hw, hw), hw)
    other = pl.ds(pl.multiple_of((1 - core) * hw, hw), hw)
    to_mate = remote(S.wb.at[other], S.rx_half, S.s_core.at[0], S.r_core.at[0], mate)
    to_mate.start()

    def cells_kv(g, carry):
        x = dot(S.wt[:, D:], S.gkv[g]).T
        for er in range(2 * RADIUS + H):
            S.gn[er, pl.ds(pl.multiple_of(g * B, B), B), :] = x[er * B : (er + 1) * B]
        return carry

    lax.fori_loop(0, NG, cells_kv, 0)

    low, high = 8, 8 + W
    rows_at = {-1: 0, 1: RADIUS + H}
    cols_at = {-1: slice(0, 8), 1: slice(high, high + 8)}
    back = []
    for i, (dr, dc) in enumerate(DIRS):
        if dc == 0:
            a = rows_at[dr]
            S.tx_row[i] = S.gn[a : a + RADIUS, low:high, :].reshape(RADIUS * W, D).astype(BF16)
            src, dst = S.tx_row.at[i], S.ry_row.at[i]
        elif dr == 0:
            S.tx_col[i - 2] = S.gn[RADIUS : RADIUS + H, cols_at[dc], :].reshape(H * 8, D).astype(BF16)
            src, dst = S.tx_col.at[i - 2], S.ry_col.at[i - 2]
        else:
            a = rows_at[dr]
            cor = S.gn[a : a + RADIUS, cols_at[dc], :].reshape(RADIUS * 8, D)
            S.tx_cor[i - 4] = jnp.concatenate([cor, jnp.zeros((8, D), F32)], axis=0).astype(BF16)
            src, dst = S.tx_cor.at[i - 4], S.ry_cor.at[i - 4]
        back.append(remote(src, dst, S.s_ret.at[i], S.r_ret.at[i], at(dr, dc)))
        back[-1].start()

    to_mate.wait_recv()
    half = S.wg[mine, :] + S.rx_half[...].astype(F32)
    S.half[...] = half
    S.hb[...] = half.astype(BF16)
    scatter = []
    for k in range(1, nc):
        t = lax.rem(col + k, nc)
        scatter.append(
            remote(
                S.hb.at[pl.ds(pl.multiple_of(t * cc, cc), cc)],
                S.rx_pl.at[k],
                S.s_pl.at[0, k],
                S.r_pl.at[0, k],
                (row, t),
            )
        )
        scatter[-1].start()

    def cells_q(j, carry):
        x = dot(S.wt[:, 0:D], S.gqb[j]).T
        for r in range(H):
            S.gn[RADIUS + r, pl.ds(pl.multiple_of(j * B + 8, 8), B), :] += x[r * B : (r + 1) * B]
        return carry

    lax.fori_loop(0, NB, cells_q, 0)

    for c in scatter:
        c.wait_recv()
    chunk = S.half[pl.ds(pl.multiple_of(col * cc, cc), cc), :]
    for k in range(1, nc):
        chunk = chunk + S.rx_pl[k].astype(F32)
    S.ys[ypos] = chunk
    over_y = []
    for m in range(1, ny):
        over_y.append(remote(S.ys.at[ypos], S.ys.at[ypos], S.s_y.at[m], S.r_y.at[m], at(2 * m, 0)))
        over_y[-1].start()

    for c in back:
        c.wait_recv()
    first, last = RADIUS, RADIUS + H - RADIUS
    S.gn[last : last + RADIUS, low:high, :] += S.ry_row[0].astype(F32).reshape(RADIUS, W, D)
    S.gn[first : first + RADIUS, low:high, :] += S.ry_row[1].astype(F32).reshape(RADIUS, W, D)
    S.gn[first : first + H, high - 8 : high, :] += S.ry_col[0].astype(F32).reshape(H, 8, D)
    S.gn[first : first + H, low : low + 8, :] += S.ry_col[1].astype(F32).reshape(H, 8, D)
    for i, (dr, dc) in enumerate(DIRS[4:]):
        a = last if dr == -1 else first
        b = high - 8 if dc == -1 else low
        cor = S.ry_cor[i].astype(F32)[: RADIUS * 8]
        S.gn[a : a + RADIUS, b : b + 8, :] += cor.reshape(RADIUS, 8, D)

    for c in over_y:
        c.wait_recv()
    chunk = S.ys[0]
    for m in range(1, ny):
        chunk = chunk + S.ys[m]
    chunk = chunk * (1.0 / math.sqrt(nr * H * nc * W))
    place = pl.ds(pl.multiple_of(core * hw + col * cc, cc), cc)
    S.fb[place, :] = chunk.astype(BF16)
    gather = []
    for k in range(1, nc):
        gather.append(
            remote(
                S.fb.at[place],
                S.fb.at[place],
                S.s_pl.at[1, k],
                S.r_pl.at[1, k],
                at(0, k),
            )
        )
        gather[-1].start()

    def last_norm(r, carry):
        g = (S.gn[RADIUS + r, low:high, :] * gain).T
        x = S.l32[pl.ds(r, D, stride=H), :]
        inv = S.inv[pl.ds(r, 1), :]
        inner = jnp.mean(g * x, axis=0, keepdims=True)
        S.l32[pl.ds(r, D, stride=H), :] = inv * (g - x * (inv * inv * inner))
        return carry

    lax.fori_loop(0, H, last_norm, 0)

    def store(i, carry):
        x = S.l32[pl.ds(pl.multiple_of(i * step * H, step * H), step * H), :]
        S.gl[pl.ds(i * step, step)] = x.reshape(step, H, W).astype(BF16)
        return carry

    lax.fori_loop(0, D // step, store, 0)

    for c in gather:
        c.wait_recv()
    done = remote(S.fb.at[mine], S.fb.at[mine], S.s_core.at[1], S.r_core.at[1], mate)
    done.start()
    done.wait_recv()
    S.gwqkv[...] = S.fb[0 : 3 * D, :].astype(F32)
    S.gwo[...] = S.fb[3 * D :, :].astype(F32)

    for c in halo + back + scatter + over_y + gather + [to_mate, done]:
        c.wait_send()


def solution(mesh):
    nr, nc = mesh.shape["row"], mesh.shape["col"]
    scratch = scratch_shapes(nr, nc)
    names = ["lat", "gain", "wqkv", "wo", "cos", "go", "gl", "gwqkv", "gwo", *scratch]

    def per_device(latent, norm_gain, qkv_weight, out_weight, cos_scale, grad_output):
        vmem = pl.BlockSpec(memory_space=pltpu.VMEM)
        return pl.pallas_call(
            functools.partial(kernel, nr, nc, names),
            out_shape=(
                jax.ShapeDtypeStruct((D, H, W), BF16),
                jax.ShapeDtypeStruct((3 * D, D), F32),
                jax.ShapeDtypeStruct((D, D), F32),
            ),
            in_specs=[vmem, vmem, vmem, vmem, pl.BlockSpec(memory_space=pltpu.SMEM), vmem],
            out_specs=(vmem, vmem, vmem),
            scratch_shapes=list(scratch.values()),
            compiler_params=pltpu.CompilerParams(
                collective_id=0, has_side_effects=True, vmem_limit_bytes=60 * 2**20
            ),
        )(latent, norm_gain.reshape(1, D), qkv_weight, out_weight, cos_scale, grad_output)

    return jax.shard_map(
        per_device,
        mesh=mesh,
        in_specs=(P(None, "row", "col"), P(), P(), P(), P(), P(None, "row", "col")),
        out_specs=(P(None, "row", "col"), P(), P()),
        check_vma=False,
    )
```

```python
import collections
import functools
import math

import jax
import jax.numpy as jnp
from jax import lax
from jax.experimental import pallas as pl
from jax.experimental.pallas import tpu as pltpu
from jax.sharding import PartitionSpec as P

MESH = pl.DeviceIdType.MESH
F32 = jnp.float32
BF16 = jnp.bfloat16

D = 256
HEADS = 4
HW = 64
RADIUS = 3
EPS = 1e-06
H = 8
W = 128
B = 16
NB = W // B
NG = NB + 1
ER = 16
GC = ER * B
WT = 4 * D
CHUNK = 64

DIRS = ((-1, 0), (1, 0), (0, -1), (0, 1), (-1, -1), (-1, 1), (1, -1), (1, 1))


def dot(a, b):
    return lax.dot_general(a, b, (((1,), (0,)), ((), ())), preferred_element_type=F32)


def dot_nt(a, b):
    return lax.dot_general(a, b, (((1,), (1,)), ((), ())), preferred_element_type=F32)


def heads(x):
    return x.reshape(HEADS, HW, x.shape[-1])


def flat(x):
    return x.reshape(HEADS * HW, x.shape[-1])


def scratch_shapes(nr, nc):
    cc = 2 * D // nc
    return collections.OrderedDict(
        l32=pltpu.VMEM((D * H, W), F32),
        g32=pltpu.VMEM((D * H, W), F32),
        inv=pltpu.VMEM((H, W), F32),
        xr=pltpu.VMEM((H * W, D), BF16),
        xe32=pltpu.VMEM((2, H * 8, D), F32),
        xe=pltpu.VMEM((2, H * 8, D), BF16),
        rx_row=pltpu.VMEM((2, RADIUS * W, D), BF16),
        rx_col=pltpu.VMEM((2, H * 8, D), BF16),
        rx_cor=pltpu.VMEM((4, 32, D), BF16),
        xg=pltpu.VMEM((NG, GC, D), BF16),
        xb=pltpu.VMEM((NB, H * B, D), BF16),
        gob=pltpu.VMEM((NB, H * B, D), BF16),
        wot=pltpu.VMEM((D, D), BF16),
        wt=pltpu.VMEM((D, 3 * D), BF16),
        kraw=pltpu.VMEM((NG, D, GC), F32),
        kinv=pltpu.VMEM((NG, HEADS, 1, GC), F32),
        kc=pltpu.VMEM((NG, GC, D), BF16),
        vc=pltpu.VMEM((NG, GC, D), BF16),
        kt=pltpu.VMEM((NG, D, GC), BF16),
        vt=pltpu.VMEM((NG, D, GC), BF16),
        qraw=pltpu.VMEM((NB, D, H * B), F32),
        qinv=pltpu.VMEM((NB, HEADS, 1, H * B), F32),
        qm=pltpu.VMEM((NB, 2, 2 * HW, 2 * H * B), BF16),
        gm=pltpu.VMEM((NB, 2, 2 * HW, 2 * H * B), BF16),
        mask=pltpu.VMEM((3, 2 * GC, H * B), F32),
        eb=pltpu.VMEM((2, 2 * GC, 2 * H * B), BF16),
        sb=pltpu.VMEM((2, 2 * GC, 2 * H * B), BF16),
        gk=pltpu.VMEM((NG, D, GC), F32),
        gv=pltpu.VMEM((NG, D, GC), F32),
        gq=pltpu.VMEM((NB, D, H * B), F32),
        at=pltpu.VMEM((NB, D, H * B), BF16),
        gqb=pltpu.VMEM((NB, D, H * B), BF16),
        gkv=pltpu.VMEM((NG, 2 * D, GC), BF16),
        gn=pltpu.VMEM((2 * RADIUS + H, NG * B, D), F32),
        tx_row=pltpu.VMEM((2, RADIUS * W, D), BF16),
        tx_col=pltpu.VMEM((2, H * 8, D), BF16),
        tx_cor=pltpu.VMEM((4, 32, D), BF16),
        ry_row=pltpu.VMEM((2, RADIUS * W, D), BF16),
        ry_col=pltpu.VMEM((2, H * 8, D), BF16),
        ry_cor=pltpu.VMEM((4, 32, D), BF16),
        wg=pltpu.VMEM((WT, D), F32),
        wb=pltpu.VMEM((WT, D), BF16),
        rx_half=pltpu.VMEM((WT // 2, D), BF16),
        half=pltpu.VMEM((WT // 2, D), F32),
        hb=pltpu.VMEM((WT // 2, D), BF16),
        rx_pl=pltpu.VMEM((nc, cc, D), BF16),
        ys=pltpu.VMEM((nr // 2, cc, D), F32),
        fb=pltpu.VMEM((WT, D), BF16),
        s_hal=pltpu.SemaphoreType.DMA((8,)),
        r_hal=pltpu.SemaphoreType.DMA((8,)),
        s_ret=pltpu.SemaphoreType.DMA((8,)),
        r_ret=pltpu.SemaphoreType.DMA((8,)),
        s_core=pltpu.SemaphoreType.DMA((2,)),
        r_core=pltpu.SemaphoreType.DMA((2,)),
        s_pl=pltpu.SemaphoreType.DMA((2, nc)),
        r_pl=pltpu.SemaphoreType.DMA((2, nc)),
        s_y=pltpu.SemaphoreType.DMA((nr // 2,)),
        r_y=pltpu.SemaphoreType.DMA((nr // 2,)),
    )


def kernel(nr, nc, names, *refs):
    S = collections.namedtuple("S", names)(*refs)
    row, col = lax.axis_index("row"), lax.axis_index("col")
    core, ypos = lax.rem(row, 2), lax.div(row, 2)
    ny = nr // 2
    cc = 2 * D // nc

    def at(dr, dc):
        return (lax.rem(row + (dr % nr), nr), lax.rem(col + (dc % nc), nc))

    mate = (row + 1 - 2 * core, col)

    def remote(src, dst, send, recv, device):
        return pltpu.make_async_remote_copy(
            src_ref=src, dst_ref=dst, send_sem=send, recv_sem=recv, device_id=device, device_id_type=MESH
        )

    partners = list(DIRS)
    partners += [(0, k) for k in range(2, nc - 1)]
    partners += [(2 * m, 0) for m in range(1, ny)]
    barrier = pltpu.get_barrier_semaphore()
    for dr, dc in partners:
        pl.semaphore_signal(barrier, inc=1, device_id=at(dr, dc), device_id_type=MESH)

    step = 32

    def load(i, acc):
        x = S.lat[pl.ds(i * step, step)].astype(F32)
        S.l32[pl.ds(pl.multiple_of(i * step * H, step * H), step * H), :] = x.reshape(step * H, W)
        g = S.go[pl.ds(i * step, step)].astype(F32)
        S.g32[pl.ds(pl.multiple_of(i * step * H, step * H), step * H), :] = g.reshape(step * H, W)
        return acc + jnp.sum(x * x, axis=0)

    total = lax.fori_loop(0, D // step, load, jnp.zeros((H, W), F32))
    S.inv[...] = lax.rsqrt(total * (1.0 / D) + EPS)
    gain = S.gain[...]

    def cells(r, carry):
        x = S.l32[pl.ds(r, D, stride=H), :] * S.inv[pl.ds(r, 1), :]
        xn = x.T * gain
        xnb = xn.astype(BF16)
        S.xr[pl.ds(pl.multiple_of(r * W, W), W), :] = xnb
        S.xe32[0, pl.ds(pl.multiple_of(r * 8, 8), 8), :] = xn[:8]
        S.xe32[1, pl.ds(pl.multiple_of(r * 8, 8), 8), :] = xn[W - 8 :]
        own = pl.ds(pl.multiple_of(r * B, B), B)
        ext = pl.ds(pl.multiple_of(r * B + RADIUS * B, B), B)
        for j in range(NB):
            S.xb[j, own, :] = xnb[j * B : (j + 1) * B]
        for g in range(1, NB):
            S.xg[g, ext, :] = xn[g * B - 8 : g * B + 8].astype(BF16)
        return carry

    lax.fori_loop(0, H, cells, 0, unroll=True)
    S.xe[...] = S.xe32[...].astype(BF16)

    pl.semaphore_wait(barrier, len(partners))
    near = 3 * W
    edge = {-1: slice(0, near), 1: slice(H * W - near, H * W)}
    part = {-1: slice(0, 32), 1: slice(32, 64)}
    halo = []
    for i, (dr, dc) in enumerate(DIRS):
        if dc == 0:
            src, dst = S.xr.at[edge[dr]], S.rx_row.at[i]
        elif dr == 0:
            src, dst = S.xe.at[(dc + 1) // 2], S.rx_col.at[i - 2]
        else:
            src, dst = S.xe.at[(dc + 1) // 2, part[dr]], S.rx_cor.at[i - 4]
        halo.append(remote(src, dst, S.s_hal.at[i], S.r_hal.at[i], at(dr, dc)))
        halo[-1].start()

    S.wot[...] = S.wo[...].T
    for i in range(3):
        S.wt[:, i * D : (i + 1) * D] = S.wqkv[i * D : (i + 1) * D, :].T

    def grads(r, carry):
        g = S.g32[pl.ds(r, D, stride=H), :].T.astype(BF16)
        own = pl.ds(pl.multiple_of(r * B, B), B)
        for j in range(NB):
            S.gob[j, own, :] = g[j * B : (j + 1) * B]
        return carry

    lax.fori_loop(0, H, grads, 0, unroll=True)

    mshape = (2, ER, B, H * B)
    half_, kr, kc = (lax.broadcasted_iota(jnp.int32, mshape, a) for a in range(3))
    lane = lax.broadcasted_iota(jnp.int32, mshape, 3)
    qr, qc = lax.div(lane, B), lax.rem(lane, B)
    dr = kr - RADIUS - qr
    off = B * half_ + kc - 8
    dc = off - qc
    grow = row * H + kr - RADIUS
    ok = (dr >= -RADIUS) & (dr <= RADIUS) & (dc >= -RADIUS) & (dc <= RADIUS)
    ok = ok & (grow >= 0) & (grow < nr * H)
    one = jnp.where(ok, 1.0, 0.0).astype(F32).reshape(2 * GC, H * B)
    off = off.reshape(2 * GC, H * B)
    S.mask[0] = jnp.where((col * W + off >= 0), one, 0.0)
    S.mask[1] = one
    S.mask[2] = jnp.where(col * W + W - B + off < nc * W, one, 0.0)

    def queries(j, carry):
        q = heads(dot_nt(S.wqkv[0:D, :], S.xb[j]))
        inv = lax.rsqrt(jnp.mean(q * q, axis=1, keepdims=True) + EPS)
        qn = (q * inv).astype(BF16)
        S.qraw[j] = flat(q)
        S.qinv[j] = inv
        ga = heads(dot_nt(S.wot[...], S.gob[j])).astype(BF16)
        z = jnp.zeros((HW, H * B), BF16)
        for p in range(2):
            for x, out in ((qn, S.qm), (ga, S.gm)):
                out[j, p, 0:HW, :] = jnp.concatenate([x[2 * p], z], axis=1)
                out[j, p, HW : 2 * HW, :] = jnp.concatenate([z, x[2 * p + 1]], axis=1)
        return carry

    lax.fori_loop(0, NB, queries, 0, unroll=True)

    for c in halo:
        c.wait_recv()
    left = S.rx_col[1].astype(F32)
    right = S.rx_col[0].astype(F32)

    def ends(er, cells_, l8, r8):
        S.xg[0, er * B : (er + 1) * B, :] = jnp.concatenate([l8, cells_[:8]], axis=0).astype(BF16)
        S.xg[NB, er * B : (er + 1) * B, :] = jnp.concatenate([cells_[-8:], r8], axis=0).astype(BF16)

    for r in range(H):
        ends(
            r + RADIUS,
            jnp.concatenate([S.xe32[0, r * 8 : r * 8 + 8, :], S.xe32[1, r * 8 : r * 8 + 8, :]], axis=0),
            left[r * 8 : r * 8 + 8],
            right[r * 8 : r * 8 + 8],
        )
    for up in (0, 1):
        l_cor = S.rx_cor[2 * up + 1].astype(F32)
        r_cor = S.rx_cor[2 * up].astype(F32)
        for i in range(RADIUS):
            er = i if up == 1 else RADIUS + H + i
            at_cor = (i + 1) * 8 if up == 1 else i * 8
            line = S.rx_row[up, i * W : (i + 1) * W, :].astype(F32)
            for g in range(1, NB):
                S.xg[g, er * B : (er + 1) * B, :] = line[g * B - 8 : g * B + 8].astype(BF16)
            ends(er, line, l_cor[at_cor : at_cor + 8], r_cor[at_cor : at_cor + 8])
    for g in range(NG):
        S.xg[g, (2 * RADIUS + H) * B :, :] = jnp.zeros((2 * B, D), BF16)

    def pairs(g, carry):
        kv = dot_nt(S.wqkv[D : 3 * D, :], S.xg[g])
        k = heads(kv[:D])
        inv = lax.rsqrt(jnp.mean(k * k, axis=1, keepdims=True) + EPS)
        kn = flat(k * inv).astype(BF16)
        v = kv[D:].astype(BF16)
        S.kraw[g] = kv[:D]
        S.kinv[g] = inv
        S.kt[g] = kn
        S.vt[g] = v
        S.kc[g] = kn.T
        S.vc[g] = v.T
        return carry

    lax.fori_loop(0, NG, pairs, 0, unroll=True)

    S.gk[0] = jnp.zeros((D, GC), F32)
    S.gv[0] = jnp.zeros((D, GC), F32)
    factor = [S.cos[h] * (1.0 / HW) for h in range(HEADS)]
    lg = [f * math.log2(math.e) for f in factor]

    def attention(j, carry):
        which = jnp.where(j == 0, 0, jnp.where(j == NB - 1, 2, 1))
        st = []
        for p in range(2):
            ch = slice(p * 2 * HW, (p + 1) * 2 * HW)
            qm, gm = S.qm[j, p], S.gm[j, p]
            keys = jnp.concatenate([S.kc[j, :, ch], S.kc[j + 1, :, ch]], axis=0)
            vals = jnp.concatenate([S.vc[j, :, ch], S.vc[j + 1, :, ch]], axis=0)
            st.append((dot(keys, qm), dot(vals, gm)))
        for p in range(2):
            ch = slice(p * 2 * HW, (p + 1) * 2 * HW)
            qm, gm = S.qm[j, p], S.gm[j, p]
            score, prod = st[p]
            lgr = jnp.concatenate([jnp.full((1, H * B), lg[2 * p + i], F32) for i in range(2)], axis=1)
            far = jnp.concatenate([jnp.full((1, H * B), factor[2 * p + i], F32) for i in range(2)], axis=1)
            tot = jnp.zeros((8, 2 * H * B), F32)
            ed = jnp.zeros((8, 2 * H * B), F32)
            for c in range(0, 2 * GC, CHUNK):
                mk = S.mask[which, c : c + CHUNK, :]
                e = jnp.exp2(score[c : c + CHUNK] * lgr) * jnp.concatenate([mk, mk], axis=1)
                tot = tot + jnp.sum(e.reshape(CHUNK // 8, 8, 2 * H * B), axis=0)
                ed = ed + jnp.sum((e * prod[c : c + CHUNK]).reshape(CHUNK // 8, 8, 2 * H * B), axis=0)
                S.eb[p, c : c + CHUNK, :] = e.astype(BF16)
            rt = 1.0 / jnp.sum(tot, axis=0, keepdims=True)
            m = jnp.sum(ed, axis=0, keepdims=True) * rt
            for c in range(0, 2 * GC, CHUNK):
                e = S.eb[p, c : c + CHUNK, :].astype(F32)
                S.sb[p, c : c + CHUNK, :] = (e * (prod[c : c + CHUNK] - m)).astype(BF16)
            prob = S.eb[p]
            slope = S.sb[p]
            keys_t = jnp.concatenate([S.kt[j, ch, :], S.kt[j + 1, ch, :]], axis=1)
            vals_t = jnp.concatenate([S.vt[j, ch, :], S.vt[j + 1, ch, :]], axis=1)
            attn = dot(vals_t, prob) * rt
            grad_q = dot(keys_t, slope) * (rt * far)
            for i in range(2):
                lanes = slice(i * H * B, (i + 1) * H * B)
                c = slice(i * HW, (i + 1) * HW)
                o = slice((2 * p + i) * HW, (2 * p + i + 1) * HW)
                S.at[j, o, :] = attn[c, lanes].astype(BF16)
                S.gq[j, o, :] = grad_q[c, lanes]
            qs = (qm.astype(F32) * rt).astype(BF16)
            gs = (gm.astype(F32) * rt).astype(BF16)
            grad_k = dot_nt(qs, slope)
            grad_v = dot_nt(gs, prob)
            S.gk[j, ch, :] += grad_k[:, :GC]
            S.gk[j + 1, ch, :] = grad_k[:, GC:]
            S.gv[j, ch, :] += grad_v[:, :GC]
            S.gv[j + 1, ch, :] = grad_v[:, GC:]
        return carry

    lax.fori_loop(0, NB, attention, 0, unroll=2)

    def norm_back(raw, inv, grad):
        inner = jnp.mean(grad * raw, axis=1, keepdims=True)
        return inv * (grad - raw * (inv * inv * inner))

    S.wg[...] = jnp.zeros((WT, D), F32)

    def back_q(j, carry):
        g = flat(norm_back(heads(S.qraw[j]), S.qinv[j], heads(S.gq[j]))).astype(BF16)
        S.gqb[j] = g
        S.wg[0:D, :] += dot(g, S.xb[j])
        S.wg[3 * D :, :] += dot(S.at[j], S.gob[j])
        return carry

    lax.fori_loop(0, NB, back_q, 0, unroll=True)
    S.wg[3 * D :, :] = S.wg[3 * D :, :].T

    def back_kv(g, carry):
        gk = heads(S.gk[g])
        gk = jnp.concatenate([gk[h : h + 1] * factor[h] for h in range(HEADS)], axis=0)
        gk = flat(norm_back(heads(S.kraw[g]), S.kinv[g], gk)).astype(BF16)
        gkv = jnp.concatenate([gk, S.gv[g].astype(BF16)], axis=0)
        S.gkv[g] = gkv
        S.wg[D : 3 * D, :] += dot(gkv, S.xg[g])
        return carry

    lax.fori_loop(0, NG, back_kv, 0, unroll=True)

    hw = WT // 2
    S.wb[...] = S.wg[...].astype(BF16)
    mine = pl.ds(pl.multiple_of(core * hw, hw), hw)
    other = pl.ds(pl.multiple_of((1 - core) * hw, hw), hw)
    to_mate = remote(S.wb.at[other], S.rx_half, S.s_core.at[0], S.r_core.at[0], mate)
    to_mate.start()

    def cells_kv(g, carry):
        x = dot(S.wt[:, D:], S.gkv[g]).T
        for er in range(2 * RADIUS + H):
            S.gn[er, pl.ds(pl.multiple_of(g * B, B), B), :] = x[er * B : (er + 1) * B]
        return carry

    lax.fori_loop(0, NG, cells_kv, 0, unroll=True)

    low, high = 8, 8 + W
    rows_at = {-1: 0, 1: RADIUS + H}
    cols_at = {-1: slice(0, 8), 1: slice(high, high + 8)}
    back = []
    for i, (dr, dc) in enumerate(DIRS):
        if dc == 0:
            a = rows_at[dr]
            S.tx_row[i] = S.gn[a : a + RADIUS, low:high, :].reshape(RADIUS * W, D).astype(BF16)
            src, dst = S.tx_row.at[i], S.ry_row.at[i]
        elif dr == 0:
            S.tx_col[i - 2] = S.gn[RADIUS : RADIUS + H, cols_at[dc], :].reshape(H * 8, D).astype(BF16)
            src, dst = S.tx_col.at[i - 2], S.ry_col.at[i - 2]
        else:
            a = rows_at[dr]
            cor = S.gn[a : a + RADIUS, cols_at[dc], :].reshape(RADIUS * 8, D)
            S.tx_cor[i - 4] = jnp.concatenate([cor, jnp.zeros((8, D), F32)], axis=0).astype(BF16)
            src, dst = S.tx_cor.at[i - 4], S.ry_cor.at[i - 4]
        back.append(remote(src, dst, S.s_ret.at[i], S.r_ret.at[i], at(dr, dc)))
        back[-1].start()

    to_mate.wait_recv()
    half = S.wg[mine, :] + S.rx_half[...].astype(F32)
    S.half[...] = half
    S.hb[...] = half.astype(BF16)
    scatter = []
    for k in range(1, nc):
        t = lax.rem(col + k, nc)
        scatter.append(
            remote(
                S.hb.at[pl.ds(pl.multiple_of(t * cc, cc), cc)],
                S.rx_pl.at[k],
                S.s_pl.at[0, k],
                S.r_pl.at[0, k],
                (row, t),
            )
        )
        scatter[-1].start()

    def cells_q(j, carry):
        x = dot(S.wt[:, 0:D], S.gqb[j]).T
        for r in range(H):
            S.gn[RADIUS + r, pl.ds(pl.multiple_of(j * B + 8, 8), B), :] += x[r * B : (r + 1) * B]
        return carry

    lax.fori_loop(0, NB, cells_q, 0, unroll=True)

    for c in scatter:
        c.wait_recv()
    chunk = S.half[pl.ds(pl.multiple_of(col * cc, cc), cc), :]
    for k in range(1, nc):
        chunk = chunk + S.rx_pl[k].astype(F32)
    S.ys[ypos] = chunk
    over_y = []
    for m in range(1, ny):
        over_y.append(remote(S.ys.at[ypos], S.ys.at[ypos], S.s_y.at[m], S.r_y.at[m], at(2 * m, 0)))
        over_y[-1].start()

    for c in back:
        c.wait_recv()
    first, last = RADIUS, RADIUS + H - RADIUS
    S.gn[last : last + RADIUS, low:high, :] += S.ry_row[0].astype(F32).reshape(RADIUS, W, D)
    S.gn[first : first + RADIUS, low:high, :] += S.ry_row[1].astype(F32).reshape(RADIUS, W, D)
    S.gn[first : first + H, high - 8 : high, :] += S.ry_col[0].astype(F32).reshape(H, 8, D)
    S.gn[first : first + H, low : low + 8, :] += S.ry_col[1].astype(F32).reshape(H, 8, D)
    for i, (dr, dc) in enumerate(DIRS[4:]):
        a = last if dr == -1 else first
        b = high - 8 if dc == -1 else low
        cor = S.ry_cor[i].astype(F32)[: RADIUS * 8]
        S.gn[a : a + RADIUS, b : b + 8, :] += cor.reshape(RADIUS, 8, D)

    for c in over_y:
        c.wait_recv()
    chunk = S.ys[0]
    for m in range(1, ny):
        chunk = chunk + S.ys[m]
    chunk = chunk * (1.0 / math.sqrt(nr * H * nc * W))
    place = pl.ds(pl.multiple_of(core * hw + col * cc, cc), cc)
    S.fb[place, :] = chunk.astype(BF16)
    gather = []
    for k in range(1, nc):
        gather.append(
            remote(
                S.fb.at[place],
                S.fb.at[place],
                S.s_pl.at[1, k],
                S.r_pl.at[1, k],
                at(0, k),
            )
        )
        gather[-1].start()

    def last_norm(r, carry):
        g = (S.gn[RADIUS + r, low:high, :] * gain).T
        x = S.l32[pl.ds(r, D, stride=H), :]
        inv = S.inv[pl.ds(r, 1), :]
        inner = jnp.mean(g * x, axis=0, keepdims=True)
        S.l32[pl.ds(r, D, stride=H), :] = inv * (g - x * (inv * inv * inner))
        return carry

    lax.fori_loop(0, H, last_norm, 0, unroll=True)

    def store(i, carry):
        x = S.l32[pl.ds(pl.multiple_of(i * step * H, step * H), step * H), :]
        S.gl[pl.ds(i * step, step)] = x.reshape(step, H, W).astype(BF16)
        return carry

    lax.fori_loop(0, D // step, store, 0)

    for c in gather:
        c.wait_recv()
    done = remote(S.fb.at[mine], S.fb.at[mine], S.s_core.at[1], S.r_core.at[1], mate)
    done.start()
    done.wait_recv()
    S.gwqkv[...] = S.fb[0 : 3 * D, :].astype(F32)
    S.gwo[...] = S.fb[3 * D :, :].astype(F32)

    for c in halo + back + scatter + over_y + gather + [to_mate, done]:
        c.wait_send()


def solution(mesh):
    nr, nc = mesh.shape["row"], mesh.shape["col"]
    scratch = scratch_shapes(nr, nc)
    names = ["lat", "gain", "wqkv", "wo", "cos", "go", "gl", "gwqkv", "gwo", *scratch]

    def per_device(latent, norm_gain, qkv_weight, out_weight, cos_scale, grad_output):
        vmem = pl.BlockSpec(memory_space=pltpu.VMEM)
        return pl.pallas_call(
            functools.partial(kernel, nr, nc, names),
            out_shape=(
                jax.ShapeDtypeStruct((D, H, W), BF16),
                jax.ShapeDtypeStruct((3 * D, D), F32),
                jax.ShapeDtypeStruct((D, D), F32),
            ),
            in_specs=[vmem, vmem, vmem, vmem, pl.BlockSpec(memory_space=pltpu.SMEM), vmem],
            out_specs=(vmem, vmem, vmem),
            scratch_shapes=list(scratch.values()),
            compiler_params=pltpu.CompilerParams(
                collective_id=0, has_side_effects=True, vmem_limit_bytes=60 * 2**20
            ),
        )(latent, norm_gain.reshape(1, D), qkv_weight, out_weight, cos_scale, grad_output)

    return jax.shard_map(
        per_device,
        mesh=mesh,
        in_specs=(P(None, "row", "col"), P(), P(), P(), P(), P(None, "row", "col")),
        out_specs=(P(None, "row", "col"), P(), P()),
        check_vma=False,
    )
```

```python
import collections
import functools
import math

import jax
import jax.numpy as jnp
from jax import lax
from jax.experimental import pallas as pl
from jax.experimental.pallas import tpu as pltpu
from jax.sharding import PartitionSpec as P

MESH = pl.DeviceIdType.MESH
F32 = jnp.float32
BF16 = jnp.bfloat16

D = 256
HEADS = 4
HW = 64
PW = 2 * HW
RADIUS = 3
EPS = 1e-06
H = 8
W = 128
B = 16
NB = W // B
QC = H * B
NG = NB + 1
ER = 16
ABOVE, BELOW, UNUSED = H, H + RADIUS, H + 2 * RADIUS
GC = ER * B
CHUNK = 64
WP = 4 * PW
HALF = WP // 2

DIRS = ((-1, 0), (1, 0), (0, -1), (0, 1), (-1, -1), (-1, 1), (1, -1), (1, 1))


def dot(a, b):
    return lax.dot_general(a, b, (((1,), (0,)), ((), ())), preferred_element_type=F32)


def dot_nt(a, b):
    return lax.dot_general(a, b, (((1,), (1,)), ((), ())), preferred_element_type=F32)


def heads(x):
    return x.reshape(x.shape[0] // HW, HW, x.shape[-1])


def flat(x):
    return x.reshape(x.shape[0] * HW, x.shape[-1])


def span(i, size):
    return slice(i * size, (i + 1) * size)


def at(i, size):
    return pl.ds(pl.multiple_of(i * size, size), size)


def norm_back(raw, inv, grad):
    inner = jnp.mean(grad * raw, axis=1, keepdims=True)
    return inv * (grad - raw * (inv * inv * inner))


def scratch_shapes(nr, nc):
    cc = HALF // nc
    ny = nr // 2
    dma = pltpu.SemaphoreType.DMA
    return collections.OrderedDict(
        lat=pltpu.VMEM((D, H, W), BF16),
        go=pltpu.VMEM((D, H, W), BF16),
        gain=pltpu.VMEM((1, D), F32),
        wqkv=pltpu.VMEM((3 * D, D), BF16),
        wo=pltpu.VMEM((D, D), BF16),
        gl=pltpu.VMEM((D, H, W), BF16),
        l32=pltpu.VMEM((D * H, W), F32),
        g32=pltpu.VMEM((D * H, W), F32),
        inv=pltpu.VMEM((H, W), F32),
        xr=pltpu.VMEM((H * W, D), BF16),
        xe32=pltpu.VMEM((2, H * 8, D), F32),
        xe=pltpu.VMEM((2, H * 8, D), BF16),
        rx_row=pltpu.VMEM((2, RADIUS * W, D), BF16),
        rx_col=pltpu.VMEM((2, H * 8, D), BF16),
        rx_cor=pltpu.VMEM((4, 32, D), BF16),
        xg=pltpu.VMEM((NG * GC, D), BF16),
        xb=pltpu.VMEM((NB * QC, D), BF16),
        gob=pltpu.VMEM((NB * QC, D), BF16),
        wot=pltpu.VMEM((D, D), BF16),
        wtq=pltpu.VMEM((D, D), BF16),
        wtp=pltpu.VMEM((2, D, 2 * PW), BF16),
        kraw=pltpu.VMEM((NG, D, GC), F32),
        kinv=pltpu.VMEM((NG, HEADS, 1, GC), F32),
        kc=pltpu.VMEM((NG, GC, D), BF16),
        vc=pltpu.VMEM((NG, GC, D), BF16),
        kt=pltpu.VMEM((NG, D, GC), BF16),
        vt=pltpu.VMEM((NG, D, GC), BF16),
        qraw=pltpu.VMEM((NB, D, QC), F32),
        qinv=pltpu.VMEM((NB, HEADS, 1, QC), F32),
        qm=pltpu.VMEM((NB, 2, PW, 2 * QC), BF16),
        gm=pltpu.VMEM((NB, 2, PW, 2 * QC), BF16),
        mask=pltpu.VMEM((3, 2 * GC, QC), F32),
        eb=pltpu.VMEM((2, 2 * GC, 2 * QC), BF16),
        sb=pltpu.VMEM((2, 2 * GC, 2 * QC), BF16),
        gk=pltpu.VMEM((PW, GC), F32),
        gv=pltpu.VMEM((PW, GC), F32),
        att=pltpu.VMEM((2, PW, NB * QC), BF16),
        gqb=pltpu.VMEM((2, PW, NB * QC), BF16),
        gkv=pltpu.VMEM((2, 2 * PW, NG * GC), BF16),
        gn=pltpu.VMEM((UNUSED, NG * B, D), F32),
        tx_row=pltpu.VMEM((2, RADIUS * W, D), BF16),
        tx_col=pltpu.VMEM((2, H * 8, D), BF16),
        tx_cor=pltpu.VMEM((4, 32, D), BF16),
        ry_row=pltpu.VMEM((2, RADIUS * W, D), BF16),
        ry_col=pltpu.VMEM((2, H * 8, D), BF16),
        ry_cor=pltpu.VMEM((4, 32, D), BF16),
        wg=pltpu.VMEM((2, WP, D), F32),
        wb=pltpu.VMEM((2, WP, D), BF16),
        rx_half=pltpu.VMEM((2, HALF, D), BF16),
        half=pltpu.VMEM((2, HALF, D), F32),
        hb=pltpu.VMEM((2, HALF, D), BF16),
        rx_pl=pltpu.VMEM((2, nc, cc, D), BF16),
        ys=pltpu.VMEM((2, ny, cc, D), F32),
        fb=pltpu.VMEM((2, HALF, D), BF16),
        cos=pltpu.SMEM((HEADS,), F32),
        s_in=dma((6,)),
        s_out=dma((3,)),
        s_hal=dma((8,)),
        r_hal=dma((8,)),
        s_ret=dma((8,)),
        r_ret=dma((8,)),
        s_core=dma((2, 2)),
        r_core=dma((2, 2)),
        s_pl=dma((2, 2, nc)),
        r_pl=dma((2, 2, nc)),
        s_y=dma((2, ny)),
        r_y=dma((2, ny)),
    )


def kernel(nr, nc, names, *refs):
    S = collections.namedtuple("S", names)(*refs)
    row, col = lax.axis_index("row"), lax.axis_index("col")
    core, ypos = lax.rem(row, 2), lax.div(row, 2)
    ny = nr // 2
    cc = HALF // nc

    def there(dr, dc):
        return (lax.rem(row + (dr % nr), nr), lax.rem(col + (dc % nc), nc))

    mate = (row + 1 - 2 * core, col)
    sent = []

    def remote(src, dst, send, recv, device):
        return pltpu.make_async_remote_copy(
            src_ref=src, dst_ref=dst, send_sem=send, recv_sem=recv, device_id=device, device_id_type=MESH
        )

    def send(*args):
        copy = remote(*args)
        copy.start()
        sent.append(copy)
        return copy

    partners = list(DIRS)
    partners += [(0, k) for k in range(2, nc - 1)]
    partners += [(2 * m, 0) for m in range(1, ny)]
    barrier = pltpu.get_barrier_semaphore()
    for dr, dc in partners:
        pl.semaphore_signal(barrier, inc=1, device_id=there(dr, dc), device_id_type=MESH)
    loads = []
    for i, (src, dst) in enumerate(
        ((S.h_lat, S.lat), (S.h_gain, S.gain), (S.h_go, S.go), (S.h_wqkv, S.wqkv), (S.h_wo, S.wo), (S.h_cos, S.cos))
    ):
        loads.append(pltpu.make_async_copy(src, dst, S.s_in.at[i]))
        loads[-1].start()

    step = 32

    def load(i, acc):
        x = S.lat[pl.ds(i * step, step)].astype(F32)
        S.l32[at(i, step * H), :] = x.reshape(step * H, W)
        return acc + jnp.sum(x * x, axis=0)

    loads[0].wait()
    total = lax.fori_loop(0, D // step, load, jnp.zeros((H, W), F32))
    S.inv[...] = lax.rsqrt(total * (1.0 / D) + EPS)
    loads[1].wait()
    gain = S.gain[...]

    for r in range(H):
        x = S.l32[pl.ds(r, D, stride=H), :] * S.inv[r : r + 1, :]
        xn = x.T * gain
        xnb = xn.astype(BF16)
        S.xr[span(r, W), :] = xnb
        S.xe32[0, span(r, 8), :] = xn[:8]
        S.xe32[1, span(r, 8), :] = xn[W - 8 :]
        for j in range(NB):
            S.xb[span(j * H + r, B), :] = xnb[span(j, B)]
        for g in range(1, NB):
            S.xg[span(g * ER + r, B), :] = xn[g * B - 8 : g * B + 8].astype(BF16)
    S.xe[...] = S.xe32[...].astype(BF16)

    pl.semaphore_wait(barrier, len(partners))
    near = RADIUS * W
    edge = {-1: slice(0, near), 1: slice(H * W - near, H * W)}
    part = {-1: slice(0, 32), 1: slice(32, 64)}
    halo = []
    for i, (dr, dc) in enumerate(DIRS):
        if dc == 0:
            src, dst = S.xr.at[edge[dr]], S.rx_row.at[i]
        elif dr == 0:
            src, dst = S.xe.at[(dc + 1) // 2], S.rx_col.at[i - 2]
        else:
            src, dst = S.xe.at[(dc + 1) // 2, part[dr]], S.rx_cor.at[i - 4]
        halo.append(send(src, dst, S.s_hal.at[i], S.r_hal.at[i], there(dr, dc)))

    for c in loads[2:]:
        c.wait()
    S.wot[...] = S.wo[...].T
    S.wtq[...] = S.wqkv[0:D, :].T
    for p in range(2):
        for i in range(2):
            a = (1 + i) * D + p * PW
            S.wtp[p, :, span(i, PW)] = S.wqkv[a : a + PW, :].T

    def widen(i, carry):
        x = S.go[pl.ds(i * step, step)].astype(F32)
        S.g32[at(i, step * H), :] = x.reshape(step * H, W)
        return carry

    lax.fori_loop(0, D // step, widen, 0)
    for r in range(H):
        g = S.g32[pl.ds(r, D, stride=H), :].T.astype(BF16)
        for j in range(NB):
            S.gob[span(j * H + r, B), :] = g[span(j, B)]

    mshape = (2, ER, B, QC)
    half_, kr, kc = (lax.broadcasted_iota(jnp.int32, mshape, a) for a in range(3))
    lane = lax.broadcasted_iota(jnp.int32, mshape, 3)
    qr, qc = lax.div(lane, B), lax.rem(lane, B)
    krow = jnp.where(kr < ABOVE, kr, jnp.where(kr < BELOW, kr - ABOVE - RADIUS, kr - BELOW + H))
    dr = krow - qr
    off = B * half_ + kc - 8
    dc = off - qc
    grow = row * H + krow
    ok = (dr >= -RADIUS) & (dr <= RADIUS) & (dc >= -RADIUS) & (dc <= RADIUS)
    ok = ok & (grow >= 0) & (grow < nr * H) & (kr < UNUSED)
    one = jnp.where(ok, 1.0, 0.0).astype(F32).reshape(2 * GC, QC)
    off = off.reshape(2 * GC, QC)
    S.mask[0] = jnp.where(col * W + off >= 0, one, 0.0)
    S.mask[1] = one
    S.mask[2] = jnp.where(col * W + W - B + off < nc * W, one, 0.0)

    zero = jnp.zeros((HW, QC), BF16)
    for j in range(NB):
        q = heads(dot_nt(S.wqkv[0:D, :], S.xb[span(j, QC), :]))
        inv = lax.rsqrt(jnp.mean(q * q, axis=1, keepdims=True) + EPS)
        qn = (q * inv).astype(BF16)
        S.qraw[j] = flat(q)
        S.qinv[j] = inv
        ga = heads(dot_nt(S.wot[...], S.gob[span(j, QC), :])).astype(BF16)
        for p in range(2):
            for x, out in ((qn, S.qm), (ga, S.gm)):
                out[j, p, 0:HW, :] = jnp.concatenate([x[2 * p], zero], axis=1)
                out[j, p, HW:PW, :] = jnp.concatenate([zero, x[2 * p + 1]], axis=1)

    def pairs(*units):
        x = jnp.concatenate([S.xg[span(2 * g + s, GC // 2), :] for g, s in units], axis=0)
        kv = dot_nt(S.wqkv[D : 3 * D, :], x)
        k = heads(kv[:D])
        inv = lax.rsqrt(jnp.mean(k * k, axis=1, keepdims=True) + EPS)
        kn = flat(k * inv).astype(BF16)
        v = kv[D:].astype(BF16)
        knt, vnt = kn.T, v.T
        for n, (g, s) in enumerate(units):
            here, lanes = span(s, GC // 2), span(n, GC // 2)
            S.kraw[g, :, here] = kv[:D, lanes]
            S.kinv[g, :, :, here] = inv[:, :, lanes]
            S.kt[g, :, here] = kn[:, lanes]
            S.vt[g, :, here] = v[:, lanes]
            S.kc[g, here, :] = knt[lanes]
            S.vc[g, here, :] = vnt[lanes]

    for g in range(1, NB - 1, 2):
        pairs((g, 0), (g + 1, 0))

    for c in halo:
        c.wait_recv()
    left = S.rx_col[1].astype(F32)
    right = S.rx_col[0].astype(F32)

    def ends(er, first, last, l8, r8):
        S.xg[span(er, B), :] = jnp.concatenate([l8, first], axis=0).astype(BF16)
        S.xg[span(NB * ER + er, B), :] = jnp.concatenate([last, r8], axis=0).astype(BF16)

    for r in range(H):
        ends(r, S.xe32[0, span(r, 8), :], S.xe32[1, span(r, 8), :], left[span(r, 8)], right[span(r, 8)])
    for down in (0, 1):
        l_cor = S.rx_cor[2 * down + 1].astype(F32)
        r_cor = S.rx_cor[2 * down].astype(F32)
        for i in range(RADIUS):
            er = (ABOVE if down else BELOW) + i
            n = i + 1 if down else i
            line = S.rx_row[down, span(i, W), :].astype(F32)
            for g in range(1, NB):
                S.xg[span(g * ER + er, B), :] = line[g * B - 8 : g * B + 8].astype(BF16)
            ends(er, line[:8], line[-8:], l_cor[span(n, 8)], r_cor[span(n, 8)])
    for g in range(NG):
        S.xg[g * GC + UNUSED * B : (g + 1) * GC, :] = jnp.zeros((2 * B, D), BF16)
    units = [(NB - 1, 0), (0, 0), (NB, 0)] + [(g, 1) for g in range(NG)]
    for n in range(0, len(units), 2):
        pairs(*units[n : n + 2])

    factor = [S.cos[h] * (1.0 / HW) for h in range(HEADS)]

    def by_lane(values):
        return jnp.concatenate([jnp.full((1, QC), x, F32) for x in values], axis=1)

    def key_done(p, g, gk, gv):
        o = span(p, PW)
        gk = jnp.concatenate([gk[span(i, HW)] * factor[2 * p + i] for i in range(2)], axis=0)
        gk = norm_back(heads(S.kraw[g, o, :]), S.kinv[g, 2 * p : 2 * p + 2], heads(gk))
        S.gkv[p, 0:PW, at(g, GC)] = flat(gk).astype(BF16)
        S.gkv[p, PW : 2 * PW, at(g, GC)] = gv.astype(BF16)

    def attention(p, n, carry):
        o = span(p, PW)
        far = by_lane(factor[2 * p : 2 * p + 2])
        lgr = far * math.log2(math.e)
        first = []
        for t in range(2):
            j = 2 * n + t
            keys = jnp.concatenate([S.kc[j, :, o], S.kc[j + 1, :, o]], axis=0)
            vals = jnp.concatenate([S.vc[j, :, o], S.vc[j + 1, :, o]], axis=0)
            first.append((dot(keys, S.qm[j, p]), dot(vals, S.gm[j, p])))
        for t in range(2):
            j = 2 * n + t
            which = jnp.where(j == 0, 0, jnp.where(j == NB - 1, 2, 1))
            score, prod = first[t]
            tot = jnp.zeros((8, 2 * QC), F32)
            ed = jnp.zeros((8, 2 * QC), F32)
            for c in range(0, 2 * GC, CHUNK):
                mk = S.mask[which, c : c + CHUNK, :]
                e = jnp.exp2(score[c : c + CHUNK] * lgr) * jnp.concatenate([mk, mk], axis=1)
                tot = tot + jnp.sum(e.reshape(CHUNK // 8, 8, 2 * QC), axis=0)
                ed = ed + jnp.sum((e * prod[c : c + CHUNK]).reshape(CHUNK // 8, 8, 2 * QC), axis=0)
                S.eb[t, c : c + CHUNK, :] = e.astype(BF16)
            rt = 1.0 / jnp.sum(tot, axis=0, keepdims=True)
            mean = jnp.sum(ed, axis=0, keepdims=True) * rt
            for c in range(0, 2 * GC, CHUNK):
                e = S.eb[t, c : c + CHUNK, :].astype(F32)
                S.sb[t, c : c + CHUNK, :] = (e * (prod[c : c + CHUNK] - mean)).astype(BF16)
            prob = S.eb[t]
            slope = S.sb[t]
            keys_t = jnp.concatenate([S.kt[j, o, :], S.kt[j + 1, o, :]], axis=1)
            vals_t = jnp.concatenate([S.vt[j, o, :], S.vt[j + 1, o, :]], axis=1)
            attn = dot(vals_t, prob) * rt
            grad_q = dot(keys_t, slope) * (rt * far)
            for i in range(2):
                c, lanes = span(i, HW), span(i, QC)
                S.att[p, c, at(j, QC)] = attn[c, lanes].astype(BF16)
                raw = S.qraw[j, span(2 * p + i, HW), :]
                g = norm_back(heads(raw), S.qinv[j, 2 * p + i : 2 * p + i + 1], heads(grad_q[c, lanes]))
                S.gqb[p, c, at(j, QC)] = flat(g).astype(BF16)
            qs = (S.qm[j, p].astype(F32) * rt).astype(BF16)
            gs = (S.gm[j, p].astype(F32) * rt).astype(BF16)
            grad_k = dot_nt(qs, slope)
            grad_v = dot_nt(gs, prob)
            key_done(p, j, S.gk[...] + grad_k[:, :GC], S.gv[...] + grad_v[:, :GC])
            S.gk[...] = grad_k[:, GC:]
            S.gv[...] = grad_v[:, GC:]
        return carry

    def begin():
        S.gk[...] = jnp.zeros((PW, GC), F32)
        S.gv[...] = jnp.zeros((PW, GC), F32)

    def weights(p):
        key_done(p, NB, S.gk[...], S.gv[...])
        S.wg[p, 0:PW, :] = dot(S.gqb[p], S.xb[...])
        S.wg[p, PW : 3 * PW, :] = dot(S.gkv[p], S.xg[...])
        S.wg[p, 3 * PW :, :] = dot(S.att[p], S.gob[...])
        S.wb[p] = S.wg[p].astype(BF16)

    mine = at(core, HALF)

    def to_core(p):
        return [send(S.wb.at[p, at(1 - core, HALF)], S.rx_half.at[p], S.s_core.at[p, 0], S.r_core.at[p, 0], mate)]

    def to_row(p):
        half = S.wg[p, mine, :] + S.rx_half[p].astype(F32)
        S.half[p] = half
        S.hb[p] = half.astype(BF16)
        out = []
        for k in range(1, nc):
            t = lax.rem(col + k, nc)
            out.append(send(S.hb.at[p, at(t, cc)], S.rx_pl.at[p, k], S.s_pl.at[p, 0, k], S.r_pl.at[p, 0, k], (row, t)))
        return out

    def to_y(p):
        chunk = S.half[p, at(col, cc), :]
        for k in range(1, nc):
            chunk = chunk + S.rx_pl[p, k].astype(F32)
        S.ys[p, ypos] = chunk
        slot = S.ys.at[p, ypos]
        return [send(slot, slot, S.s_y.at[p, m], S.r_y.at[p, m], there(2 * m, 0)) for m in range(1, ny)]

    def back_to_row(p):
        chunk = S.ys[p, 0]
        for m in range(1, ny):
            chunk = chunk + S.ys[p, m]
        S.fb[p, at(col, cc), :] = (chunk * (1.0 / math.sqrt(nr * H * nc * W))).astype(BF16)
        slot = S.fb.at[p, at(col, cc)]
        return [send(slot, slot, S.s_pl.at[p, 1, k], S.r_pl.at[p, 1, k], there(0, k)) for k in range(1, nc)]

    stores = []

    def back_to_core(p):
        stores.append(pltpu.make_async_copy(S.fb.at[p], S.h_gw.at[p, mine], S.s_out.at[p]))
        stores[-1].start()
        return [send(S.fb.at[p], S.h_gw.at[p, mine], S.s_core.at[p, 1], S.r_core.at[p, 1], mate)]

    def arrived(copies):
        for c in copies:
            c.wait_recv()

    begin()
    lax.fori_loop(0, NB // 2, functools.partial(attention, 0), 0)
    weights(0)
    core0 = to_core(0)

    begin()
    lax.fori_loop(0, NB // 4, functools.partial(attention, 1), 0)
    arrived(core0)
    row0 = to_row(0)
    lax.fori_loop(NB // 4, NB // 2, functools.partial(attention, 1), 0)
    weights(1)
    core1 = to_core(1)

    def cells_kv(g):
        x = sum(dot(S.wtp[p], S.gkv[p, :, span(g, GC)]) for p in range(2)).T
        for er in range(UNUSED):
            S.gn[er, span(g, B), :] = x[span(er, B)]

    for g in range(4):
        cells_kv(g)
    arrived(core1)
    row1 = to_row(1)
    for g in range(4, NG):
        cells_kv(g)

    low, high = 8, 8 + W
    rows_at = {-1: slice(ABOVE, BELOW), 1: slice(BELOW, UNUSED)}
    cols_at = {-1: slice(0, 8), 1: slice(high, high + 8)}
    back = []
    for i, (dr, dc) in enumerate(DIRS):
        if dc == 0:
            S.tx_row[i] = S.gn[rows_at[dr], low:high, :].reshape(RADIUS * W, D).astype(BF16)
            src, dst = S.tx_row.at[i], S.ry_row.at[i]
        elif dr == 0:
            S.tx_col[i - 2] = S.gn[0:H, cols_at[dc], :].reshape(H * 8, D).astype(BF16)
            src, dst = S.tx_col.at[i - 2], S.ry_col.at[i - 2]
        else:
            cor = S.gn[rows_at[dr], cols_at[dc], :].reshape(RADIUS * 8, D)
            S.tx_cor[i - 4] = jnp.concatenate([cor, jnp.zeros((8, D), F32)], axis=0).astype(BF16)
            src, dst = S.tx_cor.at[i - 4], S.ry_cor.at[i - 4]
        back.append(send(src, dst, S.s_ret.at[i], S.r_ret.at[i], there(dr, dc)))
    arrived(row0)
    y0 = to_y(0)

    for j in range(NB):
        g = jnp.concatenate([S.gqb[p, :, span(j, QC)] for p in range(2)], axis=0)
        x = dot(S.wtq[...], g).T
        for r in range(H):
            S.gn[r, j * B + 8 : j * B + 8 + B, :] += x[span(r, B)]
    arrived(row1)
    y1 = to_y(1)

    arrived(y0)
    gather0 = back_to_row(0)
    arrived(back)
    last = H - RADIUS
    S.gn[last:H, low:high, :] += S.ry_row[0].astype(F32).reshape(RADIUS, W, D)
    S.gn[0:RADIUS, low:high, :] += S.ry_row[1].astype(F32).reshape(RADIUS, W, D)
    S.gn[0:H, high - 8 : high, :] += S.ry_col[0].astype(F32).reshape(H, 8, D)
    S.gn[0:H, low : low + 8, :] += S.ry_col[1].astype(F32).reshape(H, 8, D)
    for i, (dr, dc) in enumerate(DIRS[4:]):
        a = last if dr == -1 else 0
        b = high - 8 if dc == -1 else low
        cor = S.ry_cor[i].astype(F32)[: RADIUS * 8]
        S.gn[a : a + RADIUS, b : b + 8, :] += cor.reshape(RADIUS, 8, D)
    arrived(y1)
    gather1 = back_to_row(1)

    for r in range(H):
        g = (S.gn[r, low:high, :] * gain).T
        x = S.l32[pl.ds(r, D, stride=H), :]
        inv = S.inv[r : r + 1, :]
        inner = jnp.mean(g * x, axis=0, keepdims=True)
        S.l32[pl.ds(r, D, stride=H), :] = inv * (g - x * (inv * inv * inner))

    def store(i, carry):
        S.gl[pl.ds(i * step, step)] = S.l32[at(i, step * H), :].reshape(step, H, W).astype(BF16)
        return carry

    lax.fori_loop(0, D // step, store, 0)
    stores.append(pltpu.make_async_copy(S.gl, S.h_gl, S.s_out.at[2]))
    stores[-1].start()

    arrived(gather0)
    done0 = back_to_core(0)
    arrived(gather1)
    done1 = back_to_core(1)
    arrived(done0)
    arrived(done1)
    for c in stores:
        c.wait()
    for c in sent:
        c.wait_send()


def finish(gl, gw, out, gwqkv, gwo):
    out[...] = gl[...]
    for p in range(2):
        for i in range(3):
            gwqkv[i * D + p * PW : i * D + (p + 1) * PW, :] = gw[p, span(i, PW), :].astype(F32)
        gwo[:, span(p, PW)] = gw[p, 3 * PW :, :].astype(F32).T


def solution(mesh):
    nr, nc = mesh.shape["row"], mesh.shape["col"]
    scratch = scratch_shapes(nr, nc)
    names = ["h_lat", "h_gain", "h_wqkv", "h_wo", "h_cos", "h_go", "h_gl", "h_gw", *scratch]
    hbm = pl.BlockSpec(memory_space=pl.ANY)
    vmem = pl.BlockSpec(memory_space=pltpu.VMEM)

    def per_device(latent, norm_gain, qkv_weight, out_weight, cos_scale, grad_output):
        gl, gw = pl.pallas_call(
            functools.partial(kernel, nr, nc, names),
            out_shape=(jax.ShapeDtypeStruct((D, H, W), BF16), jax.ShapeDtypeStruct((2, WP, D), BF16)),
            in_specs=[hbm] * 6,
            out_specs=(hbm, hbm),
            scratch_shapes=list(scratch.values()),
            compiler_params=pltpu.CompilerParams(
                collective_id=0, has_side_effects=True, vmem_limit_bytes=60 * 2**20
            ),
        )(latent, norm_gain.reshape(1, D), qkv_weight, out_weight, cos_scale, grad_output)
        return pl.pallas_call(
            finish,
            out_shape=(
                jax.ShapeDtypeStruct((D, H, W), BF16),
                jax.ShapeDtypeStruct((3 * D, D), F32),
                jax.ShapeDtypeStruct((D, D), F32),
            ),
            in_specs=[vmem, vmem],
            out_specs=(vmem, vmem, vmem),
                    )(gl, gw)

    return jax.shard_map(
        per_device,
        mesh=mesh,
        in_specs=(P(None, "row", "col"), P(), P(), P(), P(), P(None, "row", "col")),
        out_specs=(P(None, "row", "col"), P(), P()),
        check_vma=False,
    )
```

```python
import collections
import functools
import math

import jax
import jax.numpy as jnp
from jax import lax
from jax.experimental import pallas as pl
from jax.experimental.pallas import tpu as pltpu
from jax.sharding import PartitionSpec as P

MESH = pl.DeviceIdType.MESH
F32 = jnp.float32
BF16 = jnp.bfloat16

D = 256
HEADS = 4
HW = 64
PW = 2 * HW
RADIUS = 3
EPS = 1e-06
H = 8
W = 128
B = 16
NB = W // B
QC = H * B
NG = NB + 1
ER = 16
ABOVE, BELOW, UNUSED = H, H + RADIUS, H + 2 * RADIUS
GC = ER * B
CHUNK = 64
WP = 4 * PW
HALF = WP // 2

DIRS = ((-1, 0), (1, 0), (0, -1), (0, 1), (-1, -1), (-1, 1), (1, -1), (1, 1))


def dot(a, b):
    return lax.dot_general(a, b, (((1,), (0,)), ((), ())), preferred_element_type=F32)


def dot_nt(a, b):
    return lax.dot_general(a, b, (((1,), (1,)), ((), ())), preferred_element_type=F32)


def heads(x):
    return x.reshape(x.shape[0] // HW, HW, x.shape[-1])


def flat(x):
    return x.reshape(x.shape[0] * HW, x.shape[-1])


def span(i, size):
    return slice(i * size, (i + 1) * size)


def at(i, size):
    return pl.ds(pl.multiple_of(i * size, size), size)


def norm_back(raw, inv, grad):
    inner = jnp.mean(grad * raw, axis=1, keepdims=True)
    return inv * (grad - raw * (inv * inv * inner))


def scratch_shapes(nr, nc):
    cc = HALF // nc
    ny = nr // 2
    dma = pltpu.SemaphoreType.DMA
    return collections.OrderedDict(
        lat=pltpu.VMEM((D, H, W), BF16),
        go=pltpu.VMEM((D, H, W), BF16),
        gain=pltpu.VMEM((1, D), F32),
        wqkv=pltpu.VMEM((3 * D, D), BF16),
        wo=pltpu.VMEM((D, D), BF16),
        l32=pltpu.VMEM((D * H, W), F32),
        g32=pltpu.VMEM((D * H, W), F32),
        inv=pltpu.VMEM((H, W), F32),
        xr=pltpu.VMEM((H * W, D), BF16),
        xe32=pltpu.VMEM((2, H * 8, D), F32),
        xe=pltpu.VMEM((2, H * 8, D), BF16),
        rx_row=pltpu.VMEM((2, RADIUS * W, D), BF16),
        rx_col=pltpu.VMEM((2, H * 8, D), BF16),
        rx_cor=pltpu.VMEM((4, 32, D), BF16),
        xg=pltpu.VMEM((NG * GC, D), BF16),
        xb=pltpu.VMEM((NB * QC, D), BF16),
        gob=pltpu.VMEM((NB * QC, D), BF16),
        wot=pltpu.VMEM((D, D), BF16),
        wtq=pltpu.VMEM((D, D), BF16),
        wtp=pltpu.VMEM((2, D, 2 * PW), BF16),
        kraw=pltpu.VMEM((NG, D, GC), F32),
        kinv=pltpu.VMEM((NG, HEADS, 1, GC), F32),
        kc=pltpu.VMEM((NG, GC, D), BF16),
        vc=pltpu.VMEM((NG, GC, D), BF16),
        kt=pltpu.VMEM((NG, D, GC), BF16),
        vt=pltpu.VMEM((NG, D, GC), BF16),
        qraw=pltpu.VMEM((NB, D, QC), F32),
        qinv=pltpu.VMEM((NB, HEADS, 1, QC), F32),
        qm=pltpu.VMEM((NB, 2, PW, 2 * QC), BF16),
        gm=pltpu.VMEM((NB, 2, PW, 2 * QC), BF16),
        mask=pltpu.VMEM((3, 2 * GC, QC), F32),
        eb=pltpu.VMEM((2, 2 * GC, 2 * QC), BF16),
        sb=pltpu.VMEM((2, 2 * GC, 2 * QC), BF16),
        gk=pltpu.VMEM((PW, GC), F32),
        gv=pltpu.VMEM((PW, GC), F32),
        att=pltpu.VMEM((2, PW, NB * QC), BF16),
        gqb=pltpu.VMEM((2, PW, NB * QC), BF16),
        gkv=pltpu.VMEM((2, 2 * PW, NG * GC), BF16),
        gn=pltpu.VMEM((UNUSED, NG * B, D), F32),
        tx_row=pltpu.VMEM((2, RADIUS * W, D), BF16),
        tx_col=pltpu.VMEM((2, H * 8, D), BF16),
        tx_cor=pltpu.VMEM((4, 32, D), BF16),
        ry_row=pltpu.VMEM((2, RADIUS * W, D), BF16),
        ry_col=pltpu.VMEM((2, H * 8, D), BF16),
        ry_cor=pltpu.VMEM((4, 32, D), BF16),
        wg=pltpu.VMEM((2, WP, D), F32),
        wb=pltpu.VMEM((2, WP, D), BF16),
        rx_half=pltpu.VMEM((2, HALF, D), BF16),
        half=pltpu.VMEM((2, HALF, D), F32),
        hb=pltpu.VMEM((2, HALF, D), BF16),
        rx_pl=pltpu.VMEM((2, nc, cc, D), BF16),
        ys=pltpu.VMEM((2, ny, cc, D), F32),
        cos=pltpu.SMEM((HEADS,), F32),
        s_in=dma((6,)),
        s_hal=dma((8,)),
        r_hal=dma((8,)),
        s_ret=dma((8,)),
        r_ret=dma((8,)),
        s_core=dma((2, 2)),
        r_core=dma((2, 2)),
        s_pl=dma((2, 2, nc)),
        r_pl=dma((2, 2, nc)),
        s_y=dma((2, ny)),
        r_y=dma((2, ny)),
    )


def kernel(nr, nc, names, *refs):
    S = collections.namedtuple("S", names)(*refs)
    row, col = lax.axis_index("row"), lax.axis_index("col")
    core, ypos = lax.rem(row, 2), lax.div(row, 2)
    ny = nr // 2
    cc = HALF // nc

    def there(dr, dc):
        return (lax.rem(row + (dr % nr), nr), lax.rem(col + (dc % nc), nc))

    mate = (row + 1 - 2 * core, col)
    sent = []

    def remote(src, dst, send, recv, device):
        return pltpu.make_async_remote_copy(
            src_ref=src, dst_ref=dst, send_sem=send, recv_sem=recv, device_id=device, device_id_type=MESH
        )

    def send(*args):
        copy = remote(*args)
        copy.start()
        sent.append(copy)
        return copy

    partners = list(DIRS)
    partners += [(0, k) for k in range(2, nc - 1)]
    partners += [(2 * m, 0) for m in range(1, ny)]
    barrier = pltpu.get_barrier_semaphore()
    for dr, dc in partners:
        pl.semaphore_signal(barrier, inc=1, device_id=there(dr, dc), device_id_type=MESH)
    loads = []
    for i, (src, dst) in enumerate(
        ((S.h_lat, S.lat), (S.h_gain, S.gain), (S.h_go, S.go), (S.h_wqkv, S.wqkv), (S.h_wo, S.wo), (S.h_cos, S.cos))
    ):
        loads.append(pltpu.make_async_copy(src, dst, S.s_in.at[i]))
        loads[-1].start()

    step = 32

    def load(i, acc):
        x = S.lat[pl.ds(i * step, step)].astype(F32)
        S.l32[at(i, step * H), :] = x.reshape(step * H, W)
        return acc + jnp.sum(x * x, axis=0)

    loads[0].wait()
    total = lax.fori_loop(0, D // step, load, jnp.zeros((H, W), F32))
    S.inv[...] = lax.rsqrt(total * (1.0 / D) + EPS)
    loads[1].wait()
    gain = S.gain[...]

    for r in range(H):
        x = S.l32[pl.ds(r, D, stride=H), :] * S.inv[r : r + 1, :]
        xn = x.T * gain
        xnb = xn.astype(BF16)
        S.xr[span(r, W), :] = xnb
        S.xe32[0, span(r, 8), :] = xn[:8]
        S.xe32[1, span(r, 8), :] = xn[W - 8 :]
        for j in range(NB):
            S.xb[span(j * H + r, B), :] = xnb[span(j, B)]
        for g in range(1, NB):
            S.xg[span(g * ER + r, B), :] = xn[g * B - 8 : g * B + 8].astype(BF16)
    S.xe[...] = S.xe32[...].astype(BF16)

    pl.semaphore_wait(barrier, len(partners))
    near = RADIUS * W
    edge = {-1: slice(0, near), 1: slice(H * W - near, H * W)}
    part = {-1: slice(0, 32), 1: slice(32, 64)}
    halo = []
    for i, (dr, dc) in enumerate(DIRS):
        if dc == 0:
            src, dst = S.xr.at[edge[dr]], S.rx_row.at[i]
        elif dr == 0:
            src, dst = S.xe.at[(dc + 1) // 2], S.rx_col.at[i - 2]
        else:
            src, dst = S.xe.at[(dc + 1) // 2, part[dr]], S.rx_cor.at[i - 4]
        halo.append(send(src, dst, S.s_hal.at[i], S.r_hal.at[i], there(dr, dc)))

    for c in loads[2:]:
        c.wait()
    S.wot[...] = S.wo[...].T
    S.wtq[...] = S.wqkv[0:D, :].T
    for p in range(2):
        for i in range(2):
            a = (1 + i) * D + p * PW
            S.wtp[p, :, span(i, PW)] = S.wqkv[a : a + PW, :].T

    def widen(i, carry):
        x = S.go[pl.ds(i * step, step)].astype(F32)
        S.g32[at(i, step * H), :] = x.reshape(step * H, W)
        return carry

    lax.fori_loop(0, D // step, widen, 0)
    for r in range(H):
        g = S.g32[pl.ds(r, D, stride=H), :].T.astype(BF16)
        for j in range(NB):
            S.gob[span(j * H + r, B), :] = g[span(j, B)]

    mshape = (2, ER, B, QC)
    half_, kr, kc = (lax.broadcasted_iota(jnp.int32, mshape, a) for a in range(3))
    lane = lax.broadcasted_iota(jnp.int32, mshape, 3)
    qr, qc = lax.div(lane, B), lax.rem(lane, B)
    krow = jnp.where(kr < ABOVE, kr, jnp.where(kr < BELOW, kr - ABOVE - RADIUS, kr - BELOW + H))
    dr = krow - qr
    off = B * half_ + kc - 8
    dc = off - qc
    grow = row * H + krow
    ok = (dr >= -RADIUS) & (dr <= RADIUS) & (dc >= -RADIUS) & (dc <= RADIUS)
    ok = ok & (grow >= 0) & (grow < nr * H) & (kr < UNUSED)
    one = jnp.where(ok, 1.0, 0.0).astype(F32).reshape(2 * GC, QC)
    off = off.reshape(2 * GC, QC)
    S.mask[0] = jnp.where(col * W + off >= 0, one, 0.0)
    S.mask[1] = one
    S.mask[2] = jnp.where(col * W + W - B + off < nc * W, one, 0.0)

    zero = jnp.zeros((HW, QC), BF16)
    for j in range(NB):
        q = heads(dot_nt(S.wqkv[0:D, :], S.xb[span(j, QC), :]))
        inv = lax.rsqrt(jnp.mean(q * q, axis=1, keepdims=True) + EPS)
        qn = (q * inv).astype(BF16)
        S.qraw[j] = flat(q)
        S.qinv[j] = inv
        ga = heads(dot_nt(S.wot[...], S.gob[span(j, QC), :])).astype(BF16)
        for p in range(2):
            for x, out in ((qn, S.qm), (ga, S.gm)):
                out[j, p, 0:HW, :] = jnp.concatenate([x[2 * p], zero], axis=1)
                out[j, p, HW:PW, :] = jnp.concatenate([zero, x[2 * p + 1]], axis=1)

    def pairs(*units):
        x = jnp.concatenate([S.xg[span(2 * g + s, GC // 2), :] for g, s in units], axis=0)
        kv = dot_nt(S.wqkv[D : 3 * D, :], x)
        k = heads(kv[:D])
        inv = lax.rsqrt(jnp.mean(k * k, axis=1, keepdims=True) + EPS)
        kn = flat(k * inv).astype(BF16)
        v = kv[D:].astype(BF16)
        knt, vnt = kn.T, v.T
        for n, (g, s) in enumerate(units):
            here, lanes = span(s, GC // 2), span(n, GC // 2)
            S.kraw[g, :, here] = kv[:D, lanes]
            S.kinv[g, :, :, here] = inv[:, :, lanes]
            S.kt[g, :, here] = kn[:, lanes]
            S.vt[g, :, here] = v[:, lanes]
            S.kc[g, here, :] = knt[lanes]
            S.vc[g, here, :] = vnt[lanes]

    for g in range(1, NB - 1, 2):
        pairs((g, 0), (g + 1, 0))

    for c in halo:
        c.wait_recv()
    left = S.rx_col[1].astype(F32)
    right = S.rx_col[0].astype(F32)

    def ends(er, first, last, l8, r8):
        S.xg[span(er, B), :] = jnp.concatenate([l8, first], axis=0).astype(BF16)
        S.xg[span(NB * ER + er, B), :] = jnp.concatenate([last, r8], axis=0).astype(BF16)

    for r in range(H):
        ends(r, S.xe32[0, span(r, 8), :], S.xe32[1, span(r, 8), :], left[span(r, 8)], right[span(r, 8)])
    for down in (0, 1):
        l_cor = S.rx_cor[2 * down + 1].astype(F32)
        r_cor = S.rx_cor[2 * down].astype(F32)
        for i in range(RADIUS):
            er = (ABOVE if down else BELOW) + i
            n = i + 1 if down else i
            line = S.rx_row[down, span(i, W), :].astype(F32)
            for g in range(1, NB):
                S.xg[span(g * ER + er, B), :] = line[g * B - 8 : g * B + 8].astype(BF16)
            ends(er, line[:8], line[-8:], l_cor[span(n, 8)], r_cor[span(n, 8)])
    for g in range(NG):
        S.xg[g * GC + UNUSED * B : (g + 1) * GC, :] = jnp.zeros((2 * B, D), BF16)
    units = [(NB - 1, 0), (0, 0), (NB, 0)] + [(g, 1) for g in range(NG)]
    for n in range(0, len(units), 2):
        pairs(*units[n : n + 2])

    factor = [S.cos[h] * (1.0 / HW) for h in range(HEADS)]

    def by_lane(values):
        return jnp.concatenate([jnp.full((1, QC), x, F32) for x in values], axis=1)

    def key_done(p, g, gk, gv):
        o = span(p, PW)
        gk = jnp.concatenate([gk[span(i, HW)] * factor[2 * p + i] for i in range(2)], axis=0)
        gk = norm_back(heads(S.kraw[g, o, :]), S.kinv[g, 2 * p : 2 * p + 2], heads(gk))
        S.gkv[p, 0:PW, at(g, GC)] = flat(gk).astype(BF16)
        S.gkv[p, PW : 2 * PW, at(g, GC)] = gv.astype(BF16)

    def attention(p, n, carry):
        o = span(p, PW)
        far = by_lane(factor[2 * p : 2 * p + 2])
        lgr = far * math.log2(math.e)
        first = []
        for t in range(2):
            j = 2 * n + t
            keys = jnp.concatenate([S.kc[j, :, o], S.kc[j + 1, :, o]], axis=0)
            vals = jnp.concatenate([S.vc[j, :, o], S.vc[j + 1, :, o]], axis=0)
            first.append((dot(keys, S.qm[j, p]), dot(vals, S.gm[j, p])))
        for t in range(2):
            j = 2 * n + t
            which = jnp.where(j == 0, 0, jnp.where(j == NB - 1, 2, 1))
            score, prod = first[t]
            tot = jnp.zeros((8, 2 * QC), F32)
            ed = jnp.zeros((8, 2 * QC), F32)
            for c in range(0, 2 * GC, CHUNK):
                mk = S.mask[which, c : c + CHUNK, :]
                e = jnp.exp2(score[c : c + CHUNK] * lgr) * jnp.concatenate([mk, mk], axis=1)
                tot = tot + jnp.sum(e.reshape(CHUNK // 8, 8, 2 * QC), axis=0)
                ed = ed + jnp.sum((e * prod[c : c + CHUNK]).reshape(CHUNK // 8, 8, 2 * QC), axis=0)
                S.eb[t, c : c + CHUNK, :] = e.astype(BF16)
            rt = 1.0 / jnp.sum(tot, axis=0, keepdims=True)
            mean = jnp.sum(ed, axis=0, keepdims=True) * rt
            for c in range(0, 2 * GC, CHUNK):
                e = S.eb[t, c : c + CHUNK, :].astype(F32)
                S.sb[t, c : c + CHUNK, :] = (e * (prod[c : c + CHUNK] - mean)).astype(BF16)
            prob = S.eb[t]
            slope = S.sb[t]
            keys_t = jnp.concatenate([S.kt[j, o, :], S.kt[j + 1, o, :]], axis=1)
            vals_t = jnp.concatenate([S.vt[j, o, :], S.vt[j + 1, o, :]], axis=1)
            attn = dot(vals_t, prob) * rt
            grad_q = dot(keys_t, slope) * (rt * far)
            for i in range(2):
                c, lanes = span(i, HW), span(i, QC)
                S.att[p, c, at(j, QC)] = attn[c, lanes].astype(BF16)
                raw = S.qraw[j, span(2 * p + i, HW), :]
                g = norm_back(heads(raw), S.qinv[j, 2 * p + i : 2 * p + i + 1], heads(grad_q[c, lanes]))
                S.gqb[p, c, at(j, QC)] = flat(g).astype(BF16)
            qs = (S.qm[j, p].astype(F32) * rt).astype(BF16)
            gs = (S.gm[j, p].astype(F32) * rt).astype(BF16)
            grad_k = dot_nt(qs, slope)
            grad_v = dot_nt(gs, prob)
            key_done(p, j, S.gk[...] + grad_k[:, :GC], S.gv[...] + grad_v[:, :GC])
            S.gk[...] = grad_k[:, GC:]
            S.gv[...] = grad_v[:, GC:]
        return carry

    def begin():
        S.gk[...] = jnp.zeros((PW, GC), F32)
        S.gv[...] = jnp.zeros((PW, GC), F32)

    def weights(p):
        key_done(p, NB, S.gk[...], S.gv[...])
        S.wg[p, 0:PW, :] = dot(S.gqb[p], S.xb[...])
        S.wg[p, PW : 3 * PW, :] = dot(S.gkv[p], S.xg[...])
        S.wg[p, 3 * PW :, :] = dot(S.att[p], S.gob[...])
        S.wb[p] = S.wg[p].astype(BF16)

    mine = at(core, HALF)

    def to_core(p):
        return [send(S.wb.at[p, at(1 - core, HALF)], S.rx_half.at[p], S.s_core.at[p, 0], S.r_core.at[p, 0], mate)]

    def to_row(p):
        half = S.wg[p, mine, :] + S.rx_half[p].astype(F32)
        S.half[p] = half
        S.hb[p] = half.astype(BF16)
        out = []
        for k in range(1, nc):
            t = lax.rem(col + k, nc)
            out.append(send(S.hb.at[p, at(t, cc)], S.rx_pl.at[p, k], S.s_pl.at[p, 0, k], S.r_pl.at[p, 0, k], (row, t)))
        return out

    def to_y(p):
        chunk = S.half[p, at(col, cc), :]
        for k in range(1, nc):
            chunk = chunk + S.rx_pl[p, k].astype(F32)
        S.ys[p, ypos] = chunk
        slot = S.ys.at[p, ypos]
        return [send(slot, slot, S.s_y.at[p, m], S.r_y.at[p, m], there(2 * m, 0)) for m in range(1, ny)]

    def back_to_row(p):
        chunk = S.ys[p, 0]
        for m in range(1, ny):
            chunk = chunk + S.ys[p, m]
        place = pl.ds(pl.multiple_of(core * HALF + col * cc, cc), cc)
        S.gw[p, place, :] = (chunk * (1.0 / math.sqrt(nr * H * nc * W))).astype(BF16)
        slot = S.gw.at[p, place]
        return [send(slot, slot, S.s_pl.at[p, 1, k], S.r_pl.at[p, 1, k], there(0, k)) for k in range(1, nc)]

    def back_to_core(p):
        slot = S.gw.at[p, mine]
        return [send(slot, slot, S.s_core.at[p, 1], S.r_core.at[p, 1], mate)]

    def arrived(copies):
        for c in copies:
            c.wait_recv()

    begin()
    lax.fori_loop(0, NB // 2, functools.partial(attention, 0), 0)
    weights(0)
    core0 = to_core(0)

    begin()
    lax.fori_loop(0, NB // 4, functools.partial(attention, 1), 0)
    arrived(core0)
    row0 = to_row(0)
    lax.fori_loop(NB // 4, NB // 2, functools.partial(attention, 1), 0)
    weights(1)
    core1 = to_core(1)

    def cells_kv(g):
        x = sum(dot(S.wtp[p], S.gkv[p, :, span(g, GC)]) for p in range(2)).T
        for er in range(UNUSED):
            S.gn[er, span(g, B), :] = x[span(er, B)]

    for g in range(4):
        cells_kv(g)
    arrived(core1)
    row1 = to_row(1)
    for g in range(4, NG):
        cells_kv(g)

    low, high = 8, 8 + W
    rows_at = {-1: slice(ABOVE, BELOW), 1: slice(BELOW, UNUSED)}
    cols_at = {-1: slice(0, 8), 1: slice(high, high + 8)}
    back = []
    for i, (dr, dc) in enumerate(DIRS):
        if dc == 0:
            S.tx_row[i] = S.gn[rows_at[dr], low:high, :].reshape(RADIUS * W, D).astype(BF16)
            src, dst = S.tx_row.at[i], S.ry_row.at[i]
        elif dr == 0:
            S.tx_col[i - 2] = S.gn[0:H, cols_at[dc], :].reshape(H * 8, D).astype(BF16)
            src, dst = S.tx_col.at[i - 2], S.ry_col.at[i - 2]
        else:
            cor = S.gn[rows_at[dr], cols_at[dc], :].reshape(RADIUS * 8, D)
            S.tx_cor[i - 4] = jnp.concatenate([cor, jnp.zeros((8, D), F32)], axis=0).astype(BF16)
            src, dst = S.tx_cor.at[i - 4], S.ry_cor.at[i - 4]
        back.append(send(src, dst, S.s_ret.at[i], S.r_ret.at[i], there(dr, dc)))
    arrived(row0)
    y0 = to_y(0)

    for j in range(NB):
        g = jnp.concatenate([S.gqb[p, :, span(j, QC)] for p in range(2)], axis=0)
        x = dot(S.wtq[...], g).T
        for r in range(H):
            S.gn[r, j * B + 8 : j * B + 8 + B, :] += x[span(r, B)]
    arrived(row1)
    y1 = to_y(1)

    arrived(y0)
    gather0 = back_to_row(0)
    arrived(back)
    last = H - RADIUS
    S.gn[last:H, low:high, :] += S.ry_row[0].astype(F32).reshape(RADIUS, W, D)
    S.gn[0:RADIUS, low:high, :] += S.ry_row[1].astype(F32).reshape(RADIUS, W, D)
    S.gn[0:H, high - 8 : high, :] += S.ry_col[0].astype(F32).reshape(H, 8, D)
    S.gn[0:H, low : low + 8, :] += S.ry_col[1].astype(F32).reshape(H, 8, D)
    for i, (dr, dc) in enumerate(DIRS[4:]):
        a = last if dr == -1 else 0
        b = high - 8 if dc == -1 else low
        cor = S.ry_cor[i].astype(F32)[: RADIUS * 8]
        S.gn[a : a + RADIUS, b : b + 8, :] += cor.reshape(RADIUS, 8, D)
    arrived(y1)
    gather1 = back_to_row(1)

    for r in range(H):
        g = (S.gn[r, low:high, :] * gain).T
        x = S.l32[pl.ds(r, D, stride=H), :]
        inv = S.inv[r : r + 1, :]
        inner = jnp.mean(g * x, axis=0, keepdims=True)
        S.l32[pl.ds(r, D, stride=H), :] = inv * (g - x * (inv * inv * inner))

    def store(i, carry):
        S.gl[pl.ds(i * step, step)] = S.l32[at(i, step * H), :].reshape(step, H, W).astype(BF16)
        return carry

    lax.fori_loop(0, D // step, store, 0)

    arrived(gather0)
    done0 = back_to_core(0)
    arrived(gather1)
    done1 = back_to_core(1)
    arrived(done0)
    arrived(done1)
    for c in sent:
        c.wait_send()


def finish(gl, gw, out, gwqkv, gwo):
    out[...] = gl[...]
    for p in range(2):
        for i in range(3):
            gwqkv[i * D + p * PW : i * D + (p + 1) * PW, :] = gw[p, span(i, PW), :].astype(F32)
        gwo[:, span(p, PW)] = gw[p, 3 * PW :, :].astype(F32).T


def solution(mesh):
    nr, nc = mesh.shape["row"], mesh.shape["col"]
    scratch = scratch_shapes(nr, nc)
    names = ["h_lat", "h_gain", "h_wqkv", "h_wo", "h_cos", "h_go", "gl", "gw", *scratch]
    hbm = pl.BlockSpec(memory_space=pltpu.HBM)
    vmem = pl.BlockSpec(memory_space=pltpu.VMEM)

    def per_device(latent, norm_gain, qkv_weight, out_weight, cos_scale, grad_output):
        gl, gw = pl.pallas_call(
            functools.partial(kernel, nr, nc, names),
            out_shape=(pltpu.VMEM((D, H, W), BF16), pltpu.VMEM((2, WP, D), BF16)),
            in_specs=[hbm] * 6,
            out_specs=(vmem, vmem),
            scratch_shapes=list(scratch.values()),
            compiler_params=pltpu.CompilerParams(
                collective_id=0, has_side_effects=True, vmem_limit_bytes=44 * 2**20
            ),
        )(
            *(
                pltpu.with_memory_space_constraint(x, pltpu.HBM)
                for x in (latent, norm_gain.reshape(1, D), qkv_weight, out_weight, cos_scale, grad_output)
            )
        )
        return pl.pallas_call(
            finish,
            out_shape=(
                jax.ShapeDtypeStruct((D, H, W), BF16),
                jax.ShapeDtypeStruct((3 * D, D), F32),
                jax.ShapeDtypeStruct((D, D), F32),
            ),
            in_specs=[vmem, vmem],
            out_specs=(vmem, vmem, vmem),
                        compiler_params=pltpu.CompilerParams(vmem_limit_bytes=16 * 2**20),
        )(*(pltpu.with_memory_space_constraint(x, pltpu.VMEM) for x in (gl, gw)))

    return jax.shard_map(
        per_device,
        mesh=mesh,
        in_specs=(P(None, "row", "col"), P(), P(), P(), P(), P(None, "row", "col")),
        out_specs=(P(None, "row", "col"), P(), P()),
        check_vma=False,
    )
```

```python
import collections
import functools
import math

import jax
import jax.numpy as jnp
from jax import lax
from jax.experimental import pallas as pl
from jax.experimental.pallas import tpu as pltpu
from jax.sharding import PartitionSpec as P

MESH = pl.DeviceIdType.MESH
F32 = jnp.float32
BF16 = jnp.bfloat16

D = 256
HEADS = 4
HW = 64
PW = 2 * HW
RADIUS = 3
EPS = 1e-06
H = 8
W = 128
B = 16
NB = W // B
QC = H * B
NG = NB + 1
ER = 16
ABOVE, BELOW, UNUSED = H, H + RADIUS, H + 2 * RADIUS
GC = ER * B
CHUNK = 64
WP = 4 * PW
HALF = WP // 2

DIRS = ((-1, 0), (1, 0), (0, -1), (0, 1), (-1, -1), (-1, 1), (1, -1), (1, 1))


def dot(a, b):
    return lax.dot_general(a, b, (((1,), (0,)), ((), ())), preferred_element_type=F32)


def dot_nt(a, b):
    return lax.dot_general(a, b, (((1,), (1,)), ((), ())), preferred_element_type=F32)


def heads(x):
    return x.reshape(x.shape[0] // HW, HW, x.shape[-1])


def flat(x):
    return x.reshape(x.shape[0] * HW, x.shape[-1])


def span(i, size):
    return slice(i * size, (i + 1) * size)


def at(i, size):
    return pl.ds(pl.multiple_of(i * size, size), size)


def norm_back(raw, inv, grad):
    inner = jnp.mean(grad * raw, axis=1, keepdims=True)
    return inv * (grad - raw * (inv * inv * inner))


def scratch_shapes(nr, nc):
    cc = HALF // nc
    ny = nr // 2
    dma = pltpu.SemaphoreType.DMA
    return collections.OrderedDict(
        lat=pltpu.VMEM((D, H, W), BF16),
        go=pltpu.VMEM((D, H, W), BF16),
        gain=pltpu.VMEM((1, D), F32),
        wqkv=pltpu.VMEM((3 * D, D), BF16),
        wo=pltpu.VMEM((D, D), BF16),
        l32=pltpu.VMEM((D * H, W), F32),
        g32=pltpu.VMEM((D * H, W), F32),
        inv=pltpu.VMEM((H, W), F32),
        xr=pltpu.VMEM((H * W, D), BF16),
        xe32=pltpu.VMEM((2, H * 8, D), F32),
        xe=pltpu.VMEM((2, H * 8, D), BF16),
        rx_row=pltpu.VMEM((2, RADIUS * W, D), BF16),
        rx_col=pltpu.VMEM((2, H * 8, D), BF16),
        rx_cor=pltpu.VMEM((4, 32, D), BF16),
        xg=pltpu.VMEM((NG * GC, D), BF16),
        xb=pltpu.VMEM((NB * QC, D), BF16),
        gob=pltpu.VMEM((NB * QC, D), BF16),
        wot=pltpu.VMEM((D, D), BF16),
        wtq=pltpu.VMEM((D, D), BF16),
        wtp=pltpu.VMEM((2, D, 2 * PW), BF16),
        kraw=pltpu.VMEM((NG, D, GC), F32),
        kinv=pltpu.VMEM((NG, HEADS, 1, GC), F32),
        kc=pltpu.VMEM((NG, GC, D), BF16),
        vc=pltpu.VMEM((NG, GC, D), BF16),
        kt=pltpu.VMEM((NG, D, GC), BF16),
        vt=pltpu.VMEM((NG, D, GC), BF16),
        qraw=pltpu.VMEM((NB, D, QC), F32),
        qinv=pltpu.VMEM((NB, HEADS, 1, QC), F32),
        qm=pltpu.VMEM((NB, 2, PW, 2 * QC), BF16),
        gm=pltpu.VMEM((NB, 2, PW, 2 * QC), BF16),
        mask=pltpu.VMEM((3, 2 * GC, QC), F32),
        eb=pltpu.VMEM((2, 2 * GC, 2 * QC), BF16),
        sb=pltpu.VMEM((2, 2 * GC, 2 * QC), BF16),
        gk=pltpu.VMEM((PW, GC), F32),
        gv=pltpu.VMEM((PW, GC), F32),
        att=pltpu.VMEM((2, PW, NB * QC), BF16),
        gqb=pltpu.VMEM((2, PW, NB * QC), BF16),
        gkv=pltpu.VMEM((2, 2 * PW, NG * GC), BF16),
        gn=pltpu.VMEM((UNUSED, NG * B, D), F32),
        tx_row=pltpu.VMEM((2, RADIUS * W, D), BF16),
        tx_col=pltpu.VMEM((2, H * 8, D), BF16),
        tx_cor=pltpu.VMEM((4, 32, D), BF16),
        ry_row=pltpu.VMEM((2, RADIUS * W, D), BF16),
        ry_col=pltpu.VMEM((2, H * 8, D), BF16),
        ry_cor=pltpu.VMEM((4, 32, D), BF16),
        wg=pltpu.VMEM((2, WP, D), F32),
        wb=pltpu.VMEM((2, WP, D), BF16),
        rx_half=pltpu.VMEM((2, HALF, D), BF16),
        half=pltpu.VMEM((2, HALF, D), F32),
        hb=pltpu.VMEM((2, HALF, D), BF16),
        rx_pl=pltpu.VMEM((2, nc, cc, D), BF16),
        ys=pltpu.VMEM((2, ny, cc, D), F32),
        cos=pltpu.SMEM((HEADS,), F32),
        s_in=dma((6,)),
        s_hal=dma((8,)),
        r_hal=dma((8,)),
        s_ret=dma((8,)),
        r_ret=dma((8,)),
        s_core=dma((2, 2)),
        r_core=dma((2, 2)),
        s_pl=dma((2, 2)),
        r_pl=dma((2, 2)),
        s_y=dma((2, ny)),
        r_y=dma((2, ny)),
    )


def kernel(nr, nc, names, *refs):
    S = collections.namedtuple("S", names)(*refs)
    row, col = lax.axis_index("row"), lax.axis_index("col")
    core, ypos = lax.rem(row, 2), lax.div(row, 2)
    ny = nr // 2
    cc = HALF // nc

    def there(dr, dc):
        return (lax.rem(row + (dr % nr), nr), lax.rem(col + (dc % nc), nc))

    mate = (row + 1 - 2 * core, col)
    sent = []

    def remote(src, dst, send, recv, device):
        return pltpu.make_async_remote_copy(
            src_ref=src, dst_ref=dst, send_sem=send, recv_sem=recv, device_id=device, device_id_type=MESH
        )

    def send(*args):
        copy = remote(*args)
        copy.start()
        sent.append(copy)
        return copy

    def departed():
        for c in sent:
            c.wait_send()
        sent.clear()

    partners = list(DIRS)
    partners += [(0, k) for k in range(2, nc - 1)]
    partners += [(2 * m, 0) for m in range(1, ny)]
    barrier = pltpu.get_barrier_semaphore()
    for dr, dc in partners:
        pl.semaphore_signal(barrier, inc=1, device_id=there(dr, dc), device_id_type=MESH)
    loads = []
    for i, (src, dst) in enumerate(
        ((S.h_lat, S.lat), (S.h_gain, S.gain), (S.h_go, S.go), (S.h_wqkv, S.wqkv), (S.h_wo, S.wo), (S.h_cos, S.cos))
    ):
        loads.append(pltpu.make_async_copy(src, dst, S.s_in.at[i]))
        loads[-1].start()

    step = 32

    def load(i, acc):
        x = S.lat[pl.ds(i * step, step)].astype(F32)
        S.l32[at(i, step * H), :] = x.reshape(step * H, W)
        return acc + jnp.sum(x * x, axis=0)

    loads[0].wait()
    total = lax.fori_loop(0, D // step, load, jnp.zeros((H, W), F32))
    S.inv[...] = lax.rsqrt(total * (1.0 / D) + EPS)
    loads[1].wait()
    gain = S.gain[...]

    for r in range(H):
        x = S.l32[pl.ds(r, D, stride=H), :] * S.inv[r : r + 1, :]
        xn = x.T * gain
        xnb = xn.astype(BF16)
        S.xr[span(r, W), :] = xnb
        S.xe32[0, span(r, 8), :] = xn[:8]
        S.xe32[1, span(r, 8), :] = xn[W - 8 :]
        for j in range(NB):
            S.xb[span(j * H + r, B), :] = xnb[span(j, B)]
        for g in range(1, NB):
            S.xg[span(g * ER + r, B), :] = xn[g * B - 8 : g * B + 8].astype(BF16)
    S.xe[...] = S.xe32[...].astype(BF16)

    pl.semaphore_wait(barrier, len(partners))
    near = RADIUS * W
    edge = {-1: slice(0, near), 1: slice(H * W - near, H * W)}
    part = {-1: slice(0, 32), 1: slice(32, 64)}
    halo = []
    for i, (dr, dc) in enumerate(DIRS):
        if dc == 0:
            src, dst = S.xr.at[edge[dr]], S.rx_row.at[i]
        elif dr == 0:
            src, dst = S.xe.at[(dc + 1) // 2], S.rx_col.at[i - 2]
        else:
            src, dst = S.xe.at[(dc + 1) // 2, part[dr]], S.rx_cor.at[i - 4]
        halo.append(send(src, dst, S.s_hal.at[i], S.r_hal.at[i], there(dr, dc)))

    for c in loads[2:]:
        c.wait()
    S.wot[...] = S.wo[...].T
    S.wtq[...] = S.wqkv[0:D, :].T
    for p in range(2):
        for i in range(2):
            a = (1 + i) * D + p * PW
            S.wtp[p, :, span(i, PW)] = S.wqkv[a : a + PW, :].T

    def widen(i, carry):
        x = S.go[pl.ds(i * step, step)].astype(F32)
        S.g32[at(i, step * H), :] = x.reshape(step * H, W)
        return carry

    lax.fori_loop(0, D // step, widen, 0)
    for r in range(H):
        g = S.g32[pl.ds(r, D, stride=H), :].T.astype(BF16)
        for j in range(NB):
            S.gob[span(j * H + r, B), :] = g[span(j, B)]

    mshape = (2, ER, B, QC)
    half_, kr, kc = (lax.broadcasted_iota(jnp.int32, mshape, a) for a in range(3))
    lane = lax.broadcasted_iota(jnp.int32, mshape, 3)
    qr, qc = lax.div(lane, B), lax.rem(lane, B)
    krow = jnp.where(kr < ABOVE, kr, jnp.where(kr < BELOW, kr - ABOVE - RADIUS, kr - BELOW + H))
    dr = krow - qr
    off = B * half_ + kc - 8
    dc = off - qc
    grow = row * H + krow
    ok = (dr >= -RADIUS) & (dr <= RADIUS) & (dc >= -RADIUS) & (dc <= RADIUS)
    ok = ok & (grow >= 0) & (grow < nr * H) & (kr < UNUSED)
    one = jnp.where(ok, 1.0, 0.0).astype(F32).reshape(2 * GC, QC)
    off = off.reshape(2 * GC, QC)
    S.mask[0] = jnp.where(col * W + off >= 0, one, 0.0)
    S.mask[1] = one
    S.mask[2] = jnp.where(col * W + W - B + off < nc * W, one, 0.0)

    zero = jnp.zeros((HW, QC), BF16)
    for j in range(NB):
        q = heads(dot_nt(S.wqkv[0:D, :], S.xb[span(j, QC), :]))
        inv = lax.rsqrt(jnp.mean(q * q, axis=1, keepdims=True) + EPS)
        qn = (q * inv).astype(BF16)
        S.qraw[j] = flat(q)
        S.qinv[j] = inv
        ga = heads(dot_nt(S.wot[...], S.gob[span(j, QC), :])).astype(BF16)
        for p in range(2):
            for x, out in ((qn, S.qm), (ga, S.gm)):
                out[j, p, 0:HW, :] = jnp.concatenate([x[2 * p], zero], axis=1)
                out[j, p, HW:PW, :] = jnp.concatenate([zero, x[2 * p + 1]], axis=1)

    def pairs(*units):
        x = jnp.concatenate([S.xg[span(2 * g + s, GC // 2), :] for g, s in units], axis=0)
        kv = dot_nt(S.wqkv[D : 3 * D, :], x)
        k = heads(kv[:D])
        inv = lax.rsqrt(jnp.mean(k * k, axis=1, keepdims=True) + EPS)
        kn = flat(k * inv).astype(BF16)
        v = kv[D:].astype(BF16)
        knt, vnt = kn.T, v.T
        for n, (g, s) in enumerate(units):
            here, lanes = span(s, GC // 2), span(n, GC // 2)
            S.kraw[g, :, here] = kv[:D, lanes]
            S.kinv[g, :, :, here] = inv[:, :, lanes]
            S.kt[g, :, here] = kn[:, lanes]
            S.vt[g, :, here] = v[:, lanes]
            S.kc[g, here, :] = knt[lanes]
            S.vc[g, here, :] = vnt[lanes]

    for g in range(1, NB - 1, 2):
        pairs((g, 0), (g + 1, 0))

    for c in halo:
        c.wait_recv()
    left = S.rx_col[1].astype(F32)
    right = S.rx_col[0].astype(F32)

    def ends(er, first, last, l8, r8):
        S.xg[span(er, B), :] = jnp.concatenate([l8, first], axis=0).astype(BF16)
        S.xg[span(NB * ER + er, B), :] = jnp.concatenate([last, r8], axis=0).astype(BF16)

    for r in range(H):
        ends(r, S.xe32[0, span(r, 8), :], S.xe32[1, span(r, 8), :], left[span(r, 8)], right[span(r, 8)])
    for down in (0, 1):
        l_cor = S.rx_cor[2 * down + 1].astype(F32)
        r_cor = S.rx_cor[2 * down].astype(F32)
        for i in range(RADIUS):
            er = (ABOVE if down else BELOW) + i
            n = i + 1 if down else i
            line = S.rx_row[down, span(i, W), :].astype(F32)
            for g in range(1, NB):
                S.xg[span(g * ER + er, B), :] = line[g * B - 8 : g * B + 8].astype(BF16)
            ends(er, line[:8], line[-8:], l_cor[span(n, 8)], r_cor[span(n, 8)])
    for g in range(NG):
        S.xg[g * GC + UNUSED * B : (g + 1) * GC, :] = jnp.zeros((2 * B, D), BF16)
    units = [(NB - 1, 0), (0, 0), (NB, 0)] + [(g, 1) for g in range(NG)]
    for n in range(0, len(units), 2):
        pairs(*units[n : n + 2])

    factor = [S.cos[h] * (1.0 / HW) for h in range(HEADS)]

    def by_lane(values):
        return jnp.concatenate([jnp.full((1, QC), x, F32) for x in values], axis=1)

    def key_done(p, g, gk, gv):
        o = span(p, PW)
        gk = jnp.concatenate([gk[span(i, HW)] * factor[2 * p + i] for i in range(2)], axis=0)
        gk = norm_back(heads(S.kraw[g, o, :]), S.kinv[g, 2 * p : 2 * p + 2], heads(gk))
        S.gkv[p, 0:PW, at(g, GC)] = flat(gk).astype(BF16)
        S.gkv[p, PW : 2 * PW, at(g, GC)] = gv.astype(BF16)

    def attention(p, n, carry):
        o = span(p, PW)
        far = by_lane(factor[2 * p : 2 * p + 2])
        lgr = far * math.log2(math.e)
        first = []
        for t in range(2):
            j = 2 * n + t
            keys = jnp.concatenate([S.kc[j, :, o], S.kc[j + 1, :, o]], axis=0)
            vals = jnp.concatenate([S.vc[j, :, o], S.vc[j + 1, :, o]], axis=0)
            first.append((dot(keys, S.qm[j, p]), dot(vals, S.gm[j, p])))
        for t in range(2):
            j = 2 * n + t
            which = jnp.where(j == 0, 0, jnp.where(j == NB - 1, 2, 1))
            score, prod = first[t]
            tot = jnp.zeros((8, 2 * QC), F32)
            ed = jnp.zeros((8, 2 * QC), F32)
            for c in range(0, 2 * GC, CHUNK):
                mk = S.mask[which, c : c + CHUNK, :]
                e = jnp.exp2(score[c : c + CHUNK] * lgr) * jnp.concatenate([mk, mk], axis=1)
                tot = tot + jnp.sum(e.reshape(CHUNK // 8, 8, 2 * QC), axis=0)
                ed = ed + jnp.sum((e * prod[c : c + CHUNK]).reshape(CHUNK // 8, 8, 2 * QC), axis=0)
                S.eb[t, c : c + CHUNK, :] = e.astype(BF16)
            rt = 1.0 / jnp.sum(tot, axis=0, keepdims=True)
            mean = jnp.sum(ed, axis=0, keepdims=True) * rt
            for c in range(0, 2 * GC, CHUNK):
                e = S.eb[t, c : c + CHUNK, :].astype(F32)
                S.sb[t, c : c + CHUNK, :] = (e * (prod[c : c + CHUNK] - mean)).astype(BF16)
            prob = S.eb[t]
            slope = S.sb[t]
            keys_t = jnp.concatenate([S.kt[j, o, :], S.kt[j + 1, o, :]], axis=1)
            vals_t = jnp.concatenate([S.vt[j, o, :], S.vt[j + 1, o, :]], axis=1)
            attn = dot(vals_t, prob) * rt
            grad_q = dot(keys_t, slope) * (rt * far)
            for i in range(2):
                c, lanes = span(i, HW), span(i, QC)
                S.att[p, c, at(j, QC)] = attn[c, lanes].astype(BF16)
                raw = S.qraw[j, span(2 * p + i, HW), :]
                g = norm_back(heads(raw), S.qinv[j, 2 * p + i : 2 * p + i + 1], heads(grad_q[c, lanes]))
                S.gqb[p, c, at(j, QC)] = flat(g).astype(BF16)
            qs = (S.qm[j, p].astype(F32) * rt).astype(BF16)
            gs = (S.gm[j, p].astype(F32) * rt).astype(BF16)
            grad_k = dot_nt(qs, slope)
            grad_v = dot_nt(gs, prob)
            key_done(p, j, S.gk[...] + grad_k[:, :GC], S.gv[...] + grad_v[:, :GC])
            S.gk[...] = grad_k[:, GC:]
            S.gv[...] = grad_v[:, GC:]
        return carry

    def begin():
        S.gk[...] = jnp.zeros((PW, GC), F32)
        S.gv[...] = jnp.zeros((PW, GC), F32)

    def weights(p):
        key_done(p, NB, S.gk[...], S.gv[...])
        S.wg[p, 0:PW, :] = dot(S.gqb[p], S.xb[...])
        S.wg[p, PW : 3 * PW, :] = dot(S.gkv[p], S.xg[...])
        S.wg[p, 3 * PW :, :] = dot(S.att[p], S.gob[...])
        S.wb[p] = S.wg[p].astype(BF16)

    mine = at(core, HALF)

    def to_core(p):
        return [send(S.wb.at[p, at(1 - core, HALF)], S.rx_half.at[p], S.s_core.at[p, 0], S.r_core.at[p, 0], mate)]

    def to_row(p):
        half = S.wg[p, mine, :] + S.rx_half[p].astype(F32)
        S.half[p] = half
        S.hb[p] = half.astype(BF16)
        for k in range(1, nc):
            t = lax.rem(col + k, nc)
            remote(S.hb.at[p, at(t, cc)], S.rx_pl.at[p, k], S.s_pl.at[p, 0], S.r_pl.at[p, 0], (row, t)).start()

    def whole_row(p, semaphore):
        rows = S.rx_pl.at[p, 1:nc]
        pltpu.make_async_copy(rows, rows, semaphore).wait()

    def to_y(p):
        chunk = S.half[p, at(col, cc), :]
        for k in range(1, nc):
            chunk = chunk + S.rx_pl[p, k].astype(F32)
        S.ys[p, ypos] = chunk
        slot = S.ys.at[p, ypos]
        return [send(slot, slot, S.s_y.at[p, m], S.r_y.at[p, m], there(2 * m, 0)) for m in range(1, ny)]

    def back_to_row(p):
        chunk = S.ys[p, 0]
        for m in range(1, ny):
            chunk = chunk + S.ys[p, m]
        place = pl.ds(pl.multiple_of(core * HALF + col * cc, cc), cc)
        S.gw[p, place, :] = (chunk * (1.0 / math.sqrt(nr * H * nc * W))).astype(BF16)
        slot = S.gw.at[p, place]
        for k in range(1, nc):
            remote(slot, slot, S.s_pl.at[p, 1], S.r_pl.at[p, 1], there(0, k)).start()

    def back_to_core(p):
        slot = S.gw.at[p, mine]
        return [send(slot, slot, S.s_core.at[p, 1], S.r_core.at[p, 1], mate)]

    def arrived(copies):
        for c in copies:
            c.wait_recv()

    begin()
    lax.fori_loop(0, NB // 2, functools.partial(attention, 0), 0)
    weights(0)
    core0 = to_core(0)

    begin()
    lax.fori_loop(0, NB // 4, functools.partial(attention, 1), 0)
    arrived(core0)
    to_row(0)
    lax.fori_loop(NB // 4, NB // 2, functools.partial(attention, 1), 0)
    weights(1)
    core1 = to_core(1)

    def cells_kv(g):
        x = sum(dot(S.wtp[p], S.gkv[p, :, span(g, GC)]) for p in range(2)).T
        for er in range(UNUSED):
            S.gn[er, span(g, B), :] = x[span(er, B)]

    for g in range(4):
        cells_kv(g)
    arrived(core1)
    to_row(1)
    for g in range(4, NG):
        cells_kv(g)

    low, high = 8, 8 + W
    rows_at = {-1: slice(ABOVE, BELOW), 1: slice(BELOW, UNUSED)}
    cols_at = {-1: slice(0, 8), 1: slice(high, high + 8)}
    back = []
    for i, (dr, dc) in enumerate(DIRS):
        if dc == 0:
            S.tx_row[i] = S.gn[rows_at[dr], low:high, :].reshape(RADIUS * W, D).astype(BF16)
            src, dst = S.tx_row.at[i], S.ry_row.at[i]
        elif dr == 0:
            S.tx_col[i - 2] = S.gn[0:H, cols_at[dc], :].reshape(H * 8, D).astype(BF16)
            src, dst = S.tx_col.at[i - 2], S.ry_col.at[i - 2]
        else:
            cor = S.gn[rows_at[dr], cols_at[dc], :].reshape(RADIUS * 8, D)
            S.tx_cor[i - 4] = jnp.concatenate([cor, jnp.zeros((8, D), F32)], axis=0).astype(BF16)
            src, dst = S.tx_cor.at[i - 4], S.ry_cor.at[i - 4]
        back.append(send(src, dst, S.s_ret.at[i], S.r_ret.at[i], there(dr, dc)))
    whole_row(0, S.r_pl.at[0, 0])
    y0 = to_y(0)

    for j in range(NB):
        g = jnp.concatenate([S.gqb[p, :, span(j, QC)] for p in range(2)], axis=0)
        x = dot(S.wtq[...], g).T
        for r in range(H):
            S.gn[r, j * B + 8 : j * B + 8 + B, :] += x[span(r, B)]
    whole_row(1, S.r_pl.at[1, 0])
    y1 = to_y(1)

    arrived(y0)
    back_to_row(0)
    arrived(back)
    last = H - RADIUS
    S.gn[last:H, low:high, :] += S.ry_row[0].astype(F32).reshape(RADIUS, W, D)
    S.gn[0:RADIUS, low:high, :] += S.ry_row[1].astype(F32).reshape(RADIUS, W, D)
    S.gn[0:H, high - 8 : high, :] += S.ry_col[0].astype(F32).reshape(H, 8, D)
    S.gn[0:H, low : low + 8, :] += S.ry_col[1].astype(F32).reshape(H, 8, D)
    for i, (dr, dc) in enumerate(DIRS[4:]):
        a = last if dr == -1 else 0
        b = high - 8 if dc == -1 else low
        cor = S.ry_cor[i].astype(F32)[: RADIUS * 8]
        S.gn[a : a + RADIUS, b : b + 8, :] += cor.reshape(RADIUS, 8, D)
    arrived(y1)
    back_to_row(1)

    for r in range(H):
        g = (S.gn[r, low:high, :] * gain).T
        x = S.l32[pl.ds(r, D, stride=H), :]
        inv = S.inv[r : r + 1, :]
        inner = jnp.mean(g * x, axis=0, keepdims=True)
        S.l32[pl.ds(r, D, stride=H), :] = inv * (g - x * (inv * inv * inner))

    def store(i, carry):
        S.gl[pl.ds(i * step, step)] = S.l32[at(i, step * H), :].reshape(step, H, W).astype(BF16)
        return carry

    lax.fori_loop(0, D // step, store, 0)

    departed()
    whole_row(0, S.s_pl.at[0, 0])
    whole_row(1, S.s_pl.at[1, 0])
    whole_row(0, S.s_pl.at[0, 1])
    whole_row(0, S.r_pl.at[0, 1])
    done0 = back_to_core(0)
    whole_row(1, S.r_pl.at[1, 1])
    done1 = back_to_core(1)
    arrived(done0)
    arrived(done1)
    departed()
    whole_row(1, S.s_pl.at[1, 1])


def finish(gl, gw, out, gwqkv, gwo):
    out[...] = gl[...]
    for p in range(2):
        for i in range(3):
            gwqkv[i * D + p * PW : i * D + (p + 1) * PW, :] = gw[p, span(i, PW), :].astype(F32)
        gwo[:, span(p, PW)] = gw[p, 3 * PW :, :].astype(F32).T


def solution(mesh):
    nr, nc = mesh.shape["row"], mesh.shape["col"]
    scratch = scratch_shapes(nr, nc)
    names = ["h_lat", "h_gain", "h_wqkv", "h_wo", "h_cos", "h_go", "gl", "gw", *scratch]
    hbm = pl.BlockSpec(memory_space=pltpu.HBM)
    vmem = pl.BlockSpec(memory_space=pltpu.VMEM)

    def per_device(latent, norm_gain, qkv_weight, out_weight, cos_scale, grad_output):
        gl, gw = pl.pallas_call(
            functools.partial(kernel, nr, nc, names),
            out_shape=(pltpu.VMEM((D, H, W), BF16), pltpu.VMEM((2, WP, D), BF16)),
            in_specs=[hbm] * 6,
            out_specs=(vmem, vmem),
            scratch_shapes=list(scratch.values()),
            compiler_params=pltpu.CompilerParams(
                collective_id=0, has_side_effects=True, vmem_limit_bytes=44 * 2**20
            ),
        )(
            *(
                pltpu.with_memory_space_constraint(x, pltpu.HBM)
                for x in (latent, norm_gain.reshape(1, D), qkv_weight, out_weight, cos_scale, grad_output)
            )
        )
        return pl.pallas_call(
            finish,
            out_shape=(
                jax.ShapeDtypeStruct((D, H, W), BF16),
                jax.ShapeDtypeStruct((3 * D, D), F32),
                jax.ShapeDtypeStruct((D, D), F32),
            ),
            in_specs=[vmem, vmem],
            out_specs=(vmem, vmem, vmem),
                        compiler_params=pltpu.CompilerParams(vmem_limit_bytes=16 * 2**20),
        )(*(pltpu.with_memory_space_constraint(x, pltpu.VMEM) for x in (gl, gw)))

    return jax.shard_map(
        per_device,
        mesh=mesh,
        in_specs=(P(None, "row", "col"), P(), P(), P(), P(), P(None, "row", "col")),
        out_specs=(P(None, "row", "col"), P(), P()),
        check_vma=False,
    )
```

```python
import collections
import functools
import math

import jax
import jax.numpy as jnp
from jax import lax
from jax.experimental import pallas as pl
from jax.experimental.pallas import tpu as pltpu
from jax.sharding import PartitionSpec as P

MESH = pl.DeviceIdType.MESH
F32 = jnp.float32
BF16 = jnp.bfloat16

D = 256
HEADS = 4
HW = 64
PW = 2 * HW
RADIUS = 3
EPS = 1e-06
H = 8
W = 128
B = 16
NB = W // B
QC = H * B
NG = NB + 1
ER = 16
ABOVE, BELOW, UNUSED = H, H + RADIUS, H + 2 * RADIUS
GC = ER * B
CHUNK = 64
WP = 4 * PW
HALF = WP // 2

DIRS = ((-1, 0), (1, 0), (0, -1), (0, 1), (-1, -1), (-1, 1), (1, -1), (1, 1))


def dot(a, b):
    return lax.dot_general(a, b, (((1,), (0,)), ((), ())), preferred_element_type=F32)


def dot_nt(a, b):
    return lax.dot_general(a, b, (((1,), (1,)), ((), ())), preferred_element_type=F32)


def heads(x):
    return x.reshape(x.shape[0] // HW, HW, x.shape[-1])


def flat(x):
    return x.reshape(x.shape[0] * HW, x.shape[-1])


def span(i, size):
    return slice(i * size, (i + 1) * size)


def at(i, size):
    return slice(i * size, (i + 1) * size) if isinstance(i, int) else pl.ds(pl.multiple_of(i * size, size), size)


def norm_back(raw, inv, grad):
    inner = jnp.mean(grad * raw, axis=1, keepdims=True)
    return inv * (grad - raw * (inv * inv * inner))


def scratch_shapes(nr, nc):
    cc = HALF // nc
    ny = nr // 2
    dma = pltpu.SemaphoreType.DMA
    return collections.OrderedDict(
        lat=pltpu.VMEM((D, H, W), BF16),
        go=pltpu.VMEM((D, H, W), BF16),
        gain=pltpu.VMEM((1, D), F32),
        wqkv=pltpu.VMEM((3 * D, D), BF16),
        wo=pltpu.VMEM((D, D), BF16),
        l32=pltpu.VMEM((D * H, W), F32),
        g32=pltpu.VMEM((D * H, W), F32),
        inv=pltpu.VMEM((H, W), F32),
        xr=pltpu.VMEM((H * W, D), BF16),
        xe32=pltpu.VMEM((2, H * 8, D), F32),
        xe=pltpu.VMEM((2, H * 8, D), BF16),
        rx_row=pltpu.VMEM((2, RADIUS * W, D), BF16),
        rx_col=pltpu.VMEM((2, H * 8, D), BF16),
        rx_cor=pltpu.VMEM((4, 32, D), BF16),
        xg=pltpu.VMEM((NG * GC, D), BF16),
        xb=pltpu.VMEM((NB * QC, D), BF16),
        gob=pltpu.VMEM((NB * QC, D), BF16),
        wot=pltpu.VMEM((D, D), BF16),
        wtq=pltpu.VMEM((D, D), BF16),
        wtp=pltpu.VMEM((2, D, 2 * PW), BF16),
        kraw=pltpu.VMEM((NG, D, GC), F32),
        kinv=pltpu.VMEM((NG, HEADS, 1, GC), F32),
        kc=pltpu.VMEM((NG, GC, D), BF16),
        vc=pltpu.VMEM((NG, GC, D), BF16),
        kt=pltpu.VMEM((NG, D, GC), BF16),
        vt=pltpu.VMEM((NG, D, GC), BF16),
        qraw=pltpu.VMEM((NB, D, QC), F32),
        qinv=pltpu.VMEM((NB, HEADS, 1, QC), F32),
        qm=pltpu.VMEM((NB, 2, PW, 2 * QC), BF16),
        gm=pltpu.VMEM((NB, 2, PW, 2 * QC), BF16),
        mask=pltpu.VMEM((3, 2 * GC, QC), F32),
        eb=pltpu.VMEM((2, 2 * GC, 2 * QC), BF16),
        sb=pltpu.VMEM((2, 2 * GC, 2 * QC), BF16),
        gk=pltpu.VMEM((PW, GC), F32),
        gv=pltpu.VMEM((PW, GC), F32),
        att=pltpu.VMEM((2, PW, NB * QC), BF16),
        gqb=pltpu.VMEM((2, PW, NB * QC), BF16),
        gkv=pltpu.VMEM((2, 2 * PW, NG * GC), BF16),
        gn=pltpu.VMEM((UNUSED, NG * B, D), F32),
        tx_row=pltpu.VMEM((2, RADIUS * W, D), BF16),
        tx_col=pltpu.VMEM((2, H * 8, D), BF16),
        tx_cor=pltpu.VMEM((4, 32, D), BF16),
        ry_row=pltpu.VMEM((2, RADIUS * W, D), BF16),
        ry_col=pltpu.VMEM((2, H * 8, D), BF16),
        ry_cor=pltpu.VMEM((4, 32, D), BF16),
        wg=pltpu.VMEM((2, WP, D), F32),
        wb=pltpu.VMEM((2, WP, D), BF16),
        rx_half=pltpu.VMEM((2, HALF, D), BF16),
        half=pltpu.VMEM((2, HALF, D), F32),
        hb=pltpu.VMEM((2, HALF, D), BF16),
        rx_pl=pltpu.VMEM((2, nc, cc, D), BF16),
        ys=pltpu.VMEM((2, ny, cc, D), F32),
        cos=pltpu.SMEM((HEADS,), F32),
        s_in=dma((6,)),
        s_hal=dma((8,)),
        r_hal=dma((8,)),
        s_ret=dma((8,)),
        r_ret=dma((8,)),
        s_core=dma((2, 2)),
        r_core=dma((2, 2)),
        s_pl=dma((2, 2)),
        r_pl=dma((2, 2)),
        s_y=dma((2, ny)),
        r_y=dma((2, ny)),
    )


def kernel(nr, nc, names, *refs):
    S = collections.namedtuple("S", names)(*refs)
    row, col = lax.axis_index("row"), lax.axis_index("col")
    core, ypos = lax.rem(row, 2), lax.div(row, 2)
    ny = nr // 2
    cc = HALF // nc

    def there(dr, dc):
        return (lax.rem(row + (dr % nr), nr), lax.rem(col + (dc % nc), nc))

    mate = (row + 1 - 2 * core, col)
    sent = []

    def remote(src, dst, send, recv, device):
        return pltpu.make_async_remote_copy(
            src_ref=src, dst_ref=dst, send_sem=send, recv_sem=recv, device_id=device, device_id_type=MESH
        )

    def send(*args):
        copy = remote(*args)
        copy.start()
        sent.append(copy)
        return copy

    def departed():
        for c in sent:
            c.wait_send()
        sent.clear()

    partners = list(DIRS)
    partners += [(0, k) for k in range(2, nc - 1)]
    partners += [(2 * m, 0) for m in range(1, ny)]
    barrier = pltpu.get_barrier_semaphore()
    for dr, dc in partners:
        pl.semaphore_signal(barrier, inc=1, device_id=there(dr, dc), device_id_type=MESH)
    loads = []
    for i, (src, dst) in enumerate(
        ((S.h_lat, S.lat), (S.h_gain, S.gain), (S.h_go, S.go), (S.h_wqkv, S.wqkv), (S.h_wo, S.wo), (S.h_cos, S.cos))
    ):
        loads.append(pltpu.make_async_copy(src, dst, S.s_in.at[i]))
        loads[-1].start()

    step = 32

    def load(i, acc):
        x = S.lat[pl.ds(i * step, step)].astype(F32)
        S.l32[at(i, step * H), :] = x.reshape(step * H, W)
        return acc + jnp.sum(x * x, axis=0)

    loads[0].wait()
    total = lax.fori_loop(0, D // step, load, jnp.zeros((H, W), F32))
    S.inv[...] = lax.rsqrt(total * (1.0 / D) + EPS)
    loads[1].wait()
    gain = S.gain[...]

    for r in range(H):
        x = S.l32[pl.ds(r, D, stride=H), :] * S.inv[r : r + 1, :]
        xn = x.T * gain
        xnb = xn.astype(BF16)
        S.xr[span(r, W), :] = xnb
        S.xe32[0, span(r, 8), :] = xn[:8]
        S.xe32[1, span(r, 8), :] = xn[W - 8 :]
        for j in range(NB):
            S.xb[span(j * H + r, B), :] = xnb[span(j, B)]
        for g in range(1, NB):
            S.xg[span(g * ER + r, B), :] = xn[g * B - 8 : g * B + 8].astype(BF16)
    S.xe[...] = S.xe32[...].astype(BF16)

    pl.semaphore_wait(barrier, len(partners))
    near = RADIUS * W
    edge = {-1: slice(0, near), 1: slice(H * W - near, H * W)}
    part = {-1: slice(0, 32), 1: slice(32, 64)}
    halo = []
    for i, (dr, dc) in reversed([*enumerate(DIRS)]):
        if dc == 0:
            src, dst = S.xr.at[edge[dr]], S.rx_row.at[i]
        elif dr == 0:
            src, dst = S.xe.at[(dc + 1) // 2], S.rx_col.at[i - 2]
        else:
            src, dst = S.xe.at[(dc + 1) // 2, part[dr]], S.rx_cor.at[i - 4]
        halo.append(send(src, dst, S.s_hal.at[i], S.r_hal.at[i], there(dr, dc)))

    for c in loads[2:]:
        c.wait()
    S.wot[...] = S.wo[...].T
    S.wtq[...] = S.wqkv[0:D, :].T
    for p in range(2):
        for i in range(2):
            a = (1 + i) * D + p * PW
            S.wtp[p, :, span(i, PW)] = S.wqkv[a : a + PW, :].T

    def widen(i, carry):
        x = S.go[pl.ds(i * step, step)].astype(F32)
        S.g32[at(i, step * H), :] = x.reshape(step * H, W)
        return carry

    lax.fori_loop(0, D // step, widen, 0)
    for r in range(H):
        g = S.g32[pl.ds(r, D, stride=H), :].T.astype(BF16)
        for j in range(NB):
            S.gob[span(j * H + r, B), :] = g[span(j, B)]

    mshape = (2, ER, B, QC)
    half_, kr, kc = (lax.broadcasted_iota(jnp.int32, mshape, a) for a in range(3))
    lane = lax.broadcasted_iota(jnp.int32, mshape, 3)
    qr, qc = lax.div(lane, B), lax.rem(lane, B)
    krow = jnp.where(kr < ABOVE, kr, jnp.where(kr < BELOW, kr - ABOVE - RADIUS, kr - BELOW + H))
    dr = krow - qr
    off = B * half_ + kc - 8
    dc = off - qc
    grow = row * H + krow
    ok = (dr >= -RADIUS) & (dr <= RADIUS) & (dc >= -RADIUS) & (dc <= RADIUS)
    ok = ok & (grow >= 0) & (grow < nr * H) & (kr < UNUSED)
    one = jnp.where(ok, 1.0, 0.0).astype(F32).reshape(2 * GC, QC)
    off = off.reshape(2 * GC, QC)
    S.mask[0] = jnp.where(col * W + off >= 0, one, 0.0)
    S.mask[1] = one
    S.mask[2] = jnp.where(col * W + W - B + off < nc * W, one, 0.0)

    zero = jnp.zeros((HW, QC), BF16)
    for j in range(NB):
        q = heads(dot_nt(S.wqkv[0:D, :], S.xb[span(j, QC), :]))
        inv = lax.rsqrt(jnp.mean(q * q, axis=1, keepdims=True) + EPS)
        qn = (q * inv).astype(BF16)
        S.qraw[j] = flat(q)
        S.qinv[j] = inv
        ga = heads(dot_nt(S.wot[...], S.gob[span(j, QC), :])).astype(BF16)
        for p in range(2):
            for x, out in ((qn, S.qm), (ga, S.gm)):
                out[j, p, 0:HW, :] = jnp.concatenate([x[2 * p], zero], axis=1)
                out[j, p, HW:PW, :] = jnp.concatenate([zero, x[2 * p + 1]], axis=1)

    def pairs(*units):
        x = jnp.concatenate([S.xg[span(2 * g + s, GC // 2), :] for g, s in units], axis=0)
        kv = dot_nt(S.wqkv[D : 3 * D, :], x)
        k = heads(kv[:D])
        inv = lax.rsqrt(jnp.mean(k * k, axis=1, keepdims=True) + EPS)
        kn = flat(k * inv).astype(BF16)
        v = kv[D:].astype(BF16)
        knt, vnt = kn.T, v.T
        for n, (g, s) in enumerate(units):
            here, lanes = span(s, GC // 2), span(n, GC // 2)
            S.kraw[g, :, here] = kv[:D, lanes]
            S.kinv[g, :, :, here] = inv[:, :, lanes]
            S.kt[g, :, here] = kn[:, lanes]
            S.vt[g, :, here] = v[:, lanes]
            S.kc[g, here, :] = knt[lanes]
            S.vc[g, here, :] = vnt[lanes]

    for g in range(1, NB - 1, 2):
        pairs((g, 0), (g + 1, 0))

    for c in halo:
        c.wait_recv()
    left = S.rx_col[1].astype(F32)
    right = S.rx_col[0].astype(F32)

    def ends(er, first, last, l8, r8):
        S.xg[span(er, B), :] = jnp.concatenate([l8, first], axis=0).astype(BF16)
        S.xg[span(NB * ER + er, B), :] = jnp.concatenate([last, r8], axis=0).astype(BF16)

    for r in range(H):
        ends(r, S.xe32[0, span(r, 8), :], S.xe32[1, span(r, 8), :], left[span(r, 8)], right[span(r, 8)])
    for down in (0, 1):
        l_cor = S.rx_cor[2 * down + 1].astype(F32)
        r_cor = S.rx_cor[2 * down].astype(F32)
        for i in range(RADIUS):
            er = (ABOVE if down else BELOW) + i
            n = i + 1 if down else i
            line = S.rx_row[down, span(i, W), :].astype(F32)
            for g in range(1, NB):
                S.xg[span(g * ER + er, B), :] = line[g * B - 8 : g * B + 8].astype(BF16)
            ends(er, line[:8], line[-8:], l_cor[span(n, 8)], r_cor[span(n, 8)])
    for g in range(NG):
        S.xg[g * GC + UNUSED * B : (g + 1) * GC, :] = jnp.zeros((2 * B, D), BF16)
    units = [(NB - 1, 0), (0, 0), (NB, 0)] + [(g, 1) for g in range(NG)]
    for n in range(0, len(units), 2):
        pairs(*units[n : n + 2])

    factor = [S.cos[h] * (1.0 / HW) for h in range(HEADS)]

    def by_lane(values):
        return jnp.concatenate([jnp.full((1, QC), x, F32) for x in values], axis=1)

    def key_done(p, g, gk, gv):
        o = span(p, PW)
        gk = jnp.concatenate([gk[span(i, HW)] * factor[2 * p + i] for i in range(2)], axis=0)
        gk = norm_back(heads(S.kraw[g, o, :]), S.kinv[g, 2 * p : 2 * p + 2], heads(gk))
        S.gkv[p, 0:PW, at(g, GC)] = flat(gk).astype(BF16)
        S.gkv[p, PW : 2 * PW, at(g, GC)] = gv.astype(BF16)

    def attention(p, n, carry):
        o = span(p, PW)
        far = by_lane(factor[2 * p : 2 * p + 2])
        lgr = far * math.log2(math.e)
        first = []
        for t in range(2):
            j = 2 * n + t
            keys = jnp.concatenate([S.kc[j, :, o], S.kc[j + 1, :, o]], axis=0)
            vals = jnp.concatenate([S.vc[j, :, o], S.vc[j + 1, :, o]], axis=0)
            first.append((dot(keys, S.qm[j, p]), dot(vals, S.gm[j, p])))
        for t in range(2):
            j = 2 * n + t
            which = 0 if j == 0 else 2 if j == NB - 1 else 1
            score, prod = first[t]
            tot = jnp.zeros((8, 2 * QC), F32)
            ed = jnp.zeros((8, 2 * QC), F32)
            for c in range(0, 2 * GC, CHUNK):
                mk = S.mask[which, c : c + CHUNK, :]
                e = jnp.exp2(score[c : c + CHUNK] * lgr) * jnp.concatenate([mk, mk], axis=1)
                tot = tot + jnp.sum(e.reshape(CHUNK // 8, 8, 2 * QC), axis=0)
                ed = ed + jnp.sum((e * prod[c : c + CHUNK]).reshape(CHUNK // 8, 8, 2 * QC), axis=0)
                S.eb[t, c : c + CHUNK, :] = e.astype(BF16)
            rt = 1.0 / jnp.sum(tot, axis=0, keepdims=True)
            mean = jnp.sum(ed, axis=0, keepdims=True) * rt
            for c in range(0, 2 * GC, CHUNK):
                e = S.eb[t, c : c + CHUNK, :].astype(F32)
                S.sb[t, c : c + CHUNK, :] = (e * (prod[c : c + CHUNK] - mean)).astype(BF16)
            prob = S.eb[t]
            slope = S.sb[t]
            keys_t = jnp.concatenate([S.kt[j, o, :], S.kt[j + 1, o, :]], axis=1)
            vals_t = jnp.concatenate([S.vt[j, o, :], S.vt[j + 1, o, :]], axis=1)
            attn = dot(vals_t, prob) * rt
            grad_q = dot(keys_t, slope) * (rt * far)
            for i in range(2):
                c, lanes = span(i, HW), span(i, QC)
                S.att[p, c, at(j, QC)] = attn[c, lanes].astype(BF16)
                raw = S.qraw[j, span(2 * p + i, HW), :]
                g = norm_back(heads(raw), S.qinv[j, 2 * p + i : 2 * p + i + 1], heads(grad_q[c, lanes]))
                S.gqb[p, c, at(j, QC)] = flat(g).astype(BF16)
            qs = (S.qm[j, p].astype(F32) * rt).astype(BF16)
            gs = (S.gm[j, p].astype(F32) * rt).astype(BF16)
            grad_k = dot_nt(qs, slope)
            grad_v = dot_nt(gs, prob)
            key_done(p, j, S.gk[...] + grad_k[:, :GC], S.gv[...] + grad_v[:, :GC])
            S.gk[...] = grad_k[:, GC:]
            S.gv[...] = grad_v[:, GC:]
        return carry

    def begin():
        S.gk[...] = jnp.zeros((PW, GC), F32)
        S.gv[...] = jnp.zeros((PW, GC), F32)

    def weights(p):
        key_done(p, NB, S.gk[...], S.gv[...])
        S.wg[p, 0:PW, :] = dot(S.gqb[p], S.xb[...])
        S.wg[p, PW : 3 * PW, :] = dot(S.gkv[p], S.xg[...])
        S.wg[p, 3 * PW :, :] = dot(S.att[p], S.gob[...])
        S.wb[p] = S.wg[p].astype(BF16)

    mine = at(core, HALF)

    def to_core(p):
        return [send(S.wb.at[p, at(1 - core, HALF)], S.rx_half.at[p], S.s_core.at[p, 0], S.r_core.at[p, 0], mate)]

    def to_row(p):
        half = S.wg[p, mine, :] + S.rx_half[p].astype(F32)
        S.half[p] = half
        S.hb[p] = half.astype(BF16)
        for k in range(1, nc):
            t = lax.rem(col + k, nc)
            remote(S.hb.at[p, at(t, cc)], S.rx_pl.at[p, k], S.s_pl.at[p, 0], S.r_pl.at[p, 0], (row, t)).start()

    def whole_row(p, semaphore):
        rows = S.rx_pl.at[p, 1:nc]
        pltpu.make_async_copy(rows, rows, semaphore).wait()

    def to_y(p):
        chunk = S.half[p, at(col, cc), :]
        for k in range(1, nc):
            chunk = chunk + S.rx_pl[p, k].astype(F32)
        S.ys[p, ypos] = chunk
        slot = S.ys.at[p, ypos]
        return [send(slot, slot, S.s_y.at[p, m], S.r_y.at[p, m], there(2 * m, 0)) for m in range(1, ny)]

    def back_to_row(p):
        chunk = S.ys[p, 0]
        for m in range(1, ny):
            chunk = chunk + S.ys[p, m]
        place = pl.ds(pl.multiple_of(core * HALF + col * cc, cc), cc)
        S.gw[p, place, :] = (chunk * (1.0 / math.sqrt(nr * H * nc * W))).astype(BF16)
        slot = S.gw.at[p, place]
        for k in range(1, nc):
            remote(slot, slot, S.s_pl.at[p, 1], S.r_pl.at[p, 1], there(0, k)).start()

    def back_to_core(p):
        slot = S.gw.at[p, mine]
        return [send(slot, slot, S.s_core.at[p, 1], S.r_core.at[p, 1], mate)]

    def arrived(copies):
        for c in copies:
            c.wait_recv()

    begin()
    for n in range(NB // 2):
        attention(0, n, 0)
    weights(0)
    core0 = to_core(0)

    begin()
    for n in range(NB // 4):
        attention(1, n, 0)
    arrived(core0)
    to_row(0)
    for n in range(NB // 4, NB // 2):
        attention(1, n, 0)
    weights(1)
    core1 = to_core(1)

    def cells_kv(g):
        x = sum(dot(S.wtp[p], S.gkv[p, :, span(g, GC)]) for p in range(2)).T
        for er in range(UNUSED):
            S.gn[er, span(g, B), :] = x[span(er, B)]

    for g in range(4):
        cells_kv(g)
    arrived(core1)
    to_row(1)
    for g in range(4, NG):
        cells_kv(g)

    low, high = 8, 8 + W
    rows_at = {-1: slice(ABOVE, BELOW), 1: slice(BELOW, UNUSED)}
    cols_at = {-1: slice(0, 8), 1: slice(high, high + 8)}
    back = []
    for i, (dr, dc) in reversed([*enumerate(DIRS)]):
        if dc == 0:
            S.tx_row[i] = S.gn[rows_at[dr], low:high, :].reshape(RADIUS * W, D).astype(BF16)
            src, dst = S.tx_row.at[i], S.ry_row.at[i]
        elif dr == 0:
            S.tx_col[i - 2] = S.gn[0:H, cols_at[dc], :].reshape(H * 8, D).astype(BF16)
            src, dst = S.tx_col.at[i - 2], S.ry_col.at[i - 2]
        else:
            cor = S.gn[rows_at[dr], cols_at[dc], :].reshape(RADIUS * 8, D)
            S.tx_cor[i - 4] = jnp.concatenate([cor, jnp.zeros((8, D), F32)], axis=0).astype(BF16)
            src, dst = S.tx_cor.at[i - 4], S.ry_cor.at[i - 4]
        back.append(send(src, dst, S.s_ret.at[i], S.r_ret.at[i], there(dr, dc)))
    whole_row(0, S.r_pl.at[0, 0])
    y0 = to_y(0)

    for j in range(NB):
        g = jnp.concatenate([S.gqb[p, :, span(j, QC)] for p in range(2)], axis=0)
        x = dot(S.wtq[...], g).T
        for r in range(H):
            S.gn[r, j * B + 8 : j * B + 8 + B, :] += x[span(r, B)]
    whole_row(1, S.r_pl.at[1, 0])
    y1 = to_y(1)

    arrived(y0)
    back_to_row(0)
    arrived(back)
    last = H - RADIUS
    S.gn[last:H, low:high, :] += S.ry_row[0].astype(F32).reshape(RADIUS, W, D)
    S.gn[0:RADIUS, low:high, :] += S.ry_row[1].astype(F32).reshape(RADIUS, W, D)
    S.gn[0:H, high - 8 : high, :] += S.ry_col[0].astype(F32).reshape(H, 8, D)
    S.gn[0:H, low : low + 8, :] += S.ry_col[1].astype(F32).reshape(H, 8, D)
    for i, (dr, dc) in enumerate(DIRS[4:]):
        a = last if dr == -1 else 0
        b = high - 8 if dc == -1 else low
        cor = S.ry_cor[i].astype(F32)[: RADIUS * 8]
        S.gn[a : a + RADIUS, b : b + 8, :] += cor.reshape(RADIUS, 8, D)
    arrived(y1)
    back_to_row(1)

    for r in range(H):
        g = (S.gn[r, low:high, :] * gain).T
        x = S.l32[pl.ds(r, D, stride=H), :]
        inv = S.inv[r : r + 1, :]
        inner = jnp.mean(g * x, axis=0, keepdims=True)
        S.l32[pl.ds(r, D, stride=H), :] = inv * (g - x * (inv * inv * inner))

    def store(i, carry):
        S.gl[pl.ds(i * step, step)] = S.l32[at(i, step * H), :].reshape(step, H, W).astype(BF16)
        return carry

    lax.fori_loop(0, D // step, store, 0)

    departed()
    whole_row(0, S.s_pl.at[0, 0])
    whole_row(1, S.s_pl.at[1, 0])
    whole_row(0, S.s_pl.at[0, 1])
    whole_row(0, S.r_pl.at[0, 1])
    done0 = back_to_core(0)
    whole_row(1, S.r_pl.at[1, 1])
    done1 = back_to_core(1)
    arrived(done0)
    arrived(done1)
    departed()
    whole_row(1, S.s_pl.at[1, 1])


def finish(gl, gw, out, gwqkv, gwo):
    out[...] = gl[...]
    for p in range(2):
        for i in range(3):
            gwqkv[i * D + p * PW : i * D + (p + 1) * PW, :] = gw[p, span(i, PW), :].astype(F32)
        gwo[:, span(p, PW)] = gw[p, 3 * PW :, :].astype(F32).T


def solution(mesh):
    nr, nc = mesh.shape["row"], mesh.shape["col"]
    scratch = scratch_shapes(nr, nc)
    names = ["h_lat", "h_gain", "h_wqkv", "h_wo", "h_cos", "h_go", "gl", "gw", *scratch]
    hbm = pl.BlockSpec(memory_space=pltpu.HBM)
    vmem = pl.BlockSpec(memory_space=pltpu.VMEM)

    def per_device(latent, norm_gain, qkv_weight, out_weight, cos_scale, grad_output):
        gl, gw = pl.pallas_call(
            functools.partial(kernel, nr, nc, names),
            out_shape=(pltpu.VMEM((D, H, W), BF16), pltpu.VMEM((2, WP, D), BF16)),
            in_specs=[hbm] * 6,
            out_specs=(vmem, vmem),
            scratch_shapes=list(scratch.values()),
            compiler_params=pltpu.CompilerParams(
                collective_id=0, has_side_effects=True, vmem_limit_bytes=44 * 2**20
            ),
        )(
            *(
                pltpu.with_memory_space_constraint(x, pltpu.HBM)
                for x in (latent, norm_gain.reshape(1, D), qkv_weight, out_weight, cos_scale, grad_output)
            )
        )
        return pl.pallas_call(
            finish,
            out_shape=(
                jax.ShapeDtypeStruct((D, H, W), BF16),
                jax.ShapeDtypeStruct((3 * D, D), F32),
                jax.ShapeDtypeStruct((D, D), F32),
            ),
            in_specs=[vmem, vmem],
            out_specs=(vmem, vmem, vmem),
                        compiler_params=pltpu.CompilerParams(vmem_limit_bytes=16 * 2**20),
        )(*(pltpu.with_memory_space_constraint(x, pltpu.VMEM) for x in (gl, gw)))

    return jax.shard_map(
        per_device,
        mesh=mesh,
        in_specs=(P(None, "row", "col"), P(), P(), P(), P(), P(None, "row", "col")),
        out_specs=(P(None, "row", "col"), P(), P()),
        check_vma=False,
    )
```

```python
import collections
import functools
import math

import jax
import jax.numpy as jnp
from jax import lax
from jax.experimental import pallas as pl
from jax.experimental.pallas import tpu as pltpu
from jax.sharding import PartitionSpec as P

MESH = pl.DeviceIdType.MESH
F32 = jnp.float32
BF16 = jnp.bfloat16

D = 256
HEADS = 4
HW = 64
PW = 2 * HW
RADIUS = 3
EPS = 1e-06
H = 8
W = 128
B = 16
NB = W // B
QC = H * B
NG = NB + 1
ER = 16
ABOVE, BELOW, UNUSED = H, H + RADIUS, H + 2 * RADIUS
FIRST = 80
GC = ER * B
CHUNK = 64
WP = 4 * PW
HALF = WP // 2

DIRS = ((-1, 0), (1, 0), (0, -1), (0, 1), (-1, -1), (-1, 1), (1, -1), (1, 1))


def dot(a, b):
    return lax.dot_general(a, b, (((1,), (0,)), ((), ())), preferred_element_type=F32)


def dot_nt(a, b):
    return lax.dot_general(a, b, (((1,), (1,)), ((), ())), preferred_element_type=F32)


def heads(x):
    return x.reshape(x.shape[0] // HW, HW, x.shape[-1])


def flat(x):
    return x.reshape(x.shape[0] * HW, x.shape[-1])


def span(i, size):
    return slice(i * size, (i + 1) * size)


def at(i, size):
    return slice(i * size, (i + 1) * size) if isinstance(i, int) else pl.ds(pl.multiple_of(i * size, size), size)


def norm_back(raw, inv, grad):
    inner = jnp.mean(grad * raw, axis=1, keepdims=True)
    return inv * (grad - raw * (inv * inv * inner))


def scratch_shapes(nr, nc):
    cc = HALF // nc
    ny = nr // 2
    dma = pltpu.SemaphoreType.DMA
    return collections.OrderedDict(
        lat=pltpu.VMEM((D, H, W), BF16),
        go=pltpu.VMEM((D, H, W), BF16),
        gain=pltpu.VMEM((1, D), F32),
        wqkv=pltpu.VMEM((3 * D, D), BF16),
        wo=pltpu.VMEM((D, D), BF16),
        l32=pltpu.VMEM((D * H, W), F32),
        g32=pltpu.VMEM((D * H, W), F32),
        inv=pltpu.VMEM((H, W), F32),
        xr=pltpu.VMEM((H, W, D), BF16),
        xe32=pltpu.VMEM((2, H * 8, D), F32),
        xe=pltpu.VMEM((2, H * 8, D), BF16),
        rx_row=pltpu.VMEM((2, RADIUS, W, D), BF16),
        rx_col=pltpu.VMEM((2, H * 8, D), BF16),
        rx_cor=pltpu.VMEM((4, 32, D), BF16),
        xg=pltpu.VMEM((NG * GC, D), BF16),
        xb=pltpu.VMEM((NB * QC, D), BF16),
        gob=pltpu.VMEM((NB * QC, D), BF16),
        wot=pltpu.VMEM((D, D), BF16),
        wtq=pltpu.VMEM((D, D), BF16),
        wtp=pltpu.VMEM((2, D, 2 * PW), BF16),
        kraw=pltpu.VMEM((NG, D, GC), F32),
        kinv=pltpu.VMEM((NG, HEADS, 1, GC), F32),
        kc=pltpu.VMEM((NG, GC, D), BF16),
        vc=pltpu.VMEM((NG, GC, D), BF16),
        kt=pltpu.VMEM((NG, D, GC), BF16),
        vt=pltpu.VMEM((NG, D, GC), BF16),
        qraw=pltpu.VMEM((NB, D, QC), F32),
        qinv=pltpu.VMEM((NB, HEADS, 1, QC), F32),
        qm=pltpu.VMEM((NB, 2, PW, 2 * QC), BF16),
        gm=pltpu.VMEM((NB, 2, PW, 2 * QC), BF16),
        mask=pltpu.VMEM((3, 2 * GC, QC), F32),
        eb=pltpu.VMEM((NB, 2 * GC, 2 * QC), BF16),
        sb=pltpu.VMEM((NB, 2 * GC, 2 * QC), BF16),
        gk=pltpu.VMEM((PW, GC), F32),
        gv=pltpu.VMEM((PW, GC), F32),
        att=pltpu.VMEM((2, PW, NB * QC), BF16),
        gqb=pltpu.VMEM((2, PW, NB * QC), BF16),
        gkv=pltpu.VMEM((2, 2 * PW, NG * GC), BF16),
        gn=pltpu.VMEM((UNUSED, NG * B, D), F32),
        tx_row=pltpu.VMEM((2, RADIUS * W, D), BF16),
        tx_col=pltpu.VMEM((2, H * 8, D), BF16),
        tx_cor=pltpu.VMEM((4, 32, D), BF16),
        ry_row=pltpu.VMEM((2, RADIUS * W, D), BF16),
        ry_col=pltpu.VMEM((2, H * 8, D), BF16),
        ry_cor=pltpu.VMEM((4, 32, D), BF16),
        wg=pltpu.VMEM((2, WP, D), F32),
        wb=pltpu.VMEM((2, WP, D), BF16),
        rx_half=pltpu.VMEM((2, HALF, D), BF16),
        half=pltpu.VMEM((2, HALF, D), F32),
        hb=pltpu.VMEM((2, HALF, D), BF16),
        rx_pl=pltpu.VMEM((2, nc, cc, D), BF16),
        ys=pltpu.VMEM((2, ny, cc, D), F32),
        cos=pltpu.SMEM((HEADS,), F32),
        s_in=dma((6,)),
        s_hal=dma((10,)),
        r_hal=dma((10,)),
        s_ret=dma((8,)),
        r_ret=dma((8,)),
        s_core=dma((2, 2)),
        r_core=dma((2, 2)),
        s_pl=dma((2, 2)),
        r_pl=dma((2, 2)),
        s_y=dma((2, ny)),
        r_y=dma((2, ny)),
    )


def kernel(nr, nc, names, *refs):
    S = collections.namedtuple("S", names)(*refs)
    row, col = lax.axis_index("row"), lax.axis_index("col")
    core, ypos = lax.rem(row, 2), lax.div(row, 2)
    ny = nr // 2
    cc = HALF // nc

    def there(dr, dc):
        return (lax.rem(row + (dr % nr), nr), lax.rem(col + (dc % nc), nc))

    mate = (row + 1 - 2 * core, col)
    sent = []

    def remote(src, dst, send, recv, device):
        return pltpu.make_async_remote_copy(
            src_ref=src, dst_ref=dst, send_sem=send, recv_sem=recv, device_id=device, device_id_type=MESH
        )

    def send(*args):
        copy = remote(*args)
        copy.start()
        sent.append(copy)
        return copy

    def departed():
        for c in sent:
            c.wait_send()
        sent.clear()

    partners = list(DIRS)
    partners += [(0, k) for k in range(2, nc - 1)]
    partners += [(2 * m, 0) for m in range(1, ny)]
    barrier = pltpu.get_barrier_semaphore()
    for dr, dc in partners:
        pl.semaphore_signal(barrier, inc=1, device_id=there(dr, dc), device_id_type=MESH)
    loads = []
    for i, (src, dst) in enumerate(
        ((S.h_lat, S.lat), (S.h_gain, S.gain), (S.h_go, S.go), (S.h_wqkv, S.wqkv), (S.h_wo, S.wo), (S.h_cos, S.cos))
    ):
        loads.append(pltpu.make_async_copy(src, dst, S.s_in.at[i]))
        loads[-1].start()

    step = 32

    def load(i, acc):
        x = S.lat[pl.ds(i * step, step)].astype(F32)
        S.l32[at(i, step * H), :] = x.reshape(step * H, W)
        return acc + jnp.sum(x * x, axis=0)

    loads[0].wait()
    total = lax.fori_loop(0, D // step, load, jnp.zeros((H, W), F32), unroll=True)
    S.inv[...] = lax.rsqrt(total * (1.0 / D) + EPS)
    loads[1].wait()
    gain = S.gain[...]

    for r in range(H):
        x = S.l32[pl.ds(r, D, stride=H), :] * S.inv[r : r + 1, :]
        xn = x.T * gain
        xnb = xn.astype(BF16)
        S.xr[r] = xnb
        S.xe32[0, span(r, 8), :] = xn[:8]
        S.xe32[1, span(r, 8), :] = xn[W - 8 :]
        for j in range(NB):
            S.xb[span(j * H + r, B), :] = xnb[span(j, B)]
        for g in range(1, NB):
            S.xg[span(g * ER + r, B), :] = xn[g * B - 8 : g * B + 8].astype(BF16)
    S.xe[...] = S.xe32[...].astype(BF16)

    pl.semaphore_wait(barrier, len(partners))
    near = {-1: slice(0, RADIUS), 1: slice(H - RADIUS, H)}
    part = {-1: slice(0, 32), 1: slice(32, 64)}
    early, late = [], []
    for i, (dr, dc) in reversed([*enumerate(DIRS)]):
        if dc == 0:
            continue
        if dr == 0:
            src, dst = S.xe.at[(dc + 1) // 2], S.rx_col.at[i - 2]
        else:
            src, dst = S.xe.at[(dc + 1) // 2, part[dr]], S.rx_cor.at[i - 4]
        copy = send(src, dst, S.s_hal.at[i], S.r_hal.at[i], there(dr, dc))
        (early if dc == 1 else late).append(copy)
    for n, cols in enumerate((slice(0, FIRST), slice(FIRST, W))):
        for i in range(2):
            dr = DIRS[i][0]
            s = 8 * n + i
            src, dst = S.xr.at[near[dr], cols], S.rx_row.at[i, :, cols]
            (late if n else early).append(send(src, dst, S.s_hal.at[s], S.r_hal.at[s], there(dr, 0)))

    for c in loads[2:]:
        c.wait()
    S.wot[...] = S.wo[...].T
    S.wtq[...] = S.wqkv[0:D, :].T
    for p in range(2):
        for i in range(2):
            a = (1 + i) * D + p * PW
            S.wtp[p, :, span(i, PW)] = S.wqkv[a : a + PW, :].T

    def widen(i, carry):
        x = S.go[pl.ds(i * step, step)].astype(F32)
        S.g32[at(i, step * H), :] = x.reshape(step * H, W)
        return carry

    lax.fori_loop(0, D // step, widen, 0, unroll=True)
    for r in range(H):
        g = S.g32[pl.ds(r, D, stride=H), :].T.astype(BF16)
        for j in range(NB):
            S.gob[span(j * H + r, B), :] = g[span(j, B)]

    mshape = (2, ER, B, QC)
    half_, kr, kc = (lax.broadcasted_iota(jnp.int32, mshape, a) for a in range(3))
    lane = lax.broadcasted_iota(jnp.int32, mshape, 3)
    qr, qc = lax.div(lane, B), lax.rem(lane, B)
    krow = jnp.where(kr < ABOVE, kr, jnp.where(kr < BELOW, kr - ABOVE - RADIUS, kr - BELOW + H))
    dr = krow - qr
    off = B * half_ + kc - 8
    dc = off - qc
    grow = row * H + krow
    ok = (dr >= -RADIUS) & (dr <= RADIUS) & (dc >= -RADIUS) & (dc <= RADIUS)
    ok = ok & (grow >= 0) & (grow < nr * H) & (kr < UNUSED)
    one = jnp.where(ok, 1.0, 0.0).astype(F32).reshape(2 * GC, QC)
    off = off.reshape(2 * GC, QC)
    S.mask[0] = jnp.where(col * W + off >= 0, one, 0.0)
    S.mask[1] = one
    S.mask[2] = jnp.where(col * W + W - B + off < nc * W, one, 0.0)

    zero = jnp.zeros((HW, QC), BF16)
    for j in range(NB):
        q = heads(dot_nt(S.wqkv[0:D, :], S.xb[span(j, QC), :]))
        inv = lax.rsqrt(jnp.mean(q * q, axis=1, keepdims=True) + EPS)
        qn = (q * inv).astype(BF16)
        S.qraw[j] = flat(q)
        S.qinv[j] = inv
        ga = heads(dot_nt(S.wot[...], S.gob[span(j, QC), :])).astype(BF16)
        for p in range(2):
            for x, out in ((qn, S.qm), (ga, S.gm)):
                out[j, p, 0:HW, :] = jnp.concatenate([x[2 * p], zero], axis=1)
                out[j, p, HW:PW, :] = jnp.concatenate([zero, x[2 * p + 1]], axis=1)

    def pairs(*units):
        x = jnp.concatenate([S.xg[span(2 * g + s, GC // 2), :] for g, s in units], axis=0)
        kv = dot_nt(S.wqkv[D : 3 * D, :], x)
        k = heads(kv[:D])
        inv = lax.rsqrt(jnp.mean(k * k, axis=1, keepdims=True) + EPS)
        kn = flat(k * inv).astype(BF16)
        v = kv[D:].astype(BF16)
        knt, vnt = kn.T, v.T
        for n, (g, s) in enumerate(units):
            here, lanes = span(s, GC // 2), span(n, GC // 2)
            S.kraw[g, :, here] = kv[:D, lanes]
            S.kinv[g, :, :, here] = inv[:, :, lanes]
            S.kt[g, :, here] = kn[:, lanes]
            S.vt[g, :, here] = v[:, lanes]
            S.kc[g, here, :] = knt[lanes]
            S.vc[g, here, :] = vnt[lanes]

    for g in range(1, NB - 1, 2):
        pairs((g, 0), (g + 1, 0))

    def assemble(copies, groups):
        for c in copies:
            c.wait_recv()
        begin = 0 if groups[0] == 0 else FIRST - B
        size = FIRST if groups[0] == 0 else W - begin
        side = 1 if groups[0] == 0 else 0
        beside = S.rx_col[side].astype(F32)
        own = S.xe32[1 - side]

        def joined(at_side, inner):
            return jnp.concatenate([at_side, inner] if side else [inner, at_side], axis=0).astype(BF16)

        for g in groups:
            S.xg[g * GC + UNUSED * B : (g + 1) * GC, :] = jnp.zeros((2 * B, D), BF16)
        outer = 0 if side else NB
        for r in range(H):
            S.xg[span(outer * ER + r, B), :] = joined(beside[span(r, 8)], own[span(r, 8)])
        for down in (0, 1):
            corner = S.rx_cor[2 * down + side].astype(F32)
            for i in range(RADIUS):
                er = (ABOVE if down else BELOW) + i
                line = S.rx_row[down, i, begin : begin + size, :].astype(F32)
                for g in groups:
                    a = g * B - 8 - begin
                    if g != outer:
                        S.xg[span(g * ER + er, B), :] = line[a : a + B].astype(BF16)
                inner = line[:8] if side else line[-8:]
                S.xg[span(outer * ER + er, B), :] = joined(corner[span(i + 1 if down else i, 8)], inner)

    def first_groups():
        assemble(early, range(0, 5))
        pairs((0, 0), (0, 1))
        pairs((1, 1), (2, 1))

    def last_groups():
        assemble(late, range(5, NG))
        pairs((5, 1), (6, 1))

    def end_groups():
        pairs((7, 0), (7, 1))
        pairs((8, 0), (8, 1))

    factor = [S.cos[h] * (1.0 / HW) for h in range(HEADS)]

    def by_lane(values):
        return jnp.concatenate([jnp.full((1, QC), x, F32) for x in values], axis=1)

    def key_done(p, g, gk, gv):
        o = span(p, PW)
        gk = jnp.concatenate([gk[span(i, HW)] * factor[2 * p + i] for i in range(2)], axis=0)
        gk = norm_back(heads(S.kraw[g, o, :]), S.kinv[g, 2 * p : 2 * p + 2], heads(gk))
        S.gkv[p, 0:PW, at(g, GC)] = flat(gk).astype(BF16)
        S.gkv[p, PW : 2 * PW, at(g, GC)] = gv.astype(BF16)

    def scores(p, j):
        o = span(p, PW)
        keys = jnp.concatenate([S.kc[j, :, o], S.kc[j + 1, :, o]], axis=0)
        vals = jnp.concatenate([S.vc[j, :, o], S.vc[j + 1, :, o]], axis=0)
        return dot(keys, S.qm[j, p]), dot(vals, S.gm[j, p])

    def softmax(p, j, score, prod):
        lgr = by_lane(factor[2 * p : 2 * p + 2]) * math.log2(math.e)
        which = 0 if j == 0 else 2 if j == NB - 1 else 1
        tot = jnp.zeros((8, 2 * QC), F32)
        ed = jnp.zeros((8, 2 * QC), F32)
        for c in range(0, 2 * GC, CHUNK):
            mk = S.mask[which, c : c + CHUNK, :]
            e = jnp.exp2(score[c : c + CHUNK] * lgr) * jnp.concatenate([mk, mk], axis=1)
            tot = tot + jnp.sum(e.reshape(CHUNK // 8, 8, 2 * QC), axis=0)
            ed = ed + jnp.sum((e * prod[c : c + CHUNK]).reshape(CHUNK // 8, 8, 2 * QC), axis=0)
            S.eb[j, c : c + CHUNK, :] = e.astype(BF16)
        rt = 1.0 / jnp.sum(tot, axis=0, keepdims=True)
        mean = jnp.sum(ed, axis=0, keepdims=True) * rt
        for c in range(0, 2 * GC, CHUNK):
            e = S.eb[j, c : c + CHUNK, :].astype(F32)
            S.sb[j, c : c + CHUNK, :] = (e * (prod[c : c + CHUNK] - mean)).astype(BF16)
        return rt

    def backward(p, j, rt, gk, gv):
        o = span(p, PW)
        far = by_lane(factor[2 * p : 2 * p + 2])
        prob = S.eb[j]
        slope = S.sb[j]
        keys_t = jnp.concatenate([S.kt[j, o, :], S.kt[j + 1, o, :]], axis=1)
        vals_t = jnp.concatenate([S.vt[j, o, :], S.vt[j + 1, o, :]], axis=1)
        attn = dot(vals_t, prob) * rt
        grad_q = dot(keys_t, slope) * (rt * far)
        for i in range(2):
            c, lanes = span(i, HW), span(i, QC)
            S.att[p, c, at(j, QC)] = attn[c, lanes].astype(BF16)
            raw = S.qraw[j, span(2 * p + i, HW), :]
            g = norm_back(heads(raw), S.qinv[j, 2 * p + i : 2 * p + i + 1], heads(grad_q[c, lanes]))
            S.gqb[p, c, at(j, QC)] = flat(g).astype(BF16)
        qs = (S.qm[j, p].astype(F32) * rt).astype(BF16)
        gs = (S.gm[j, p].astype(F32) * rt).astype(BF16)
        grad_k = dot_nt(qs, slope)
        grad_v = dot_nt(gs, prob)
        key_done(p, j, gk + grad_k[:, :GC], gv + grad_v[:, :GC])
        return grad_k[:, GC:], grad_v[:, GC:]

    def attention(p, ahead):
        gk, gv = jnp.zeros((PW, GC), F32), jnp.zeros((PW, GC), F32)
        first, rts = {}, {}
        for j in range(NB + 1):
            if j in ahead:
                ahead[j]()
            if j < NB:
                first[j] = scores(p, j)
            if j < NB:
                rts[j] = softmax(p, j, *first.pop(j))
            if 0 <= j - 1 < NB:
                gk, gv = backward(p, j - 1, rts.pop(j - 1), gk, gv)
        S.gk[...] = gk
        S.gv[...] = gv

    def weights(p):
        key_done(p, NB, S.gk[...], S.gv[...])
        S.wg[p, 0:PW, :] = dot(S.gqb[p], S.xb[...])
        S.wg[p, PW : 3 * PW, :] = dot(S.gkv[p], S.xg[...])
        S.wg[p, 3 * PW :, :] = dot(S.att[p], S.gob[...])
        S.wb[p] = S.wg[p].astype(BF16)

    mine = at(core, HALF)

    def to_core(p):
        return [send(S.wb.at[p, at(1 - core, HALF)], S.rx_half.at[p], S.s_core.at[p, 0], S.r_core.at[p, 0], mate)]

    def to_row(p):
        half = S.wg[p, mine, :] + S.rx_half[p].astype(F32)
        S.half[p] = half
        S.hb[p] = half.astype(BF16)
        for k in range(1, nc):
            t = lax.rem(col + k, nc)
            remote(S.hb.at[p, at(t, cc)], S.rx_pl.at[p, k], S.s_pl.at[p, 0], S.r_pl.at[p, 0], (row, t)).start()

    def whole_row(p, semaphore):
        rows = S.rx_pl.at[p, 1:nc]
        pltpu.make_async_copy(rows, rows, semaphore).wait()

    def to_y(p):
        chunk = S.half[p, at(col, cc), :]
        for k in range(1, nc):
            chunk = chunk + S.rx_pl[p, k].astype(F32)
        S.ys[p, ypos] = chunk
        slot = S.ys.at[p, ypos]
        return [send(slot, slot, S.s_y.at[p, m], S.r_y.at[p, m], there(2 * m, 0)) for m in range(1, ny)]

    def back_to_row(p):
        chunk = S.ys[p, 0]
        for m in range(1, ny):
            chunk = chunk + S.ys[p, m]
        place = pl.ds(pl.multiple_of(core * HALF + col * cc, cc), cc)
        S.gw[p, place, :] = (chunk * (1.0 / math.sqrt(nr * H * nc * W))).astype(BF16)
        slot = S.gw.at[p, place]
        for k in range(1, nc):
            remote(slot, slot, S.s_pl.at[p, 1], S.r_pl.at[p, 1], there(0, k)).start()

    def back_to_core(p):
        slot = S.gw.at[p, mine]
        return [send(slot, slot, S.s_core.at[p, 1], S.r_core.at[p, 1], mate)]

    def arrived(copies):
        for c in copies:
            c.wait_recv()

    attention(0, {0: first_groups, 2: lambda: pairs((3, 1), (4, 1)), 4: last_groups, 6: end_groups})
    weights(0)
    core0 = to_core(0)

    def midway():
        arrived(core0)
        to_row(0)

    attention(1, {NB // 2: midway})
    weights(1)
    core1 = to_core(1)

    def cells_kv(g):
        x = sum(dot(S.wtp[p], S.gkv[p, :, span(g, GC)]) for p in range(2)).T
        for er in range(UNUSED):
            S.gn[er, span(g, B), :] = x[span(er, B)]

    for g in range(4):
        cells_kv(g)
    arrived(core1)
    to_row(1)
    for g in range(4, NG):
        cells_kv(g)

    low, high = 8, 8 + W
    rows_at = {-1: slice(ABOVE, BELOW), 1: slice(BELOW, UNUSED)}
    cols_at = {-1: slice(0, 8), 1: slice(high, high + 8)}
    back = []
    for i, (dr, dc) in reversed([*enumerate(DIRS)]):
        if dc == 0:
            S.tx_row[i] = S.gn[rows_at[dr], low:high, :].reshape(RADIUS * W, D).astype(BF16)
            src, dst = S.tx_row.at[i], S.ry_row.at[i]
        elif dr == 0:
            S.tx_col[i - 2] = S.gn[0:H, cols_at[dc], :].reshape(H * 8, D).astype(BF16)
            src, dst = S.tx_col.at[i - 2], S.ry_col.at[i - 2]
        else:
            cor = S.gn[rows_at[dr], cols_at[dc], :].reshape(RADIUS * 8, D)
            S.tx_cor[i - 4] = jnp.concatenate([cor, jnp.zeros((8, D), F32)], axis=0).astype(BF16)
            src, dst = S.tx_cor.at[i - 4], S.ry_cor.at[i - 4]
        back.append(send(src, dst, S.s_ret.at[i], S.r_ret.at[i], there(dr, dc)))
    whole_row(0, S.r_pl.at[0, 0])
    y0 = to_y(0)

    for j in range(NB):
        g = jnp.concatenate([S.gqb[p, :, span(j, QC)] for p in range(2)], axis=0)
        x = dot(S.wtq[...], g).T
        for r in range(H):
            S.gn[r, j * B + 8 : j * B + 8 + B, :] += x[span(r, B)]
    whole_row(1, S.r_pl.at[1, 0])
    y1 = to_y(1)

    arrived(y0)
    back_to_row(0)
    arrived(back)
    last = H - RADIUS
    S.gn[last:H, low:high, :] += S.ry_row[0].astype(F32).reshape(RADIUS, W, D)
    S.gn[0:RADIUS, low:high, :] += S.ry_row[1].astype(F32).reshape(RADIUS, W, D)
    S.gn[0:H, high - 8 : high, :] += S.ry_col[0].astype(F32).reshape(H, 8, D)
    S.gn[0:H, low : low + 8, :] += S.ry_col[1].astype(F32).reshape(H, 8, D)
    for i, (dr, dc) in enumerate(DIRS[4:]):
        a = last if dr == -1 else 0
        b = high - 8 if dc == -1 else low
        cor = S.ry_cor[i].astype(F32)[: RADIUS * 8]
        S.gn[a : a + RADIUS, b : b + 8, :] += cor.reshape(RADIUS, 8, D)
    arrived(y1)
    back_to_row(1)

    for r in range(H):
        g = (S.gn[r, low:high, :] * gain).T
        x = S.l32[pl.ds(r, D, stride=H), :]
        inv = S.inv[r : r + 1, :]
        inner = jnp.mean(g * x, axis=0, keepdims=True)
        S.l32[pl.ds(r, D, stride=H), :] = inv * (g - x * (inv * inv * inner))

    def store(i, carry):
        S.gl[pl.ds(i * step, step)] = S.l32[at(i, step * H), :].reshape(step, H, W).astype(BF16)
        return carry

    lax.fori_loop(0, D // step, store, 0, unroll=True)

    departed()
    whole_row(0, S.s_pl.at[0, 0])
    whole_row(1, S.s_pl.at[1, 0])
    whole_row(0, S.s_pl.at[0, 1])
    whole_row(0, S.r_pl.at[0, 1])
    done0 = back_to_core(0)
    whole_row(1, S.r_pl.at[1, 1])
    done1 = back_to_core(1)
    arrived(done0)
    arrived(done1)
    departed()
    whole_row(1, S.s_pl.at[1, 1])


def finish(gl, gw, out, gwqkv, gwo):
    out[...] = gl[...]
    for p in range(2):
        for i in range(3):
            gwqkv[i * D + p * PW : i * D + (p + 1) * PW, :] = gw[p, span(i, PW), :].astype(F32)
        gwo[:, span(p, PW)] = gw[p, 3 * PW :, :].astype(F32).T


def solution(mesh):
    nr, nc = mesh.shape["row"], mesh.shape["col"]
    scratch = scratch_shapes(nr, nc)
    names = ["h_lat", "h_gain", "h_wqkv", "h_wo", "h_cos", "h_go", "gl", "gw", *scratch]
    hbm = pl.BlockSpec(memory_space=pltpu.HBM)
    vmem = pl.BlockSpec(memory_space=pltpu.VMEM)

    def per_device(latent, norm_gain, qkv_weight, out_weight, cos_scale, grad_output):
        gl, gw = pl.pallas_call(
            functools.partial(kernel, nr, nc, names),
            out_shape=(pltpu.VMEM((D, H, W), BF16), pltpu.VMEM((2, WP, D), BF16)),
            in_specs=[hbm] * 6,
            out_specs=(vmem, vmem),
            scratch_shapes=list(scratch.values()),
            compiler_params=pltpu.CompilerParams(
                collective_id=0, has_side_effects=True, vmem_limit_bytes=44 * 2**20
            ),
        )(
            *(
                pltpu.with_memory_space_constraint(x, pltpu.HBM)
                for x in (latent, norm_gain.reshape(1, D), qkv_weight, out_weight, cos_scale, grad_output)
            )
        )
        return pl.pallas_call(
            finish,
            out_shape=(
                jax.ShapeDtypeStruct((D, H, W), BF16),
                jax.ShapeDtypeStruct((3 * D, D), F32),
                jax.ShapeDtypeStruct((D, D), F32),
            ),
            in_specs=[vmem, vmem],
            out_specs=(vmem, vmem, vmem),
                        compiler_params=pltpu.CompilerParams(vmem_limit_bytes=16 * 2**20),
        )(*(pltpu.with_memory_space_constraint(x, pltpu.VMEM) for x in (gl, gw)))

    return jax.shard_map(
        per_device,
        mesh=mesh,
        in_specs=(P(None, "row", "col"), P(), P(), P(), P(), P(None, "row", "col")),
        out_specs=(P(None, "row", "col"), P(), P()),
        check_vma=False,
    )
```

```python
import collections
import functools
import math

import jax
import jax.numpy as jnp
from jax import lax
from jax.experimental import pallas as pl
from jax.experimental.pallas import tpu as pltpu
from jax.sharding import PartitionSpec as P

MESH = pl.DeviceIdType.MESH
F32 = jnp.float32
BF16 = jnp.bfloat16

D = 256
HEADS = 4
HW = 64
PW = 2 * HW
RADIUS = 3
EPS = 1e-06
H = 8
W = 128
B = 16
NB = W // B
QC = H * B
NG = NB + 1
ER = 16
ABOVE, BELOW, UNUSED = H, H + RADIUS, H + 2 * RADIUS
FIRST = 80
GC = ER * B
CHUNK = 64
WP = 4 * PW
HALF = WP // 2

DIRS = ((-1, 0), (1, 0), (0, -1), (0, 1), (-1, -1), (-1, 1), (1, -1), (1, 1))


def dot(a, b):
    return lax.dot_general(a, b, (((1,), (0,)), ((), ())), preferred_element_type=F32)


def dot_nt(a, b):
    return lax.dot_general(a, b, (((1,), (1,)), ((), ())), preferred_element_type=F32)


def heads(x):
    return x.reshape(x.shape[0] // HW, HW, x.shape[-1])


def flat(x):
    return x.reshape(x.shape[0] * HW, x.shape[-1])


def span(i, size):
    return slice(i * size, (i + 1) * size)


def at(i, size):
    return slice(i * size, (i + 1) * size) if isinstance(i, int) else pl.ds(pl.multiple_of(i * size, size), size)


def norm_back(raw, inv, grad):
    inner = jnp.mean(grad * raw, axis=1, keepdims=True)
    return inv * (grad - raw * (inv * inv * inner))


def scratch_shapes(nr, nc):
    cc = HALF // nc
    ny = nr // 2
    dma = pltpu.SemaphoreType.DMA
    return collections.OrderedDict(
        lat=pltpu.VMEM((D, H, W), BF16),
        go=pltpu.VMEM((D, H, W), BF16),
        gain=pltpu.VMEM((1, D), F32),
        wqkv=pltpu.VMEM((3 * D, D), BF16),
        wo=pltpu.VMEM((D, D), BF16),
        l32=pltpu.VMEM((D * H, W), F32),
        g32=pltpu.VMEM((D * H, W), F32),
        inv=pltpu.VMEM((H, W), F32),
        xr=pltpu.VMEM((H, W, D), BF16),
        xe32=pltpu.VMEM((2, H * 8, D), F32),
        xe=pltpu.VMEM((2, H * 8, D), BF16),
        rx_row=pltpu.VMEM((2, RADIUS, W, D), BF16),
        rx_col=pltpu.VMEM((2, H * 8, D), BF16),
        rx_cor=pltpu.VMEM((4, 32, D), BF16),
        xg=pltpu.VMEM((NG * GC, D), BF16),
        xb=pltpu.VMEM((NB * QC, D), BF16),
        gob=pltpu.VMEM((NB * QC, D), BF16),
        wot=pltpu.VMEM((D, D), BF16),
        wtq=pltpu.VMEM((D, D), BF16),
        wtp=pltpu.VMEM((2, D, 2 * PW), BF16),
        kraw=pltpu.VMEM((NG, D, GC), F32),
        kinv=pltpu.VMEM((NG, HEADS, 1, GC), F32),
        kc=pltpu.VMEM((NG, GC, D), BF16),
        vc=pltpu.VMEM((NG, GC, D), BF16),
        kt=pltpu.VMEM((NG, D, GC), BF16),
        vt=pltpu.VMEM((NG, D, GC), BF16),
        qraw=pltpu.VMEM((NB, D, QC), F32),
        qinv=pltpu.VMEM((NB, HEADS, 1, QC), F32),
        qm=pltpu.VMEM((NB, 2, PW, 2 * QC), BF16),
        gm=pltpu.VMEM((NB, 2, PW, 2 * QC), BF16),
        mask=pltpu.VMEM((3, 2 * GC, QC), F32),
        eb=pltpu.VMEM((NB, 2 * GC, 2 * QC), BF16),
        sb=pltpu.VMEM((NB, 2 * GC, 2 * QC), BF16),
        gk=pltpu.VMEM((PW, GC), F32),
        gv=pltpu.VMEM((PW, GC), F32),
        att=pltpu.VMEM((2, PW, NB * QC), BF16),
        gqb=pltpu.VMEM((2, PW, NB * QC), BF16),
        gkv=pltpu.VMEM((2, 2 * PW, NG * GC), BF16),
        gn=pltpu.VMEM((UNUSED, NG * B, D), F32),
        tx_row=pltpu.VMEM((2, RADIUS * W, D), BF16),
        tx_col=pltpu.VMEM((2, H * 8, D), BF16),
        tx_cor=pltpu.VMEM((4, 32, D), BF16),
        ry_row=pltpu.VMEM((2, RADIUS * W, D), BF16),
        ry_col=pltpu.VMEM((2, H * 8, D), BF16),
        ry_cor=pltpu.VMEM((4, 32, D), BF16),
        wg=pltpu.VMEM((2, WP, D), F32),
        wb=pltpu.VMEM((2, WP, D), BF16),
        rx_half=pltpu.VMEM((2, HALF, D), BF16),
        half=pltpu.VMEM((2, HALF, D), F32),
        hb=pltpu.VMEM((2, HALF, D), BF16),
        rx_pl=pltpu.VMEM((2, nc, cc, D), BF16),
        ys=pltpu.VMEM((2, ny, cc, D), F32),
        cos=pltpu.SMEM((HEADS,), F32),
        s_in=dma((6,)),
        s_hal=dma((10,)),
        r_hal=dma((10,)),
        s_ret=dma((8,)),
        r_ret=dma((8,)),
        s_core=dma((2, 2)),
        r_core=dma((2, 2)),
        s_pl=dma((2, 2)),
        r_pl=dma((2, 2)),
        s_y=dma((2, ny)),
        r_y=dma((2, ny)),
    )


def kernel(nr, nc, names, *refs):
    S = collections.namedtuple("S", names)(*refs)
    row, col = lax.axis_index("row"), lax.axis_index("col")
    core, ypos = lax.rem(row, 2), lax.div(row, 2)
    ny = nr // 2
    cc = HALF // nc

    def there(dr, dc):
        return (lax.rem(row + (dr % nr), nr), lax.rem(col + (dc % nc), nc))

    mate = (row + 1 - 2 * core, col)
    sent = []

    def remote(src, dst, send, recv, device):
        return pltpu.make_async_remote_copy(
            src_ref=src, dst_ref=dst, send_sem=send, recv_sem=recv, device_id=device, device_id_type=MESH
        )

    def send(*args):
        copy = remote(*args)
        copy.start()
        sent.append(copy)
        return copy

    def departed():
        for c in sent:
            c.wait_send()
        sent.clear()

    partners = list(DIRS)
    partners += [(0, k) for k in range(2, nc - 1)]
    partners += [(2 * m, 0) for m in range(1, ny)]
    barrier = pltpu.get_barrier_semaphore()
    for dr, dc in partners:
        pl.semaphore_signal(barrier, inc=1, device_id=there(dr, dc), device_id_type=MESH)
    loads = []
    for i, (src, dst) in enumerate(
        ((S.h_lat, S.lat), (S.h_gain, S.gain), (S.h_go, S.go), (S.h_wqkv, S.wqkv), (S.h_wo, S.wo), (S.h_cos, S.cos))
    ):
        loads.append(pltpu.make_async_copy(src, dst, S.s_in.at[i]))
        loads[-1].start()

    step = 32

    def load(i, acc):
        x = S.lat[pl.ds(i * step, step)].astype(F32)
        S.l32[at(i, step * H), :] = x.reshape(step * H, W)
        return acc + jnp.sum(x * x, axis=0)

    loads[0].wait()
    total = lax.fori_loop(0, D // step, load, jnp.zeros((H, W), F32), unroll=True)
    S.inv[...] = lax.rsqrt(total * (1.0 / D) + EPS)
    loads[1].wait()
    gain = S.gain[...]

    for r in range(H):
        x = S.l32[pl.ds(r, D, stride=H), :] * S.inv[r : r + 1, :]
        xn = x.T * gain
        xnb = xn.astype(BF16)
        S.xr[r] = xnb
        S.xe32[0, span(r, 8), :] = xn[:8]
        S.xe32[1, span(r, 8), :] = xn[W - 8 :]
        for j in range(NB):
            S.xb[span(j * H + r, B), :] = xnb[span(j, B)]
        for g in range(1, NB):
            S.xg[span(g * ER + r, B), :] = xn[g * B - 8 : g * B + 8].astype(BF16)
    S.xe[...] = S.xe32[...].astype(BF16)

    pl.semaphore_wait(barrier, len(partners))
    near = {-1: slice(0, RADIUS), 1: slice(H - RADIUS, H)}
    part = {-1: slice(0, 32), 1: slice(32, 64)}
    early, late = [], []
    for i, (dr, dc) in reversed([*enumerate(DIRS)]):
        if dc == 0:
            continue
        if dr == 0:
            src, dst = S.xe.at[(dc + 1) // 2], S.rx_col.at[i - 2]
        else:
            src, dst = S.xe.at[(dc + 1) // 2, part[dr]], S.rx_cor.at[i - 4]
        copy = send(src, dst, S.s_hal.at[i], S.r_hal.at[i], there(dr, dc))
        (early if dc == 1 else late).append(copy)
    for n, cols in enumerate((slice(0, FIRST), slice(FIRST, W))):
        for i in range(2):
            dr = DIRS[i][0]
            s = 8 * n + i
            src, dst = S.xr.at[near[dr], cols], S.rx_row.at[i, :, cols]
            (late if n else early).append(send(src, dst, S.s_hal.at[s], S.r_hal.at[s], there(dr, 0)))

    for c in loads[2:]:
        c.wait()
    S.wot[...] = S.wo[...].T
    S.wtq[...] = S.wqkv[0:D, :].T
    for p in range(2):
        for i in range(2):
            a = (1 + i) * D + p * PW
            S.wtp[p, :, span(i, PW)] = S.wqkv[a : a + PW, :].T

    def widen(i, carry):
        x = S.go[pl.ds(i * step, step)].astype(F32)
        S.g32[at(i, step * H), :] = x.reshape(step * H, W)
        return carry

    lax.fori_loop(0, D // step, widen, 0, unroll=True)
    for r in range(H):
        g = S.g32[pl.ds(r, D, stride=H), :].T.astype(BF16)
        for j in range(NB):
            S.gob[span(j * H + r, B), :] = g[span(j, B)]

    mshape = (2, ER, B, QC)
    half_, kr, kc = (lax.broadcasted_iota(jnp.int32, mshape, a) for a in range(3))
    lane = lax.broadcasted_iota(jnp.int32, mshape, 3)
    qr, qc = lax.div(lane, B), lax.rem(lane, B)
    krow = jnp.where(kr < ABOVE, kr, jnp.where(kr < BELOW, kr - ABOVE - RADIUS, kr - BELOW + H))
    dr = krow - qr
    off = B * half_ + kc - 8
    dc = off - qc
    grow = row * H + krow
    ok = (dr >= -RADIUS) & (dr <= RADIUS) & (dc >= -RADIUS) & (dc <= RADIUS)
    ok = ok & (grow >= 0) & (grow < nr * H) & (kr < UNUSED)
    one = jnp.where(ok, 1.0, 0.0).astype(F32).reshape(2 * GC, QC)
    off = off.reshape(2 * GC, QC)
    S.mask[0] = jnp.where(col * W + off >= 0, one, 0.0)
    S.mask[1] = one
    S.mask[2] = jnp.where(col * W + W - B + off < nc * W, one, 0.0)

    zero = jnp.zeros((HW, QC), BF16)
    for j in range(NB):
        q = heads(dot_nt(S.wqkv[0:D, :], S.xb[span(j, QC), :]))
        inv = lax.rsqrt(jnp.mean(q * q, axis=1, keepdims=True) + EPS)
        qn = (q * inv).astype(BF16)
        S.qraw[j] = flat(q)
        S.qinv[j] = inv
        ga = heads(dot_nt(S.wot[...], S.gob[span(j, QC), :])).astype(BF16)
        for p in range(2):
            for x, out in ((qn, S.qm), (ga, S.gm)):
                out[j, p, 0:HW, :] = jnp.concatenate([x[2 * p], zero], axis=1)
                out[j, p, HW:PW, :] = jnp.concatenate([zero, x[2 * p + 1]], axis=1)

    def pairs(*units):
        x = jnp.concatenate([S.xg[span(2 * g + s, GC // 2), :] for g, s in units], axis=0)
        kv = dot_nt(S.wqkv[D : 3 * D, :], x)
        k = heads(kv[:D])
        inv = lax.rsqrt(jnp.mean(k * k, axis=1, keepdims=True) + EPS)
        kn = flat(k * inv).astype(BF16)
        v = kv[D:].astype(BF16)
        knt, vnt = kn.T, v.T
        for n, (g, s) in enumerate(units):
            here, lanes = span(s, GC // 2), span(n, GC // 2)
            S.kraw[g, :, here] = kv[:D, lanes]
            S.kinv[g, :, :, here] = inv[:, :, lanes]
            S.kt[g, :, here] = kn[:, lanes]
            S.vt[g, :, here] = v[:, lanes]
            S.kc[g, here, :] = knt[lanes]
            S.vc[g, here, :] = vnt[lanes]

    for g in range(1, NB - 1, 2):
        pairs((g, 0), (g + 1, 0))

    def assemble(copies, groups):
        for c in copies:
            c.wait_recv()
        begin = 0 if groups[0] == 0 else FIRST - B
        size = FIRST if groups[0] == 0 else W - begin
        side = 1 if groups[0] == 0 else 0
        beside = S.rx_col[side].astype(F32)
        own = S.xe32[1 - side]

        def joined(at_side, inner):
            return jnp.concatenate([at_side, inner] if side else [inner, at_side], axis=0).astype(BF16)

        for g in groups:
            S.xg[g * GC + UNUSED * B : (g + 1) * GC, :] = jnp.zeros((2 * B, D), BF16)
        outer = 0 if side else NB
        for r in range(H):
            S.xg[span(outer * ER + r, B), :] = joined(beside[span(r, 8)], own[span(r, 8)])
        for down in (0, 1):
            corner = S.rx_cor[2 * down + side].astype(F32)
            for i in range(RADIUS):
                er = (ABOVE if down else BELOW) + i
                line = S.rx_row[down, i, begin : begin + size, :].astype(F32)
                for g in groups:
                    a = g * B - 8 - begin
                    if g != outer:
                        S.xg[span(g * ER + er, B), :] = line[a : a + B].astype(BF16)
                inner = line[:8] if side else line[-8:]
                S.xg[span(outer * ER + er, B), :] = joined(corner[span(i + 1 if down else i, 8)], inner)

    def first_groups():
        assemble(early, range(0, 5))
        pairs((0, 0), (0, 1))
        pairs((1, 1), (2, 1))

    def last_groups():
        assemble(late, range(5, NG))
        pairs((5, 1), (6, 1))

    def end_groups():
        pairs((7, 0), (7, 1))
        pairs((8, 0), (8, 1))

    factor = [S.cos[h] * (1.0 / HW) for h in range(HEADS)]

    def by_lane(values):
        return jnp.concatenate([jnp.full((1, QC), x, F32) for x in values], axis=1)

    def key_done(p, g, gk, gv):
        o = span(p, PW)
        gk = jnp.concatenate([gk[span(i, HW)] * factor[2 * p + i] for i in range(2)], axis=0)
        gk = norm_back(heads(S.kraw[g, o, :]), S.kinv[g, 2 * p : 2 * p + 2], heads(gk))
        S.gkv[p, 0:PW, at(g, GC)] = flat(gk).astype(BF16)
        S.gkv[p, PW : 2 * PW, at(g, GC)] = gv.astype(BF16)

    def scores(p, j):
        o = span(p, PW)
        keys = jnp.concatenate([S.kc[j, :, o], S.kc[j + 1, :, o]], axis=0)
        vals = jnp.concatenate([S.vc[j, :, o], S.vc[j + 1, :, o]], axis=0)
        return dot(keys, S.qm[j, p]), dot(vals, S.gm[j, p])

    def softmax(p, j, score, prod):
        lgr = by_lane(factor[2 * p : 2 * p + 2]) * math.log2(math.e)
        which = 0 if j == 0 else 2 if j == NB - 1 else 1
        tot = jnp.zeros((8, 2 * QC), F32)
        ed = jnp.zeros((8, 2 * QC), F32)
        for c in range(0, 2 * GC, CHUNK):
            mk = S.mask[which, c : c + CHUNK, :]
            e = jnp.exp2(score[c : c + CHUNK] * lgr) * jnp.concatenate([mk, mk], axis=1)
            tot = tot + jnp.sum(e.reshape(CHUNK // 8, 8, 2 * QC), axis=0)
            ed = ed + jnp.sum((e * prod[c : c + CHUNK]).reshape(CHUNK // 8, 8, 2 * QC), axis=0)
            S.eb[j, c : c + CHUNK, :] = e.astype(BF16)
        rt = 1.0 / jnp.sum(tot, axis=0, keepdims=True)
        mean = jnp.sum(ed, axis=0, keepdims=True) * rt
        for c in range(0, 2 * GC, CHUNK):
            e = S.eb[j, c : c + CHUNK, :].astype(F32)
            S.sb[j, c : c + CHUNK, :] = (e * (prod[c : c + CHUNK] - mean)).astype(BF16)
        return rt

    def backward(p, j, rt):
        o = span(p, PW)
        far = by_lane(factor[2 * p : 2 * p + 2])
        prob = S.eb[j]
        slope = S.sb[j]
        keys_t = jnp.concatenate([S.kt[j, o, :], S.kt[j + 1, o, :]], axis=1)
        vals_t = jnp.concatenate([S.vt[j, o, :], S.vt[j + 1, o, :]], axis=1)
        attn = dot(vals_t, prob) * rt
        grad_q = dot(keys_t, slope) * (rt * far)
        for i in range(2):
            c, lanes = span(i, HW), span(i, QC)
            S.att[p, c, at(j, QC)] = attn[c, lanes].astype(BF16)
            raw = S.qraw[j, span(2 * p + i, HW), :]
            g = norm_back(heads(raw), S.qinv[j, 2 * p + i : 2 * p + i + 1], heads(grad_q[c, lanes]))
            S.gqb[p, c, at(j, QC)] = flat(g).astype(BF16)

    def backward_keys(p, j, rt, gk, gv):
        prob = S.eb[j]
        slope = S.sb[j]
        qs = (S.qm[j, p].astype(F32) * rt).astype(BF16)
        gs = (S.gm[j, p].astype(F32) * rt).astype(BF16)
        grad_k = dot_nt(qs, slope)
        grad_v = dot_nt(gs, prob)
        key_done(p, j, gk + grad_k[:, :GC], gv + grad_v[:, :GC])
        return grad_k[:, GC:], grad_v[:, GC:]

    def attention(p, ahead):
        gk, gv = jnp.zeros((PW, GC), F32), jnp.zeros((PW, GC), F32)
        first, rts = {}, {}
        for j in range(NB + 1):
            if j in ahead:
                ahead[j]()
            if j < NB:
                first[j] = scores(p, j)
            if j < NB:
                rts[j] = softmax(p, j, *first.pop(j))
            if 0 <= j - 1 < NB:
                gk, gv = backward_keys(p, j - 1, rts[j - 1], gk, gv)
                backward(p, j - 1, rts.pop(j - 1))
        S.gk[...] = gk
        S.gv[...] = gv

    def weights(p):
        key_done(p, NB, S.gk[...], S.gv[...])
        S.wg[p, 0:PW, :] = dot(S.gqb[p], S.xb[...])
        S.wg[p, PW : 3 * PW, :] = dot(S.gkv[p], S.xg[...])
        S.wg[p, 3 * PW :, :] = dot(S.att[p], S.gob[...])
        S.wb[p] = S.wg[p].astype(BF16)

    mine = at(core, HALF)

    def to_core(p):
        return [send(S.wb.at[p, at(1 - core, HALF)], S.rx_half.at[p], S.s_core.at[p, 0], S.r_core.at[p, 0], mate)]

    def to_row(p):
        half = S.wg[p, mine, :] + S.rx_half[p].astype(F32)
        S.half[p] = half
        S.hb[p] = half.astype(BF16)
        for k in range(1, nc):
            t = lax.rem(col + k, nc)
            remote(S.hb.at[p, at(t, cc)], S.rx_pl.at[p, k], S.s_pl.at[p, 0], S.r_pl.at[p, 0], (row, t)).start()

    def whole_row(p, semaphore):
        rows = S.rx_pl.at[p, 1:nc]
        pltpu.make_async_copy(rows, rows, semaphore).wait()

    def to_y(p):
        chunk = S.half[p, at(col, cc), :]
        for k in range(1, nc):
            chunk = chunk + S.rx_pl[p, k].astype(F32)
        S.ys[p, ypos] = chunk
        slot = S.ys.at[p, ypos]
        return [send(slot, slot, S.s_y.at[p, m], S.r_y.at[p, m], there(2 * m, 0)) for m in range(1, ny)]

    def back_to_row(p):
        chunk = S.ys[p, 0]
        for m in range(1, ny):
            chunk = chunk + S.ys[p, m]
        place = pl.ds(pl.multiple_of(core * HALF + col * cc, cc), cc)
        S.gw[p, place, :] = (chunk * (1.0 / math.sqrt(nr * H * nc * W))).astype(BF16)
        slot = S.gw.at[p, place]
        for k in range(1, nc):
            remote(slot, slot, S.s_pl.at[p, 1], S.r_pl.at[p, 1], there(0, k)).start()

    def back_to_core(p):
        slot = S.gw.at[p, mine]
        return [send(slot, slot, S.s_core.at[p, 1], S.r_core.at[p, 1], mate)]

    def arrived(copies):
        for c in copies:
            c.wait_recv()

    attention(0, {0: first_groups, 2: lambda: pairs((3, 1), (4, 1)), 4: last_groups, 6: end_groups})
    weights(0)
    core0 = to_core(0)

    def midway():
        arrived(core0)
        to_row(0)

    attention(1, {NB // 2: midway})
    weights(1)
    core1 = to_core(1)

    def cells_kv(g):
        x = sum(dot(S.wtp[p], S.gkv[p, :, span(g, GC)]) for p in range(2)).T
        for er in range(UNUSED):
            S.gn[er, span(g, B), :] = x[span(er, B)]

    for g in range(4):
        cells_kv(g)
    arrived(core1)
    to_row(1)
    for g in range(4, NG):
        cells_kv(g)

    low, high = 8, 8 + W
    rows_at = {-1: slice(ABOVE, BELOW), 1: slice(BELOW, UNUSED)}
    cols_at = {-1: slice(0, 8), 1: slice(high, high + 8)}
    back = []
    for i, (dr, dc) in reversed([*enumerate(DIRS)]):
        if dc == 0:
            S.tx_row[i] = S.gn[rows_at[dr], low:high, :].reshape(RADIUS * W, D).astype(BF16)
            src, dst = S.tx_row.at[i], S.ry_row.at[i]
        elif dr == 0:
            S.tx_col[i - 2] = S.gn[0:H, cols_at[dc], :].reshape(H * 8, D).astype(BF16)
            src, dst = S.tx_col.at[i - 2], S.ry_col.at[i - 2]
        else:
            cor = S.gn[rows_at[dr], cols_at[dc], :].reshape(RADIUS * 8, D)
            S.tx_cor[i - 4] = jnp.concatenate([cor, jnp.zeros((8, D), F32)], axis=0).astype(BF16)
            src, dst = S.tx_cor.at[i - 4], S.ry_cor.at[i - 4]
        back.append(send(src, dst, S.s_ret.at[i], S.r_ret.at[i], there(dr, dc)))
    whole_row(0, S.r_pl.at[0, 0])
    y0 = to_y(0)

    for j in range(NB):
        g = jnp.concatenate([S.gqb[p, :, span(j, QC)] for p in range(2)], axis=0)
        x = dot(S.wtq[...], g).T
        for r in range(H):
            S.gn[r, j * B + 8 : j * B + 8 + B, :] += x[span(r, B)]
    whole_row(1, S.r_pl.at[1, 0])
    y1 = to_y(1)

    arrived(y0)
    back_to_row(0)
    arrived(back)
    last = H - RADIUS
    S.gn[last:H, low:high, :] += S.ry_row[0].astype(F32).reshape(RADIUS, W, D)
    S.gn[0:RADIUS, low:high, :] += S.ry_row[1].astype(F32).reshape(RADIUS, W, D)
    S.gn[0:H, high - 8 : high, :] += S.ry_col[0].astype(F32).reshape(H, 8, D)
    S.gn[0:H, low : low + 8, :] += S.ry_col[1].astype(F32).reshape(H, 8, D)
    for i, (dr, dc) in enumerate(DIRS[4:]):
        a = last if dr == -1 else 0
        b = high - 8 if dc == -1 else low
        cor = S.ry_cor[i].astype(F32)[: RADIUS * 8]
        S.gn[a : a + RADIUS, b : b + 8, :] += cor.reshape(RADIUS, 8, D)
    arrived(y1)
    back_to_row(1)

    for r in range(H):
        g = (S.gn[r, low:high, :] * gain).T
        x = S.l32[pl.ds(r, D, stride=H), :]
        inv = S.inv[r : r + 1, :]
        inner = jnp.mean(g * x, axis=0, keepdims=True)
        S.l32[pl.ds(r, D, stride=H), :] = inv * (g - x * (inv * inv * inner))

    def store(i, carry):
        S.gl[pl.ds(i * step, step)] = S.l32[at(i, step * H), :].reshape(step, H, W).astype(BF16)
        return carry

    lax.fori_loop(0, D // step, store, 0, unroll=True)

    departed()
    whole_row(0, S.s_pl.at[0, 0])
    whole_row(1, S.s_pl.at[1, 0])
    whole_row(0, S.s_pl.at[0, 1])
    whole_row(0, S.r_pl.at[0, 1])
    done0 = back_to_core(0)
    whole_row(1, S.r_pl.at[1, 1])
    done1 = back_to_core(1)
    arrived(done0)
    arrived(done1)
    departed()
    whole_row(1, S.s_pl.at[1, 1])


def finish(gl, gw, out, gwqkv, gwo):
    out[...] = gl[...]
    for p in range(2):
        for i in range(3):
            gwqkv[i * D + p * PW : i * D + (p + 1) * PW, :] = gw[p, span(i, PW), :].astype(F32)
        gwo[:, span(p, PW)] = gw[p, 3 * PW :, :].astype(F32).T


def solution(mesh):
    nr, nc = mesh.shape["row"], mesh.shape["col"]
    scratch = scratch_shapes(nr, nc)
    names = ["h_lat", "h_gain", "h_wqkv", "h_wo", "h_cos", "h_go", "gl", "gw", *scratch]
    hbm = pl.BlockSpec(memory_space=pltpu.HBM)
    vmem = pl.BlockSpec(memory_space=pltpu.VMEM)

    def per_device(latent, norm_gain, qkv_weight, out_weight, cos_scale, grad_output):
        gl, gw = pl.pallas_call(
            functools.partial(kernel, nr, nc, names),
            out_shape=(pltpu.VMEM((D, H, W), BF16), pltpu.VMEM((2, WP, D), BF16)),
            in_specs=[hbm] * 6,
            out_specs=(vmem, vmem),
            scratch_shapes=list(scratch.values()),
            compiler_params=pltpu.CompilerParams(
                collective_id=0, has_side_effects=True, vmem_limit_bytes=44 * 2**20
            ),
        )(
            *(
                pltpu.with_memory_space_constraint(x, pltpu.HBM)
                for x in (latent, norm_gain.reshape(1, D), qkv_weight, out_weight, cos_scale, grad_output)
            )
        )
        return pl.pallas_call(
            finish,
            out_shape=(
                jax.ShapeDtypeStruct((D, H, W), BF16),
                jax.ShapeDtypeStruct((3 * D, D), F32),
                jax.ShapeDtypeStruct((D, D), F32),
            ),
            in_specs=[vmem, vmem],
            out_specs=(vmem, vmem, vmem),
                        compiler_params=pltpu.CompilerParams(vmem_limit_bytes=16 * 2**20),
        )(*(pltpu.with_memory_space_constraint(x, pltpu.VMEM) for x in (gl, gw)))

    return jax.shard_map(
        per_device,
        mesh=mesh,
        in_specs=(P(None, "row", "col"), P(), P(), P(), P(), P(None, "row", "col")),
        out_specs=(P(None, "row", "col"), P(), P()),
        check_vma=False,
    )
```
